128 devices in a mesh: row: 8 (over x_lo, y), col: 16 (over x_hi, z, core).
Axes of the slice: x: 4 (x_hi: 2, x_lo: 2; x = x_hi * 2 + x_lo), y: 4, z: 4, core: 2. Of those that a mesh axis runs over, the one named last changes fastest.
Arguments:
- block_input: bfloat16 [128, 1024, 512], P('row', 'col'), may hold values from -6 to 6
- cotangent: bfloat16 [128, 1024, 512], P('row', 'col'), may hold values from -6 to 6
- qkv_weight: bfloat16 [512, 1536], replicated, as said below
- out_weight: bfloat16 [512, 512], replicated, may hold values from -0.25 to 0.25
- bias_table: float32 [16, 225], replicated, may hold values from -4 to 4
- norm_gain: float32 [512], replicated, may hold values from 0.5 to 1.5
- norm_shift: float32 [512], replicated, may hold values from -1.5 to 1.5
Outputs:
- grad_input: bfloat16 [128, 1024, 512], P('row', 'col')
- grad_qkv: float32 [512, 1536], P(('row', 'col'))
- grad_out: float32 [512, 512], P(('row', 'col'))
- grad_table: float32 [16, 225], replicated
- grad_gain: float32 [512], replicated
- grad_shift: float32 [512], replicated
The draws below stay inside these ranges and needn't reach their ends.
Inputs may be any that keep to these rules, and one draw needn't show every extreme that they name: `qkv_weight`: entries lie within -96 / sqrt(512) and 96 / sqrt(512).
All inputs are finite; a program needn't handle non-finite values.
Results may differ from the reference program's by a relative error of at most 0.012.
The reference program's roundings to bfloat16 on the way (of `normed`, `projected`, `prob_b`, `attended`, `grad_attended`, `scaled_grad`, `grad_projected` and `branch`) count: a program that leaves them out, or rounds other values in their place, can miss the bound.
Values may be sent and summed in bfloat16 or wider, within the bound.
No kernel may reach another device: no remote copies, remote signals or barrier semaphores. Data moves between devices by JAX's collectives and lax.ppermute only.
A program may use at most 128 MiB of HBM per device.

```python
import math
import jax
import jax.numpy as jnp
from jax import lax

D = 512
HEADS = 16
GRID = 8
REL = 225
IMG_H = 128
IMG_W = 1024
TOKENS = 131072


def draw_qkv_weight(key, part):
    key = jax.random.fold_in(key, 17)
    base_key = jax.random.fold_in(key, 0)
    weight = jax.random.truncated_normal(base_key, -4.0, 4.0, (D, 3 * D), jnp.float32) * D ** (-0.5)
    return weight.astype(jnp.bfloat16)


def steps_of(key, extent, shards, smallest, largest):
    loudness, own = 1.0, jax.random.fold_in(key, 6)
    for dim, blocks in shards:
        draws = jnp.exp(jax.random.uniform(jax.random.fold_in(own, dim), (blocks,), jnp.float32, smallest / len(shards), largest / len(shards)))
        loudness = loudness * jnp.repeat(draws, extent[dim] // blocks).reshape([-1 if axis == dim else 1 for axis in range(len(extent))])
    return loudness


def normal_values(rng, dims, scale, bound, cuts=(), kind=jnp.bfloat16):
    values = jax.random.normal(rng, dims, jnp.float32) * scale
    if len(cuts) > 0:
        values = steps_of(rng, dims, cuts, -0.22, 0.18) * values
    return jnp.clip(values, min=-bound, max=bound).astype(kind)


def setup_inputs(seed: int = 0) -> dict:
    keys = jax.random.split(jax.random.key(seed), 8)
    return {
        "block_input": normal_values(keys[0], (IMG_H, IMG_W, D), 1.0, 6.0, ((0, 8), (1, 16))),
        "cotangent": normal_values(keys[1], (IMG_H, IMG_W, D), 1.0, 6.0, ((0, 8), (1, 16))),
        "qkv_weight": draw_qkv_weight(jax.random.fold_in(keys[7], 71), 0),
        "out_weight": normal_values(keys[3], (D, D), D ** -0.5, 0.25),
        "bias_table": normal_values(keys[4], (HEADS, REL), 1.0, 4.0, (), jnp.float32),
        "norm_gain": jnp.clip(1.0 + 0.1 * jax.random.normal(keys[5], (D,), jnp.float32), 0.5, 1.5),
        "norm_shift": normal_values(keys[6], (D,), 0.3, 1.5, (), jnp.float32),
    }


EPSILON = 1e-05

def relative_onehot(members):
    span = 2 * GRID - 1
    position = jnp.arange(members * members, dtype=jnp.int32)
    first = position // members
    second = position % members
    row_delta = first // GRID - second // GRID + GRID - 1
    col_delta = first % GRID - second % GRID + GRID - 1
    rel_index = (row_delta * span + col_delta).astype(jnp.int32)
    offsets = jnp.arange(span * span, dtype=jnp.int32)
    return (rel_index[:, None] == offsets[None, :]).astype(jnp.float32)

def grid_backward(grid_x, grid_dy, qkv_weight, out_weight, bias_table, norm_gain, norm_shift, onehot):
    groups, members, model_width = grid_x.shape
    head_count = bias_table.shape[0]
    head_dim = model_width // head_count
    total_rows = groups * members
    input_f32 = grid_x.reshape(total_rows, model_width).astype(jnp.float32)
    centred = input_f32 - lax.optimization_barrier(jnp.mean(input_f32, axis=-1, keepdims=True))
    inv_std = lax.rsqrt(lax.optimization_barrier(jnp.mean(centred * centred, axis=-1, keepdims=True)) + EPSILON)
    normalized = centred * inv_std
    normed = (normalized * norm_gain + norm_shift).astype(jnp.bfloat16)
    projected = jnp.dot(normed, qkv_weight, preferred_element_type=jnp.float32).astype(jnp.bfloat16)
    projected = projected.reshape(groups, members, 3, head_count, head_dim).astype(jnp.float32)
    queries = projected[:, :, 0]
    key_heads = projected[:, :, 1]
    values = projected[:, :, 2]
    score_scale = head_dim ** (-0.5)
    rel_bias = jnp.dot(bias_table, onehot.T, precision=lax.Precision.HIGHEST).reshape(head_count, members, members)
    scores = jnp.einsum('gqhd,gkhd->ghqk', queries, key_heads) * score_scale + rel_bias
    probabilities = jax.nn.softmax(scores, axis=-1)
    prob_b = probabilities.astype(jnp.bfloat16).astype(jnp.float32)
    attended = jnp.einsum('ghqk,gkhd->gqhd', prob_b, values).astype(jnp.bfloat16).reshape(total_rows, model_width)
    cotangent_rows = grid_dy.reshape(total_rows, model_width)
    grad_attended = jnp.dot(cotangent_rows, out_weight.T, preferred_element_type=jnp.float32).astype(jnp.bfloat16)
    grad_attended = grad_attended.reshape(groups, members, head_count, head_dim).astype(jnp.float32)
    grad_out = jnp.dot(attended.T, cotangent_rows, preferred_element_type=jnp.float32)
    grad_prob = jnp.einsum('gqhd,gkhd->ghqk', grad_attended, values)
    grad_values = jnp.einsum('ghqk,gqhd->gkhd', prob_b, grad_attended)
    grad_scores = probabilities * (grad_prob - lax.optimization_barrier(jnp.sum(grad_prob * probabilities, axis=-1, keepdims=True)))
    scaled_grad = (grad_scores * score_scale).astype(jnp.bfloat16).astype(jnp.float32)
    grad_queries = jnp.einsum('ghqk,gkhd->gqhd', scaled_grad, key_heads)
    grad_keys = jnp.einsum('ghqk,gqhd->gkhd', scaled_grad, queries)
    grad_projected = jnp.stack((grad_queries, grad_keys, grad_values), axis=2).astype(jnp.bfloat16)
    grad_projected = grad_projected.reshape(total_rows, 3 * model_width)
    grad_qkv = jnp.dot(normed.T, grad_projected, preferred_element_type=jnp.float32)
    grad_normed = jnp.dot(grad_projected, qkv_weight.T, preferred_element_type=jnp.float32)
    grad_gain = lax.optimization_barrier(jnp.sum(grad_normed * normalized, axis=0))
    grad_shift = lax.optimization_barrier(jnp.sum(grad_normed, axis=0))
    grad_hat = grad_normed * norm_gain
    branch = inv_std * (grad_hat - lax.optimization_barrier(jnp.mean(grad_hat, axis=-1, keepdims=True)) - normalized * lax.optimization_barrier(jnp.mean(grad_hat * normalized, axis=-1, keepdims=True)))
    branch = branch.astype(jnp.bfloat16).reshape(groups, members, model_width)
    grad_bias = lax.optimization_barrier(jnp.sum(grad_scores, axis=0)).reshape(head_count, members * members)
    return (branch, grad_qkv, grad_out, grad_bias, grad_gain, grad_shift)

def reference(block_input, cotangent, qkv_weight, out_weight, bias_table, norm_gain, norm_shift):
    span_h = IMG_H // GRID
    span_w = IMG_W // GRID
    members = GRID * GRID

    def to_groups(field):
        return field.reshape(GRID, span_h, GRID, span_w, D).transpose(1, 3, 0, 2, 4).reshape(-1, members, D)
    grid_x = to_groups(block_input)
    grid_dy = to_groups(cotangent)
    total_groups = grid_x.shape[0]
    block_groups = math.gcd(total_groups, 128)
    block_count = total_groups // block_groups
    grid_x = grid_x.reshape(block_count, block_groups, members, D)
    grid_dy = grid_dy.reshape(block_count, block_groups, members, D)
    onehot = relative_onehot(members)

    def step_block(carry, pair):
        result = grid_backward(pair[0], pair[1], qkv_weight, out_weight, bias_table, norm_gain, norm_shift, onehot)
        updated = tuple((total + part for total, part in zip(carry, result[1:])))
        return (updated, result[0])
    initial = (jnp.zeros((D, 3 * D), jnp.float32), jnp.zeros((D, D), jnp.float32), jnp.zeros((HEADS, members * members), jnp.float32), jnp.zeros((D,), jnp.float32), jnp.zeros((D,), jnp.float32))
    sums, branch = lax.scan(step_block, initial, (grid_x, grid_dy))
    branch = branch.reshape(span_h, span_w, GRID, GRID, D).transpose(2, 0, 3, 1, 4).reshape(IMG_H, IMG_W, D)
    grad_input = (cotangent.astype(jnp.float32) + branch.astype(jnp.float32)).astype(jnp.bfloat16)
    factor = float(TOKENS) ** (-0.5)
    grad_table = jnp.dot(sums[2], onehot, precision=lax.Precision.HIGHEST)
    return (grad_input, sums[0] * factor, sums[1] * factor, grad_table * factor, sums[3] * factor, sums[4] * factor)
```

```python
import functools
import jax
import jax.numpy as jnp
from jax import lax
from jax.experimental import pallas as pl
from jax.experimental.pallas import tpu as pltpu
from jax.sharding import Mesh, PartitionSpec as P

GRID = 8
EPSILON = 1e-05
MEMBERS = GRID * GRID
PACK = 4


def dot(a, b, ca, cb):
    return lax.dot_general(a, b, (((ca,), (cb,)), ((), ())), preferred_element_type=jnp.float32)


def backward_kernel(
    core_ref, pair_ref, wqkv_ref, wout_ref, bias_ref, gain_ref, shift_ref,
    branch_ref, keep_ref, send_ref, gbias_ref, gvec_ref,
    proj, gatt, normed, dyp, hat, istd, gproj, att, bran, *, groups, width, head_dim,
):
    rows = groups * MEMBERS
    chunk = 256
    per = chunk // MEMBERS
    bf16, f32 = jnp.bfloat16, jnp.float32
    scale = head_dim ** (-0.5)

    def norm_step(c, carry):
        r = lax.broadcasted_iota(jnp.int32, (chunk, rows), 0)
        s = lax.broadcasted_iota(jnp.int32, (chunk, rows), 1)
        sel = (s == (r % MEMBERS) * groups + c * per + r // MEMBERS).astype(f32).astype(bf16)
        pair = pair_ref[...]
        xs = pair[:, :groups].reshape(rows, width)
        ds = pair[:, groups:].reshape(rows, width)
        x = dot(sel, xs, 1, 0)
        dy = dot(sel, ds, 1, 0).astype(bf16)
        here = pl.ds(pl.multiple_of(c * chunk, chunk), chunk)
        dyp[here, :] = dy
        centred = x - jnp.mean(x, axis=-1, keepdims=True)
        inv = lax.rsqrt(jnp.mean(centred * centred, axis=-1, keepdims=True) + EPSILON)
        normalized = centred * inv
        hat[here, :] = normalized
        istd[here, :] = jnp.broadcast_to(inv, (chunk, 128))
        nb = (normalized * gain_ref[...] + shift_ref[...]).astype(bf16)
        normed[here, :] = nb
        proj[here, :] = dot(nb, wqkv_ref[...], 1, 0).astype(bf16)
        gatt[here, :] = dot(dy, wout_ref[...], 1, 1).astype(bf16)
        return carry

    lax.fori_loop(0, rows // chunk, norm_step, 0)

    gbias_ref[...] = jnp.zeros_like(gbias_ref)
    lane = lax.broadcasted_iota(jnp.int32, (MEMBERS, 128), 1) // head_dim

    def spread(a):
        zero = jnp.zeros_like(a)
        return jnp.concatenate([jnp.where(lane == h, a, zero) for h in range(PACK)], axis=0)

    def gather(a):
        out = a[:MEMBERS]
        for h in range(1, PACK):
            out = jnp.where(lane == h, a[h * MEMBERS : (h + 1) * MEMBERS], out)
        return out

    def group_step(g, carry):
        here = pl.ds(pl.multiple_of(g * MEMBERS, MEMBERS), MEMBERS)
        for block in range(width // 128):
            cols = slice(block * 128, (block + 1) * 128)
            q = proj[here, cols]
            k = proj[here, width + block * 128 : width + (block + 1) * 128]
            v = proj[here, 2 * width + block * 128 : 2 * width + (block + 1) * 128]
            ga = gatt[here, cols]
            q_bd = spread(q)
            ga_bd = spread(ga)
            scores = dot(k, q_bd, 1, 1) * scale + bias_ref[block]
            gp = dot(v, ga_bd, 1, 1)
            e = jnp.exp(scores - jnp.max(scores, axis=0, keepdims=True))
            p = e / jnp.sum(e, axis=0, keepdims=True)
            pb = p.astype(bf16)
            gs = p * (gp - jnp.sum(gp * p, axis=0, keepdims=True))
            gbias_ref[block] += gs
            sg = (gs * scale).astype(bf16)
            att[here, cols] = gather(dot(pb, v, 0, 0)).astype(bf16)
            gproj[here, cols] = gather(dot(sg, k, 0, 0)).astype(bf16)
            gproj[here, width + block * 128 : width + (block + 1) * 128] = dot(sg, q_bd, 1, 0).astype(bf16)
            gproj[here, 2 * width + block * 128 : 2 * width + (block + 1) * 128] = dot(pb, ga_bd, 1, 0).astype(bf16)
        return carry

    lax.fori_loop(0, groups, group_step, 0)

    def back_step(c, carry):
        gg, gsh = carry
        here = pl.ds(pl.multiple_of(c * chunk, chunk), chunk)
        gn = dot(gproj[here, :], wqkv_ref[...], 1, 1)
        normalized = hat[here, :]
        prod = gn * normalized
        gg = gg + jnp.sum(prod.reshape(chunk // 8, 8, width), axis=0)
        gsh = gsh + jnp.sum(gn.reshape(chunk // 8, 8, width), axis=0)
        gh = gn * gain_ref[...]
        m1 = jnp.mean(gh, axis=-1, keepdims=True)
        m2 = jnp.mean(prod * gain_ref[...], axis=-1, keepdims=True)
        inv = istd[here, :][:, :1]
        bran[here, :] = (inv * (gh - m1 - normalized * m2)).astype(bf16)
        return gg, gsh

    zero = jnp.zeros((8, width), f32)
    gg, gsh = lax.fori_loop(0, rows // chunk, back_step, (zero, zero))
    gvec_ref[0:1, :] = jnp.sum(gg, axis=0, keepdims=True)
    gvec_ref[1:2, :] = jnp.sum(gsh, axis=0, keepdims=True)

    def out_step(c, carry):
        r = lax.broadcasted_iota(jnp.int32, (chunk, rows), 0)
        s = lax.broadcasted_iota(jnp.int32, (chunk, rows), 1)
        mem = chunk // groups
        sel = (s == (r % groups) * MEMBERS + c * mem + r // groups).astype(f32).astype(bf16)
        here = pl.ds(pl.multiple_of(c * mem, mem), mem)
        branch_ref[here] = dot(sel, bran[...], 1, 0).astype(bf16).reshape(mem, groups, width)
        return carry

    lax.fori_loop(0, rows // chunk, out_step, 0)

    half = 2 * width
    gw = dot(normed[...], gproj[...], 0, 0)
    go = dot(att[...], dyp[...], 0, 0)
    low = gw[:, :half]
    high = jnp.concatenate([gw[:, half:], go], axis=1)

    @pl.when(core_ref[0] == 0)
    def _():
        keep_ref[...] = low
        send_ref[...] = high.astype(bf16)

    @pl.when(core_ref[0] != 0)
    def _():
        keep_ref[...] = high
        send_ref[...] = low.astype(bf16)


def fused(core, pair, wqkv, wout, bias, gain, shift, head_dim=32):
    members, two_groups, width = pair.shape
    groups = two_groups // 2
    rows = groups * MEMBERS
    f32, bf16 = jnp.float32, jnp.bfloat16
    vm = pl.BlockSpec(memory_space=pltpu.VMEM)
    return pl.pallas_call(
        functools.partial(backward_kernel, groups=groups, width=width, head_dim=head_dim),
        out_shape=(
            jax.ShapeDtypeStruct((members, groups, width), bf16),
            jax.ShapeDtypeStruct((width, 2 * width), f32),
            jax.ShapeDtypeStruct((width, 2 * width), bf16),
            jax.ShapeDtypeStruct(bias.shape, f32),
            jax.ShapeDtypeStruct((8, width), f32),
        ),
        in_specs=[pl.BlockSpec(memory_space=pltpu.SMEM)] + [vm] * 6,
        out_specs=(vm,) * 5,
        scratch_shapes=[
            pltpu.VMEM((rows, 3 * width), bf16),
            pltpu.VMEM((rows, width), bf16),
            pltpu.VMEM((rows, width), bf16),
            pltpu.VMEM((rows, width), bf16),
            pltpu.VMEM((rows, width), f32),
            pltpu.VMEM((rows, 128), f32),
            pltpu.VMEM((rows, 3 * width), bf16),
            pltpu.VMEM((rows, width), bf16),
            pltpu.VMEM((rows, width), bf16),
        ],
        compiler_params=pltpu.CompilerParams(vmem_limit_bytes=56 * 1024 * 1024),
        name="fused_backward",
    )(core, pair, wqkv, wout, bias, gain.reshape(1, width), shift.reshape(1, width))


AXES = ("x_lo", "y", "x_hi", "z", "core")
CHIPS = AXES[:4]


def relative_onehot(members):
    span = 2 * GRID - 1
    second = jnp.arange(members, dtype=jnp.int32)[:, None]
    first = jnp.arange(members, dtype=jnp.int32)[None, :]
    row_delta = first // GRID - second // GRID + GRID - 1
    col_delta = first % GRID - second % GRID + GRID - 1
    rel_index = row_delta * span + col_delta
    offsets = jnp.arange(span * span, dtype=jnp.int32)
    return (rel_index[:, :, None] == offsets).astype(jnp.float32)


def swap(a, axis, mask):
    size = lax.axis_size(axis)
    return lax.ppermute(a, axis, [(i, i ^ mask) for i in range(size)])


def sum_everywhere(a):
    a = a + swap(a, "core", 1)
    for axis in ("z", "y", ("x_lo", "x_hi")):
        parts = [swap(a, axis, mask) for mask in (1, 2, 3)]
        a = (a + parts[0]) + (parts[1] + parts[2])
    return a


def local(block_input, cotangent, qkv_weight, out_weight, bias_table, norm_gain, norm_shift):
    tile_h, tile_w, width = block_input.shape
    heads, offsets = bias_table.shape
    chips = lax.axis_size(CHIPS)
    owned = tile_h * tile_w // chips
    devices = chips * lax.axis_size("core")
    core = lax.axis_index("core")
    onehot = relative_onehot(MEMBERS)
    bias = jnp.einsum(
        "bhr,kqr->bkhq",
        bias_table.reshape(heads // PACK, PACK, offsets),
        onehot,
        precision=lax.Precision.HIGHEST,
    ).reshape(heads // PACK, MEMBERS, PACK * MEMBERS)
    pair = jnp.concatenate(
        (block_input.reshape(chips, owned, width), cotangent.reshape(chips, owned, width)), axis=1
    )
    pair = lax.all_to_all(pair, CHIPS, split_axis=0, concat_axis=0, tiled=True)
    branch, keep, send, gbias, gvec = fused(
        core.reshape(1), pair, qkv_weight, out_weight, bias, norm_gain, norm_shift, width // heads
    )
    weights = (keep + swap(send, "core", 1).astype(jnp.float32)).astype(jnp.bfloat16)
    weights = weights.reshape(chips, width // chips, 2 * width)
    weights = lax.all_to_all(weights, CHIPS, split_axis=0, concat_axis=0, tiled=True)
    returned = lax.all_to_all(branch, CHIPS, split_axis=0, concat_axis=0, tiled=True)
    returned = returned.reshape(tile_h, tile_w, width)
    grad_input = (cotangent.astype(jnp.float32) + returned.astype(jnp.float32)).astype(jnp.bfloat16)

    factor = float(tile_h * tile_w * devices) ** (-0.5)
    table = jnp.einsum(
        "bkhq,kqr->bhr",
        gbias.reshape(heads // PACK, MEMBERS, PACK, MEMBERS),
        onehot,
        precision=lax.Precision.HIGHEST,
    )
    small = jnp.concatenate((table.reshape(-1), gvec[:2].reshape(-1)))
    small = jnp.pad(small, (0, -small.size % 128)).reshape(-1, 128)
    small = sum_everywhere(small).reshape(-1) * factor
    cut = heads * offsets

    part = jnp.sum(weights.astype(jnp.float32), axis=0) * factor
    share = part.shape[0] // 2
    mine = lax.dynamic_slice_in_dim(part, core * share, share, 0)
    other = swap(lax.dynamic_slice_in_dim(part, (1 - core) * share, share, 0), "core", 1)
    low = jnp.where(core == 0, mine, other)
    high = jnp.where(core == 0, other, mine)
    grad_qkv = jnp.concatenate((low, high[:, :width]), axis=1)
    grad_out = high[:, width:]
    return (
        grad_input,
        grad_qkv,
        grad_out,
        small[:cut].reshape(heads, offsets),
        small[cut : cut + width],
        small[cut + width : cut + 2 * width],
    )


def solution(mesh):
    fine = Mesh(mesh.devices.reshape(2, 4, 2, 4, 2), AXES)
    tile = P(("x_lo", "y"), ("x_hi", "z", "core"), None)
    return jax.shard_map(
        local,
        mesh=fine,
        in_specs=(tile, tile, P(), P(), P(), P(), P()),
        out_specs=(tile, P(AXES, None), P(AXES, None), P(), P(), P()),
        check_vma=False,
    )
```

```python
import functools
import jax
import jax.numpy as jnp
from jax import lax
from jax.experimental import pallas as pl
from jax.experimental.pallas import tpu as pltpu
from jax.sharding import Mesh, PartitionSpec as P

GRID = 8
EPSILON = 1e-05
MEMBERS = GRID * GRID
PACK = 4


def dot(a, b, ca, cb):
    return lax.dot_general(a, b, (((ca,), (cb,)), ((), ())), preferred_element_type=jnp.float32)


def backward_kernel(
    core_ref, pair_ref, wqkv_ref, wout_ref, bias_ref, gain_ref, shift_ref,
    branch_ref, keep_ref, send_ref, gbias_ref, gvec_ref,
    proj, gatt, normed, dyp, hat, istd, gproj, att, bran, order, *, groups, width, head_dim,
):
    rows = groups * MEMBERS
    chunk = 256
    per = chunk // MEMBERS
    bf16, f32 = jnp.bfloat16, jnp.float32
    scale = head_dim ** (-0.5)
    half = width // 2

    f = lax.broadcasted_iota(jnp.int32, (width, width), 0)
    r = lax.broadcasted_iota(jnp.int32, (width, width), 1)
    chip = (((r // 8 % 2) * 4 + r // 16 % 4) * 2 + r // 4 % 2) * 4 + r // 64 % 4
    order[...] = (f == chip * 8 + r // half * 4 + r % 4).astype(f32).astype(bf16)

    def norm_step(c, carry):
        r = lax.broadcasted_iota(jnp.int32, (chunk, rows), 0)
        s = lax.broadcasted_iota(jnp.int32, (chunk, rows), 1)
        sel = (s == (r % MEMBERS) * groups + c * per + r // MEMBERS).astype(f32).astype(bf16)
        pair = pair_ref[...]
        xs = pair[:, :groups].reshape(rows, width)
        ds = pair[:, groups:].reshape(rows, width)
        x = dot(sel, xs, 1, 0)
        dy = dot(sel, ds, 1, 0).astype(bf16)
        here = pl.ds(pl.multiple_of(c * chunk, chunk), chunk)
        dyp[here, :] = dy
        centred = x - jnp.mean(x, axis=-1, keepdims=True)
        inv = lax.rsqrt(jnp.mean(centred * centred, axis=-1, keepdims=True) + EPSILON)
        normalized = centred * inv
        hat[here, :] = normalized
        istd[here, :] = jnp.broadcast_to(inv, (chunk, 128))
        nb = (normalized * gain_ref[...] + shift_ref[...]).astype(bf16)
        normed[here, :] = dot(nb, order[...], 1, 0).astype(bf16)
        proj[here, :] = dot(nb, wqkv_ref[...], 1, 0).astype(bf16)
        gatt[here, :] = dot(dy, wout_ref[...], 1, 1).astype(bf16)
        return carry

    lax.fori_loop(0, rows // chunk, norm_step, 0)

    gbias_ref[...] = jnp.zeros_like(gbias_ref)
    lane = lax.broadcasted_iota(jnp.int32, (MEMBERS, 128), 1) // head_dim

    def spread(a):
        zero = jnp.zeros_like(a)
        return jnp.concatenate([jnp.where(lane == h, a, zero) for h in range(PACK)], axis=0)

    def gather(a):
        out = a[:MEMBERS]
        for h in range(1, PACK):
            out = jnp.where(lane == h, a[h * MEMBERS : (h + 1) * MEMBERS], out)
        return out

    def group_step(g, carry):
        here = pl.ds(pl.multiple_of(g * MEMBERS, MEMBERS), MEMBERS)
        for block in range(width // 128):
            cols = slice(block * 128, (block + 1) * 128)
            q = proj[here, cols]
            k = proj[here, width + block * 128 : width + (block + 1) * 128]
            v = proj[here, 2 * width + block * 128 : 2 * width + (block + 1) * 128]
            ga = gatt[here, cols]
            q_bd = spread(q)
            ga_bd = spread(ga)
            scores = dot(k, q_bd, 1, 1) * scale + bias_ref[block]
            gp = dot(v, ga_bd, 1, 1)
            e = jnp.exp(scores - jnp.max(scores, axis=0, keepdims=True))
            p = e / jnp.sum(e, axis=0, keepdims=True)
            pb = p.astype(bf16)
            gs = p * (gp - jnp.sum(gp * p, axis=0, keepdims=True))
            gbias_ref[block] += gs
            sg = (gs * scale).astype(bf16)
            att[here, cols] = gather(dot(pb, v, 0, 0)).astype(bf16)
            gproj[here, cols] = gather(dot(sg, k, 0, 0)).astype(bf16)
            gproj[here, width + block * 128 : width + (block + 1) * 128] = dot(sg, q_bd, 1, 0).astype(bf16)
            gproj[here, 2 * width + block * 128 : 2 * width + (block + 1) * 128] = dot(pb, ga_bd, 1, 0).astype(bf16)
        return carry

    lax.fori_loop(0, groups, group_step, 0)

    def back_step(c, carry):
        gg, gsh = carry
        here = pl.ds(pl.multiple_of(c * chunk, chunk), chunk)
        gn = dot(gproj[here, :], wqkv_ref[...], 1, 1)
        normalized = hat[here, :]
        prod = gn * normalized
        gg = gg + jnp.sum(prod.reshape(chunk // 8, 8, width), axis=0)
        gsh = gsh + jnp.sum(gn.reshape(chunk // 8, 8, width), axis=0)
        gh = gn * gain_ref[...]
        m1 = jnp.mean(gh, axis=-1, keepdims=True)
        m2 = jnp.mean(prod * gain_ref[...], axis=-1, keepdims=True)
        inv = istd[here, :][:, :1]
        bran[here, :] = (inv * (gh - m1 - normalized * m2)).astype(bf16)
        return gg, gsh

    zero = jnp.zeros((8, width), f32)
    gg, gsh = lax.fori_loop(0, rows // chunk, back_step, (zero, zero))
    gvec_ref[0:1, :] = jnp.sum(gg, axis=0, keepdims=True)
    gvec_ref[1:2, :] = jnp.sum(gsh, axis=0, keepdims=True)

    def out_step(c, carry):
        r = lax.broadcasted_iota(jnp.int32, (chunk, rows), 0)
        s = lax.broadcasted_iota(jnp.int32, (chunk, rows), 1)
        mem = chunk // groups
        sel = (s == (r % groups) * MEMBERS + c * mem + r // groups).astype(f32).astype(bf16)
        here = pl.ds(pl.multiple_of(c * mem, mem), mem)
        branch_ref[here] = dot(sel, bran[...], 1, 0).astype(bf16).reshape(mem, groups, width)
        return carry

    lax.fori_loop(0, rows // chunk, out_step, 0)

    attended = dot(att[...], order[...], 1, 0).astype(bf16)

    def put(ref, p):
        rows_p = slice(p * half, (p + 1) * half)
        ref[:, : 3 * width] = dot(normed[:, rows_p], gproj[...], 0, 0).astype(ref.dtype)
        ref[:, 3 * width :] = dot(attended[:, rows_p], dyp[...], 0, 0).astype(ref.dtype)

    for p in range(2):
        @pl.when(core_ref[0] == p)
        def _():
            put(keep_ref, p)
            put(send_ref, 1 - p)


def fused(core, pair, wqkv, wout, bias, gain, shift, head_dim=32):
    members, two_groups, width = pair.shape
    groups = two_groups // 2
    rows = groups * MEMBERS
    f32, bf16 = jnp.float32, jnp.bfloat16
    vm = pl.BlockSpec(memory_space=pltpu.VMEM)
    return pl.pallas_call(
        functools.partial(backward_kernel, groups=groups, width=width, head_dim=head_dim),
        out_shape=(
            jax.ShapeDtypeStruct((members, groups, width), bf16),
            jax.ShapeDtypeStruct((width // 2, 4 * width), f32),
            jax.ShapeDtypeStruct((width // 2, 4 * width), bf16),
            jax.ShapeDtypeStruct(bias.shape, f32),
            jax.ShapeDtypeStruct((8, width), f32),
        ),
        in_specs=[pl.BlockSpec(memory_space=pltpu.SMEM)] + [vm] * 6,
        out_specs=(vm,) * 5,
        scratch_shapes=[
            pltpu.VMEM((rows, 3 * width), bf16),
            pltpu.VMEM((rows, width), bf16),
            pltpu.VMEM((rows, width), bf16),
            pltpu.VMEM((rows, width), bf16),
            pltpu.VMEM((rows, width), f32),
            pltpu.VMEM((rows, 128), f32),
            pltpu.VMEM((rows, 3 * width), bf16),
            pltpu.VMEM((rows, width), bf16),
            pltpu.VMEM((rows, width), bf16),
            pltpu.VMEM((width, width), bf16),
        ],
        compiler_params=pltpu.CompilerParams(vmem_limit_bytes=56 * 1024 * 1024),
        name="fused_backward",
    )(core, pair, wqkv, wout, bias, gain.reshape(1, width), shift.reshape(1, width))


def split_pair(a):
    high = a.astype(jnp.bfloat16)
    return high, (a - high.astype(jnp.float32)).astype(jnp.bfloat16)


def stage_kernel(index_ref, *refs, arrivals, blocks, tail):
    own_ref, small_ref = refs[:2]
    arrived = refs[2 : 2 + arrivals]
    outs = refs[2 + arrivals :]
    f32 = jnp.float32
    span = own_ref.shape[0]

    def total(parts):
        if len(parts) == 2:
            return parts[0] + parts[1]
        return (parts[0] + parts[1]) + (parts[2] + parts[3])

    small = small_ref[...]
    if arrivals == 3:
        sent = [a[span : span + tail].astype(f32) + a[span + tail : span + 2 * tail].astype(f32) for a in arrived]
        high, low = split_pair(small)
        small = total([high.astype(f32) + low.astype(f32)] + sent)
    else:
        small = small + refs[2 + arrivals][...]
        outs = refs[3 + arrivals :]
    if blocks == 1:
        outs[0][...] = total([own_ref[...]] + [a[:span].astype(f32) for a in arrived])
        outs[1][...] = small
        return
    size = span // blocks
    high, low = split_pair(small)
    index = index_ref[0]
    if size % 8:
        whole = total([own_ref[...]] + [a[:span].astype(f32) for a in arrived])
    for k in range(blocks):
        if size % 8:
            block = whole[:size]
            for b in range(1, blocks):
                block = jnp.where((index ^ k) == b, whole[b * size : (b + 1) * size], block)
        else:
            at = pl.ds(pl.multiple_of((index ^ k) * size, size), size)
            block = total([own_ref[at, :]] + [a[at, :].astype(f32) for a in arrived])
        if k == 0:
            outs[0][...] = block
            outs[1][...] = small
        else:
            outs[k + 1][:size] = block.astype(jnp.bfloat16)
            outs[k + 1][size : size + tail] = high
            outs[k + 1][size + tail : size + 2 * tail] = low


def stage(index, own, small, arrived, blocks, small_arrived=()):
    span, width = own.shape
    tail = small.shape[0]
    size = span // blocks
    f32, bf16 = jnp.float32, jnp.bfloat16
    vm = pl.BlockSpec(memory_space=pltpu.VMEM)
    shapes = [jax.ShapeDtypeStruct((size, width), f32), jax.ShapeDtypeStruct((tail, width), f32)]
    message = -(-(size + 2 * tail) // 16) * 16
    shapes += [jax.ShapeDtypeStruct((message, width), bf16)] * (blocks - 1)
    arrays = (own, small) + tuple(arrived) + tuple(small_arrived)
    out = pl.pallas_call(
        functools.partial(stage_kernel, arrivals=len(arrived), blocks=blocks, tail=tail),
        out_shape=tuple(shapes),
        in_specs=[pl.BlockSpec(memory_space=pltpu.SMEM)] + [vm] * len(arrays),
        out_specs=(vm,) * len(shapes),
        compiler_params=pltpu.CompilerParams(vmem_limit_bytes=32 * 1024 * 1024),
        name=f"sum_in_{blocks}_blocks",
    )(index.reshape(1), *arrays)
    return out[0], out[1], out[2:]


AXES = ("x_lo", "y", "x_hi", "z", "core")
CHIPS = AXES[:4]


def relative_onehot(members):
    span = 2 * GRID - 1
    second = jnp.arange(members, dtype=jnp.int32)[:, None]
    first = jnp.arange(members, dtype=jnp.int32)[None, :]
    row_delta = first // GRID - second // GRID + GRID - 1
    col_delta = first % GRID - second % GRID + GRID - 1
    rel_index = row_delta * span + col_delta
    offsets = jnp.arange(span * span, dtype=jnp.int32)
    return (rel_index[:, :, None] == offsets).astype(jnp.float32)


def swap(a, axis, mask):
    size = lax.axis_size(axis)
    return lax.ppermute(a, axis, [(i, i ^ mask) for i in range(size)])


def local(block_input, cotangent, qkv_weight, out_weight, bias_table, norm_gain, norm_shift):
    tile_h, tile_w, width = block_input.shape
    heads, offsets = bias_table.shape
    chips = lax.axis_size(CHIPS)
    owned = tile_h * tile_w // chips
    devices = chips * lax.axis_size("core")
    core = lax.axis_index("core")
    onehot = relative_onehot(MEMBERS)
    bias = jnp.einsum(
        "bhr,kqr->bkhq",
        bias_table.reshape(heads // PACK, PACK, offsets),
        onehot,
        precision=lax.Precision.HIGHEST,
    ).reshape(heads // PACK, MEMBERS, PACK * MEMBERS)
    pair = jnp.concatenate(
        (block_input.reshape(chips, owned, width), cotangent.reshape(chips, owned, width)), axis=1
    )
    pair = lax.all_to_all(pair, CHIPS, split_axis=0, concat_axis=0, tiled=True)
    branch, keep, send, gbias, gvec = fused(
        core.reshape(1), pair, qkv_weight, out_weight, bias, norm_gain, norm_shift, width // heads
    )
    returned = lax.all_to_all(branch, CHIPS, split_axis=0, concat_axis=0, tiled=True)
    returned = returned.reshape(tile_h, tile_w, width)
    grad_input = (cotangent.astype(jnp.float32) + returned.astype(jnp.float32)).astype(jnp.bfloat16)

    factor = float(tile_h * tile_w * devices) ** (-0.5)
    table = jnp.einsum(
        "bkhq,kqr->bhr",
        gbias.reshape(heads // PACK, MEMBERS, PACK, MEMBERS),
        onehot,
        precision=lax.Precision.HIGHEST,
    )
    small = jnp.concatenate((table.reshape(-1), gvec[:2].reshape(-1)))
    columns = 4 * width
    small = jnp.pad(small, (0, -small.size % columns)).reshape(-1, columns)
    arrived, small_arrived = (swap(send, "core", 1),), (swap(small, "core", 1),)
    share = keep
    for axis in ("z", "y", ("x_lo", "x_hi")):
        index = lax.axis_index(axis)
        share, small, messages = stage(index, share, small, arrived, 4, small_arrived)
        arrived = tuple(swap(message, axis, k + 1) for k, message in enumerate(messages))
        small_arrived = ()
    share, small, _ = stage(index, share, small, arrived, 1)
    share = share * factor
    small = small.reshape(-1) * factor
    cut = heads * offsets
    return (
        grad_input,
        share[:, : 3 * width],
        share[:, 3 * width :],
        small[:cut].reshape(heads, offsets),
        small[cut : cut + width],
        small[cut + width : cut + 2 * width],
    )


def solution(mesh):
    fine = Mesh(mesh.devices.reshape(2, 4, 2, 4, 2), AXES)
    tile = P(("x_lo", "y"), ("x_hi", "z", "core"), None)
    return jax.shard_map(
        local,
        mesh=fine,
        in_specs=(tile, tile, P(), P(), P(), P(), P()),
        out_specs=(tile, P(AXES, None), P(AXES, None), P(), P(), P()),
        check_vma=False,
    )
```

```python
import functools
import jax
import jax.numpy as jnp
from jax import lax
from jax.experimental import pallas as pl
from jax.experimental.pallas import tpu as pltpu
from jax.sharding import Mesh, PartitionSpec as P

GRID = 8
EPSILON = 1e-05
MEMBERS = GRID * GRID
PACK = 4
PARTS = 2


def dot(a, b, ca, cb):
    return lax.dot_general(a, b, (((ca,), (cb,)), ((), ())), preferred_element_type=jnp.float32)


def backward_kernel(*refs, groups, width, head_dim, last):
    pair_ref, wqkv_ref, wout_ref, bias_ref, gain_ref, shift_ref = refs[:6]
    if last:
        core_ref, before_ref, gbias_before, gvec_before = refs[6:10]
        branch_ref, keep_ref, send_ref, gbias_ref, gvec_ref = refs[10:15]
        proj, gatt, normed, dyp, hat, istd, gproj, att, dyf, before, before_sem = refs[15:]
        fetch = pltpu.make_async_copy(before_ref, before, before_sem)
        fetch.start()
    else:
        branch_ref, sums_ref, gbias_ref, gvec_ref = refs[6:10]
        proj, gatt, normed, dyp, hat, istd, gproj, att, dyf = refs[10:]
    rows = groups * MEMBERS
    chunk = 256
    per = chunk // MEMBERS
    bf16, f32 = jnp.bfloat16, jnp.float32
    scale = head_dim ** (-0.5)

    mem = chunk // groups

    lanes = width // 128

    def put(ref, at, value):
        for b in range(lanes):
            ref[b, at, :] = value[:, b * 128 : (b + 1) * 128]

    def take(ref, at):
        return jnp.concatenate([ref[b, at, :] for b in range(lanes)], axis=1)

    def hat_step(c, carry):
        here = pl.ds(pl.multiple_of(c * chunk, chunk), chunk)
        pair = pair_ref[pl.ds(pl.multiple_of(c * mem, mem), mem)].astype(f32)
        x = pair[:, 0].reshape(chunk, width)
        centred = x - jnp.mean(x, axis=-1, keepdims=True)
        inv = lax.rsqrt(jnp.mean(centred * centred, axis=-1, keepdims=True) + EPSILON)
        put(hat, here, centred * inv)
        istd[here, :] = jnp.broadcast_to(inv, (chunk, 128))
        put(dyf, here, pair[:, 1].reshape(chunk, width))
        return carry

    lax.fori_loop(0, rows // chunk, hat_step, 0)

    def by_group(ref, c):
        return jnp.concatenate(
            [take(ref, pl.ds(c * per + g, MEMBERS, stride=groups)) for g in range(per)], axis=0
        )

    def norm_step(c, carry):
        here = pl.ds(pl.multiple_of(c * chunk, chunk), chunk)
        nb = (by_group(hat, c) * gain_ref[...] + shift_ref[...]).astype(bf16)
        dy = by_group(dyf, c).astype(bf16)
        dyp[here, :] = dy
        normed[here, :] = nb
        proj[here, :] = dot(nb, wqkv_ref[...], 1, 0).astype(bf16)
        gatt[here, :] = dot(dy, wout_ref[...], 1, 1).astype(bf16)
        return carry

    lax.fori_loop(0, rows // chunk, norm_step, 0)

    gbias_ref[...] = gbias_before[...] if last else jnp.zeros_like(gbias_ref)
    lane = lax.broadcasted_iota(jnp.int32, (MEMBERS, 128), 1) // head_dim

    def spread(a):
        zero = jnp.zeros_like(a)
        return jnp.concatenate([jnp.where(lane == h, a, zero) for h in range(PACK)], axis=0)

    def gather(a):
        out = a[:MEMBERS]
        for h in range(1, PACK):
            out = jnp.where(lane == h, a[h * MEMBERS : (h + 1) * MEMBERS], out)
        return out

    blocks = range(width // 128)

    def group_step(g, carry):
        here = pl.ds(pl.multiple_of(g * MEMBERS, MEMBERS), MEMBERS)
        cols = [slice(b * 128, (b + 1) * 128) for b in blocks]
        kcols = [slice(width + b * 128, width + (b + 1) * 128) for b in blocks]
        vcols = [slice(2 * width + b * 128, 2 * width + (b + 1) * 128) for b in blocks]
        ks = [proj[here, c] for c in kcols]
        vs = [proj[here, c] for c in vcols]
        none = jnp.zeros_like(ks[0])
        ws = [jnp.concatenate([spread(proj[here, c]), spread(gatt[here, c])], axis=1) for c in cols]
        both = [
            dot(
                jnp.concatenate(
                    [jnp.concatenate([k, none], axis=1), jnp.concatenate([none, v], axis=1)], axis=0
                ),
                w, 1, 1,
            )
            for k, v, w in zip(ks, vs, ws)
        ]
        pds = []
        for b in blocks:
            scores = both[b][:MEMBERS] * scale + bias_ref[b]
            gp = both[b][MEMBERS:]
            e = jnp.exp(scores - jnp.max(scores, axis=0, keepdims=True))
            p = e * (1.0 / jnp.sum(e, axis=0, keepdims=True))
            gs = p * (gp - jnp.sum(gp * p, axis=0, keepdims=True))
            gbias_ref[b] += gs
            pds.append(jnp.concatenate([p.astype(bf16), (gs * scale).astype(bf16)], axis=0))
        keyed = [dot(pd, w, 1, 0) for pd, w in zip(pds, ws)]
        queried = [
            dot(
                pd,
                jnp.concatenate(
                    [jnp.concatenate([v, none], axis=1), jnp.concatenate([none, k], axis=1)], axis=0
                ),
                0, 0,
            )
            for k, v, pd in zip(ks, vs, pds)
        ]
        for b in blocks:
            att[here, cols[b]] = gather(queried[b][:, :128]).astype(bf16)
            gproj[here, cols[b]] = gather(queried[b][:, 128:]).astype(bf16)
            gproj[here, kcols[b]] = keyed[b][MEMBERS:, :128].astype(bf16)
            gproj[here, vcols[b]] = keyed[b][:MEMBERS, 128:].astype(bf16)
        return carry

    lax.fori_loop(0, groups, group_step, 0)

    def gn_step(c, carry):
        here = pl.ds(pl.multiple_of(c * chunk, chunk), chunk)
        gn = dot(gproj[here, :], wqkv_ref[...], 1, 1)
        for g in range(per):
            put(dyf, pl.ds(c * per + g, MEMBERS, stride=groups), gn[g * MEMBERS : (g + 1) * MEMBERS])
        return carry

    lax.fori_loop(0, rows // chunk, gn_step, 0)

    def back_step(c, carry):
        gg, gsh = carry
        here = pl.ds(pl.multiple_of(c * chunk, chunk), chunk)
        gn = take(dyf, here)
        normalized = take(hat, here)
        prod = gn * normalized
        gg = gg + jnp.sum(prod.reshape(chunk // 8, 8, width), axis=0)
        gsh = gsh + jnp.sum(gn.reshape(chunk // 8, 8, width), axis=0)
        gh = gn * gain_ref[...]
        m1 = jnp.mean(gh, axis=-1, keepdims=True)
        m2 = jnp.mean(prod * gain_ref[...], axis=-1, keepdims=True)
        inv = istd[here, :][:, :1]
        branch = (inv * (gh - m1 - normalized * m2)).astype(bf16)
        branch_ref[pl.ds(pl.multiple_of(c * mem, mem), mem)] = branch.reshape(mem, groups, width)
        return gg, gsh

    zero = jnp.zeros((8, width), f32)
    gg, gsh = lax.fori_loop(0, rows // chunk, back_step, (zero, zero))
    gvec = jnp.concatenate([jnp.sum(gg, axis=0, keepdims=True), jnp.sum(gsh, axis=0, keepdims=True)], axis=0)
    gvec_ref[...] = gvec + gvec_before[...] if last else gvec

    gw = dot(normed[...], gproj[...], 0, 0)
    go = dot(att[...], dyp[...], 0, 0)
    if not last:
        sums_ref[:, : 3 * width] = gw
        sums_ref[:, 3 * width :] = go
        return
    fetch.wait()
    half = 2 * width
    low = gw[:, :half] + before[:, :half]
    high = jnp.concatenate([gw[:, half:], go], axis=1) + before[:, half:]

    @pl.when(core_ref[0] == 0)
    def _():
        keep_ref[...] = low
        send_ref[...] = high.astype(bf16)

    @pl.when(core_ref[0] != 0)
    def _():
        keep_ref[...] = high
        send_ref[...] = low.astype(bf16)


VMEM = pl.BlockSpec(memory_space=pltpu.VMEM)
SMEM = pl.BlockSpec(memory_space=pltpu.SMEM)
ANY = pl.BlockSpec(memory_space=pl.ANY)


def backward(pair, wqkv, wout, bias, gain, shift, head_dim, core=None, before=None):
    members, _, groups, width = pair.shape
    rows = groups * MEMBERS
    last = before is not None
    f32, bf16 = jnp.float32, jnp.bfloat16
    if last:
        sums = (jax.ShapeDtypeStruct((width, 2 * width), f32), jax.ShapeDtypeStruct((width, 2 * width), bf16))
        more = (core.reshape(1),) + before
    else:
        sums = (jax.ShapeDtypeStruct((width, 4 * width), f32),)
        more = ()
    scratch = [
        pltpu.VMEM((rows, 3 * width), bf16),
        pltpu.VMEM((rows, width), bf16),
        pltpu.VMEM((rows, width), bf16),
        pltpu.VMEM((rows, width), bf16),
        pltpu.VMEM((width // 128, rows, 128), f32),
        pltpu.VMEM((rows, 128), f32),
        pltpu.VMEM((rows, 3 * width), bf16),
        pltpu.VMEM((rows, width), bf16),
        pltpu.VMEM((width // 128, rows, 128), f32),
    ]
    if last:
        scratch += [pltpu.VMEM((width, 4 * width), f32), pltpu.SemaphoreType.DMA]
    dense = 2 * rows * width * 10 * width
    return pl.pallas_call(
        functools.partial(backward_kernel, groups=groups, width=width, head_dim=head_dim, last=last),
        out_shape=(jax.ShapeDtypeStruct((members, groups, width), bf16),)
        + sums
        + (jax.ShapeDtypeStruct(bias.shape, f32), jax.ShapeDtypeStruct((2, width), f32)),
        in_specs=[VMEM] * 6 + ([SMEM, ANY, VMEM, VMEM] if last else []),
        out_specs=(VMEM,) * (5 if last else 4),
        scratch_shapes=scratch,
        compiler_params=pltpu.CompilerParams(vmem_limit_bytes=40 * 1024 * 1024),
        cost_estimate=pl.CostEstimate(flops=4 * dense, bytes_accessed=12 << 20, transcendentals=0),
        name="last_backward" if last else "first_backward",
    )(pair, wqkv, wout, bias, gain.reshape(1, width), shift.reshape(1, width), *more)


def pair_kernel(x_ref, dy_ref, *refs):
    outs, sems = refs[:-1], refs[-1]
    copies = []
    for c, out in enumerate(outs):
        for t, source in enumerate((x_ref, dy_ref)):
            copies.append(pltpu.make_async_copy(source.at[c], out.at[:, t], sems.at[c, t]))
    for copy in copies:
        copy.start()
    for copy in copies:
        copy.wait()


def pairs(x, dy):
    parts, chips, groups, width = x.shape
    return pl.pallas_call(
        pair_kernel,
        out_shape=(jax.ShapeDtypeStruct((chips, 2, groups, width), x.dtype),) * parts,
        in_specs=[ANY, ANY],
        out_specs=(ANY,) * parts,
        scratch_shapes=[pltpu.SemaphoreType.DMA((parts, 2))],
        name="pairs",
    )(x, dy)


def outgoing_kernel(first_ref, second_ref, keep_ref, recv_ref, out_ref):
    chips, _, groups, width = out_ref.shape
    out_ref[:, 0] = first_ref[...]
    out_ref[:, 1] = second_ref[...]
    for part in range(2):
        cols = slice(part * width, (part + 1) * width)
        total = (keep_ref[:, cols] + recv_ref[:, cols].astype(jnp.float32)).astype(jnp.bfloat16)
        out_ref[:, 2 + part] = total.reshape(chips, groups, width)


def outgoing(first, second, keep, recv):
    chips, groups, width = first.shape
    return pl.pallas_call(
        outgoing_kernel,
        out_shape=jax.ShapeDtypeStruct((chips, 4, groups, width), first.dtype),
        in_specs=[VMEM] * 4,
        out_specs=VMEM,
        compiler_params=pltpu.CompilerParams(vmem_limit_bytes=24 * 1024 * 1024),
        name="outgoing",
    )(first, second, keep, recv)


def final_kernel(got_ref, dy_ref, grad_ref, weights_ref, *, factor):
    f32 = jnp.float32
    chips, _, groups, width = got_ref.shape
    for part in range(2):
        grad_ref[part] = (dy_ref[part].astype(f32) + got_ref[:, part].astype(f32)).astype(grad_ref.dtype)
        total = got_ref[0, 2 + part].astype(f32)
        for chip in range(1, chips):
            total = total + got_ref[chip, 2 + part].astype(f32)
        weights_ref[:, part * width : (part + 1) * width] = total * factor


def final(got, dy, factor):
    chips, _, groups, width = got.shape
    return pl.pallas_call(
        functools.partial(final_kernel, factor=factor),
        out_shape=(
            jax.ShapeDtypeStruct(dy.shape, dy.dtype),
            jax.ShapeDtypeStruct((groups, 2 * width), jnp.float32),
        ),
        in_specs=[VMEM] * 2,
        out_specs=(VMEM,) * 2,
        compiler_params=pltpu.CompilerParams(vmem_limit_bytes=24 * 1024 * 1024),
        name="final",
    )(got, dy)


AXES = ("x_lo", "y", "x_hi", "z", "core")
CHIPS = AXES[:4]


def relative_onehot(members):
    span = 2 * GRID - 1
    second = jnp.arange(members, dtype=jnp.int32)[:, None]
    first = jnp.arange(members, dtype=jnp.int32)[None, :]
    row_delta = first // GRID - second // GRID + GRID - 1
    col_delta = first % GRID - second % GRID + GRID - 1
    rel_index = row_delta * span + col_delta
    offsets = jnp.arange(span * span, dtype=jnp.int32)
    return (rel_index[:, :, None] == offsets).astype(jnp.float32)


def swap(a, axis, mask):
    size = lax.axis_size(axis)
    return lax.ppermute(a, axis, [(i, i ^ mask) for i in range(size)])


def sum_everywhere(a):
    a = a + swap(a, "core", 1)
    for axis in ("z", "y", ("x_lo", "x_hi")):
        parts = [swap(a, axis, mask) for mask in (1, 2, 3)]
        a = (a + parts[0]) + (parts[1] + parts[2])
    return a


def local(block_input, cotangent, qkv_weight, out_weight, bias_table, norm_gain, norm_shift):
    tile_h, tile_w, width = block_input.shape
    heads, offsets = bias_table.shape
    chips = lax.axis_size(CHIPS)
    devices = chips * lax.axis_size("core")
    owned = tile_h * tile_w // chips // PARTS
    core = lax.axis_index("core")
    onehot = relative_onehot(MEMBERS)
    bias = jnp.einsum(
        "bhr,kqr->bkhq",
        bias_table.reshape(heads // PACK, PACK, offsets),
        onehot,
        precision=lax.Precision.HIGHEST,
    ).reshape(heads // PACK, MEMBERS, PACK * MEMBERS)
    shape = (PARTS, chips, owned, width)
    sent = pairs(block_input.reshape(shape), cotangent.reshape(shape))
    got = [lax.all_to_all(part, CHIPS, split_axis=0, concat_axis=0, tiled=True) for part in sent]
    common = (qkv_weight, out_weight, bias, norm_gain, norm_shift, width // heads)
    first, *sums = backward(got[0], *common)
    second, keep, send, gbias, gvec = backward(got[1], *common, core, tuple(sums))
    back = outgoing(first, second, keep, swap(send, "core", 1))
    back = lax.all_to_all(back, CHIPS, split_axis=0, concat_axis=0, tiled=True)
    factor = float(tile_h * tile_w * devices) ** (-0.5)
    table = jnp.einsum(
        "bkhq,kqr->bhr",
        gbias.reshape(heads // PACK, MEMBERS, PACK, MEMBERS),
        onehot,
        precision=lax.Precision.HIGHEST,
    )
    small = jnp.concatenate((table.reshape(-1), gvec.reshape(-1)))
    small = jnp.pad(small, (0, -small.size % 128)).reshape(-1, 128)
    small = sum_everywhere(small).reshape(-1) * factor
    cut = heads * offsets

    grad_input, part = final(back, cotangent.reshape(shape), factor)
    share = part.shape[0] // 2
    mine = lax.dynamic_slice_in_dim(part, core * share, share, 0)
    other = swap(lax.dynamic_slice_in_dim(part, (1 - core) * share, share, 0), "core", 1)
    low = jnp.where(core == 0, mine, other)
    high = jnp.where(core == 0, other, mine)
    grad_qkv = jnp.concatenate((low, high[:, :width]), axis=1)
    grad_out = high[:, width:]
    return (
        grad_input.reshape(tile_h, tile_w, width),
        grad_qkv,
        grad_out,
        small[:cut].reshape(heads, offsets),
        small[cut : cut + width],
        small[cut + width : cut + 2 * width],
    )


def solution(mesh):
    fine = Mesh(mesh.devices.reshape(2, 4, 2, 4, 2), AXES)
    tile = P(("x_lo", "y"), ("x_hi", "z", "core"), None)
    return jax.shard_map(
        local,
        mesh=fine,
        in_specs=(tile, tile, P(), P(), P(), P(), P()),
        out_specs=(tile, P(AXES, None), P(AXES, None), P(), P(), P()),
        check_vma=False,
    )
```

```python
import functools
import jax
import jax.numpy as jnp
from jax import lax
from jax.experimental import pallas as pl
from jax.experimental.pallas import tpu as pltpu
from jax.sharding import Mesh, PartitionSpec as P

GRID = 8
EPSILON = 1e-05
MEMBERS = GRID * GRID
PACK = 4
PARTS = 2


def dot(a, b, ca, cb):
    return lax.dot_general(a, b, (((ca,), (cb,)), ((), ())), preferred_element_type=jnp.float32)


def backward_kernel(*refs, groups, width, head_dim, last):
    pair_ref, wqkv_ref, wout_ref, bias_ref, gain_ref, shift_ref = refs[:6]
    if last:
        gbias_before, gvec_before = refs[6:8]
        branch_ref, small_ref, normed, gproj, att, dyp = refs[8:14]
        proj, gatt, hat, istd, dyf, gbias_ref = refs[14:]
    else:
        branch_ref, sums_ref, gbias_ref, gvec_ref = refs[6:10]
        normed, gproj, att, dyp, proj, gatt, hat, istd, dyf = refs[10:]
    rows = groups * MEMBERS
    chunk = 256
    heads = width // head_dim
    per = chunk // MEMBERS
    bf16, f32 = jnp.bfloat16, jnp.float32
    scale = head_dim ** (-0.5)

    mem = chunk // groups

    lanes = width // 128

    def put(ref, at, value):
        for b in range(lanes):
            ref[b, at, :] = value[:, b * 128 : (b + 1) * 128]

    def take(ref, at):
        return jnp.concatenate([ref[b, at, :] for b in range(lanes)], axis=1)

    def hat_step(c, carry):
        here = pl.ds(pl.multiple_of(c * chunk, chunk), chunk)
        pair = pair_ref[pl.ds(pl.multiple_of(c * mem, mem), mem)].astype(f32)
        x = pair[:, 0].reshape(chunk, width)
        centred = x - jnp.mean(x, axis=-1, keepdims=True)
        inv = lax.rsqrt(jnp.mean(centred * centred, axis=-1, keepdims=True) + EPSILON)
        put(hat, here, centred * inv)
        istd[here, :] = jnp.broadcast_to(inv, (chunk, 128))
        put(dyf, here, pair[:, 1].reshape(chunk, width))
        return carry

    lax.fori_loop(0, rows // chunk, hat_step, 0)

    def by_group(ref, c):
        return jnp.concatenate(
            [take(ref, pl.ds(c * per + g, MEMBERS, stride=groups)) for g in range(per)], axis=0
        )

    def norm_step(c, carry):
        here = pl.ds(pl.multiple_of(c * chunk, chunk), chunk)
        nb = (by_group(hat, c) * gain_ref[...] + shift_ref[...]).astype(bf16)
        dy = by_group(dyf, c).astype(bf16)
        dyp[here, :] = dy
        normed[here, :] = nb
        proj[here, :] = dot(nb, wqkv_ref[...], 1, 0).astype(bf16)
        gatt[here, :] = dot(dy, wout_ref[...], 1, 1).astype(bf16)
        return carry

    lax.fori_loop(0, rows // chunk, norm_step, 0)

    gbias_ref[...] = gbias_before[...] if last else jnp.zeros_like(gbias_ref)
    lane = lax.broadcasted_iota(jnp.int32, (MEMBERS, 128), 1) // head_dim

    def spread(a):
        zero = jnp.zeros_like(a)
        return jnp.concatenate([jnp.where(lane == h, a, zero) for h in range(PACK)], axis=0)

    def gather(a):
        out = a[:MEMBERS]
        for h in range(1, PACK):
            out = jnp.where(lane == h, a[h * MEMBERS : (h + 1) * MEMBERS], out)
        return out

    blocks = range(width // 128)

    def group_step(g, carry):
        here = pl.ds(pl.multiple_of(g * MEMBERS, MEMBERS), MEMBERS)
        cols = [slice(b * 128, (b + 1) * 128) for b in blocks]
        kcols = [slice(width + b * 128, width + (b + 1) * 128) for b in blocks]
        vcols = [slice(2 * width + b * 128, 2 * width + (b + 1) * 128) for b in blocks]
        ks = [proj[here, c] for c in kcols]
        vs = [proj[here, c] for c in vcols]
        none = jnp.zeros_like(ks[0])
        ws = [jnp.concatenate([spread(proj[here, c]), spread(gatt[here, c])], axis=1) for c in cols]
        both = [
            dot(
                jnp.concatenate(
                    [jnp.concatenate([k, none], axis=1), jnp.concatenate([none, v], axis=1)], axis=0
                ),
                w, 1, 1,
            )
            for k, v, w in zip(ks, vs, ws)
        ]
        pds = []
        for b in blocks:
            scores = both[b][:MEMBERS] * scale + bias_ref[b]
            gp = both[b][MEMBERS:]
            e = jnp.exp(scores - jnp.max(scores, axis=0, keepdims=True))
            p = e * (1.0 / jnp.sum(e, axis=0, keepdims=True))
            gs = p * (gp - jnp.sum(gp * p, axis=0, keepdims=True))
            gbias_ref[b] += gs
            pds.append(jnp.concatenate([p.astype(bf16), (gs * scale).astype(bf16)], axis=0))
        keyed = [dot(pd, w, 1, 0) for pd, w in zip(pds, ws)]
        queried = [
            dot(
                pd,
                jnp.concatenate(
                    [jnp.concatenate([v, none], axis=1), jnp.concatenate([none, k], axis=1)], axis=0
                ),
                0, 0,
            )
            for k, v, pd in zip(ks, vs, pds)
        ]
        for b in blocks:
            att[here, cols[b]] = gather(queried[b][:, :128]).astype(bf16)
            gproj[here, cols[b]] = gather(queried[b][:, 128:]).astype(bf16)
            gproj[here, kcols[b]] = keyed[b][MEMBERS:, :128].astype(bf16)
            gproj[here, vcols[b]] = keyed[b][:MEMBERS, 128:].astype(bf16)
        return carry

    lax.fori_loop(0, groups, group_step, 0)

    def gn_step(c, carry):
        here = pl.ds(pl.multiple_of(c * chunk, chunk), chunk)
        gn = dot(gproj[here, :], wqkv_ref[...], 1, 1)
        for g in range(per):
            put(dyf, pl.ds(c * per + g, MEMBERS, stride=groups), gn[g * MEMBERS : (g + 1) * MEMBERS])
        return carry

    lax.fori_loop(0, rows // chunk, gn_step, 0)

    def back_step(c, carry):
        gg, gsh = carry
        here = pl.ds(pl.multiple_of(c * chunk, chunk), chunk)
        gn = take(dyf, here)
        normalized = take(hat, here)
        prod = gn * normalized
        gg = gg + jnp.sum(prod.reshape(chunk // 8, 8, width), axis=0)
        gsh = gsh + jnp.sum(gn.reshape(chunk // 8, 8, width), axis=0)
        gh = gn * gain_ref[...]
        m1 = jnp.mean(gh, axis=-1, keepdims=True)
        m2 = jnp.mean(prod * gain_ref[...], axis=-1, keepdims=True)
        inv = istd[here, :][:, :1]
        branch = (inv * (gh - m1 - normalized * m2)).astype(bf16)
        branch_ref[pl.ds(pl.multiple_of(c * mem, mem), mem)] = branch.reshape(mem, groups, width)
        return gg, gsh

    zero = jnp.zeros((8, width), f32)
    gg, gsh = lax.fori_loop(0, rows // chunk, back_step, (zero, zero))
    gvec = jnp.concatenate([jnp.sum(gg, axis=0, keepdims=True), jnp.sum(gsh, axis=0, keepdims=True)], axis=0)
    if last:
        small_ref[...] = jnp.zeros_like(small_ref)
        small_ref[:heads, :] = offset_sums(gbias_ref)
        gvec = gvec + gvec_before[...]
        for i in range(2):
            for part in range(width // 256):
                row = heads + i * (width // 256) + part
                small_ref[row : row + 1, :] = gvec[i : i + 1, part * 256 : (part + 1) * 256]
    else:
        gvec_ref[...] = gvec
        sums_ref[:, : 3 * width] = dot(normed[...], gproj[...], 0, 0)
        sums_ref[:, 3 * width :] = dot(att[...], dyp[...], 0, 0)


def offset_sums(gbias_ref):
    f32, bf16 = jnp.float32, jnp.bfloat16
    blocks, members, lanes = gbias_ref.shape
    i = lax.broadcasted_iota(jnp.int32, (lanes, 2 * lanes), 0)
    o = lax.broadcasted_iota(jnp.int32, (lanes, 2 * lanes), 1)
    query = i % members
    place = (i // members) * 128 + query // GRID * 16 + query % GRID
    wide = (o == place).astype(f32).astype(bf16)
    frames = []
    for b in range(blocks):
        value = gbias_ref[b]
        high = value.astype(bf16)
        rest = value - high.astype(f32)
        low = rest.astype(bf16)
        lowest = (rest - low.astype(f32)).astype(bf16)
        spread = dot(jnp.concatenate([high, low, lowest], axis=0), wide, 1, 0)
        spread = spread[:members] + (spread[members : 2 * members] + spread[2 * members :])
        frames += [spread[None, :, h * 128 : (h + 1) * 128] for h in range(PACK)]
    frame = jnp.concatenate(frames, axis=0)
    heads = frame.shape[0]
    frame = jnp.concatenate([frame, jnp.zeros_like(frame)], axis=2).reshape(heads * members, 256)
    column = GRID - 1 - lax.broadcasted_iota(jnp.int32, frame.shape, 0) % GRID
    for bit in (1, 2, 4):
        frame = jnp.where((column & bit) != 0, pltpu.roll(frame, bit, 1), frame)
    frame = jnp.sum(frame.reshape(heads * GRID, GRID, 256), axis=1)
    row = GRID - 1 - lax.broadcasted_iota(jnp.int32, frame.shape, 0) % GRID
    for bit in (1, 2, 4):
        frame = jnp.where((row & bit) != 0, pltpu.roll(frame, 16 * bit, 1), frame)
    return jnp.sum(frame.reshape(heads, GRID, 256), axis=1)


VMEM = pl.BlockSpec(memory_space=pltpu.VMEM)
SMEM = pl.BlockSpec(memory_space=pltpu.SMEM)


def backward(pair, wqkv, wout, bias, gain, shift, head_dim, before=None):
    members, _, groups, width = pair.shape
    rows = groups * MEMBERS
    last = before is not None
    f32, bf16 = jnp.float32, jnp.bfloat16
    shape = jax.ShapeDtypeStruct
    kept = [(rows, width), (rows, 3 * width), (rows, width), (rows, width)]
    scratch = [
        pltpu.VMEM((rows, 3 * width), bf16),
        pltpu.VMEM((rows, width), bf16),
        pltpu.VMEM((width // 128, rows, 128), f32),
        pltpu.VMEM((rows, 128), f32),
        pltpu.VMEM((width // 128, rows, 128), f32),
    ]
    outs = [shape((members, groups, width), bf16)]
    if last:
        outs += [shape((24, 256), f32)] + [shape(k, bf16) for k in kept]
        scratch += [pltpu.VMEM(bias.shape, f32)]
    else:
        outs += [shape((width, 4 * width), f32), shape(bias.shape, f32), shape((2, width), f32)]
        scratch = [pltpu.VMEM(k, bf16) for k in kept] + scratch
    return pl.pallas_call(
        functools.partial(backward_kernel, groups=groups, width=width, head_dim=head_dim, last=last),
        out_shape=tuple(outs),
        in_specs=[VMEM] * (8 if last else 6),
        out_specs=(VMEM,) * len(outs),
        scratch_shapes=scratch,
        compiler_params=pltpu.CompilerParams(vmem_limit_bytes=24 * 1024 * 1024),
        cost_estimate=pl.CostEstimate(flops=10_000_000_000, bytes_accessed=8 << 20, transcendentals=0),
        name="last_backward" if last else "first_backward",
    )(pair, wqkv, wout, bias, gain.reshape(1, width), shift.reshape(1, width), *(before or ()))


def weights_kernel(core_ref, normed, gproj, att, dyp, before, keep_ref, send_ref):
    width = normed.shape[1]
    half = 2 * width
    gw = dot(normed[...], gproj[...], 0, 0)
    go = dot(att[...], dyp[...], 0, 0)
    low = gw[:, :half] + before[:, :half]
    high = jnp.concatenate([gw[:, half:], go], axis=1) + before[:, half:]

    @pl.when(core_ref[0] == 0)
    def _():
        keep_ref[...] = low
        send_ref[...] = high.astype(send_ref.dtype)

    @pl.when(core_ref[0] != 0)
    def _():
        keep_ref[...] = high
        send_ref[...] = low.astype(send_ref.dtype)


def weight_halves(core, normed, gproj, att, dyp, before):
    width = normed.shape[1]
    return pl.pallas_call(
        weights_kernel,
        out_shape=(
            jax.ShapeDtypeStruct((width, 2 * width), jnp.float32),
            jax.ShapeDtypeStruct((width, 2 * width), jnp.bfloat16),
        ),
        in_specs=[SMEM] + [VMEM] * 5,
        out_specs=(VMEM,) * 2,
        compiler_params=pltpu.CompilerParams(vmem_limit_bytes=24 * 1024 * 1024),
        cost_estimate=pl.CostEstimate(flops=3_000_000_000, bytes_accessed=4 << 20, transcendentals=0),
        name="weight_halves",
    )(core.reshape(1), normed, gproj, att, dyp, before)


def pair_kernel(x_ref, dy_ref, out_ref):
    out_ref[:, 0] = x_ref[0]
    out_ref[:, 1] = dy_ref[0]


def pair_of(x, dy, part):
    _, chips, groups, width = x.shape
    steps = 4
    source = pl.BlockSpec((1, chips // steps, groups, width), lambda i: (part, i, 0, 0))
    return pl.pallas_call(
        pair_kernel,
        grid=(steps,),
        out_shape=jax.ShapeDtypeStruct((chips, 2, groups, width), x.dtype),
        in_specs=[source, source],
        out_specs=pl.BlockSpec((chips // steps, 2, groups, width), lambda i: (i, 0, 0, 0)),
        cost_estimate=pl.CostEstimate(flops=0, bytes_accessed=2 << 20, transcendentals=0),
        name="pair",
    )(x, dy)


def outgoing_kernel(first_ref, second_ref, keep_ref, recv_ref, out_ref):
    chips, _, groups, width = out_ref.shape
    out_ref[:, 0] = first_ref[...]
    out_ref[:, 1] = second_ref[...]
    for part in range(2):
        cols = slice(part * width, (part + 1) * width)
        total = (keep_ref[:, cols] + recv_ref[:, cols].astype(jnp.float32)).astype(jnp.bfloat16)
        out_ref[:, 2 + part] = total.reshape(chips, groups, width)


def outgoing(first, second, keep, recv):
    chips, groups, width = first.shape
    return pl.pallas_call(
        outgoing_kernel,
        out_shape=jax.ShapeDtypeStruct((chips, 4, groups, width), first.dtype),
        in_specs=[VMEM] * 4,
        out_specs=VMEM,
        compiler_params=pltpu.CompilerParams(vmem_limit_bytes=24 * 1024 * 1024),
        name="outgoing",
    )(first, second, keep, recv)


def final_kernel(got_ref, dy_ref, grad_ref, weights_ref, *, factor):
    f32 = jnp.float32
    chips, _, groups, width = got_ref.shape
    for part in range(2):
        grad_ref[part] = (dy_ref[part].astype(f32) + got_ref[:, part].astype(f32)).astype(grad_ref.dtype)
        total = got_ref[0, 2 + part].astype(f32)
        for chip in range(1, chips):
            total = total + got_ref[chip, 2 + part].astype(f32)
        weights_ref[:, part * width : (part + 1) * width] = total * factor


def final(got, dy, factor):
    chips, _, groups, width = got.shape
    return pl.pallas_call(
        functools.partial(final_kernel, factor=factor),
        out_shape=(
            jax.ShapeDtypeStruct(dy.shape, dy.dtype),
            jax.ShapeDtypeStruct((groups, 2 * width), jnp.float32),
        ),
        in_specs=[VMEM] * 2,
        out_specs=(VMEM,) * 2,
        compiler_params=pltpu.CompilerParams(vmem_limit_bytes=24 * 1024 * 1024),
        name="final",
    )(got, dy)


AXES = ("x_lo", "y", "x_hi", "z", "core")
CHIPS = AXES[:4]


def relative_onehot(members):
    span = 2 * GRID - 1
    second = jnp.arange(members, dtype=jnp.int32)[:, None]
    first = jnp.arange(members, dtype=jnp.int32)[None, :]
    row_delta = first // GRID - second // GRID + GRID - 1
    col_delta = first % GRID - second % GRID + GRID - 1
    rel_index = row_delta * span + col_delta
    offsets = jnp.arange(span * span, dtype=jnp.int32)
    return (rel_index[:, :, None] == offsets).astype(jnp.float32)


def swap(a, axis, mask):
    size = lax.axis_size(axis)
    return lax.ppermute(a, axis, [(i, i ^ mask) for i in range(size)])


def sum_over(a, axis):
    parts = [swap(a, axis, mask) for mask in (1, 2, 3)]
    return (a + parts[0]) + (parts[1] + parts[2])


def local(block_input, cotangent, qkv_weight, out_weight, bias_table, norm_gain, norm_shift):
    tile_h, tile_w, width = block_input.shape
    heads, offsets = bias_table.shape
    chips = lax.axis_size(CHIPS)
    devices = chips * lax.axis_size("core")
    owned = tile_h * tile_w // chips // PARTS
    core = lax.axis_index("core")
    onehot = relative_onehot(MEMBERS)
    bias = jnp.einsum(
        "bhr,kqr->bkhq",
        bias_table.reshape(heads // PACK, PACK, offsets),
        onehot,
        precision=lax.Precision.HIGHEST,
    ).reshape(heads // PACK, MEMBERS, PACK * MEMBERS)
    shape = (PARTS, chips, owned, width)
    x, dy = block_input.reshape(shape), cotangent.reshape(shape)
    sent = [pair_of(x, dy, part) for part in range(PARTS)]
    sent[1], bias = lax.optimization_barrier((sent[1], bias))
    got = [lax.all_to_all(part, CHIPS, split_axis=0, concat_axis=0, tiled=True) for part in sent]
    common = (qkv_weight, out_weight, bias, norm_gain, norm_shift, width // heads)
    first, sums, gbias, gvec = backward(got[0], *common)
    second, small, *operands = backward(got[1], *common, (gbias, gvec))
    keep, send = weight_halves(core, *operands, sums)
    small = small + swap(small, "core", 1)
    small = sum_over(small, "z")
    back = outgoing(first, second, keep, swap(send, "core", 1))
    back, small = lax.optimization_barrier((back, small))
    back = lax.all_to_all(back, CHIPS, split_axis=0, concat_axis=0, tiled=True)
    for axis in ("y", ("x_lo", "x_hi")):
        small = sum_over(small, axis)
    factor = float(tile_h * tile_w * devices) ** (-0.5)
    small = small * factor
    table = small[:heads].reshape(heads, 16, 16)[:, : 2 * GRID - 1, : 2 * GRID - 1]
    vectors = small[heads : heads + 4].reshape(2, width)
    grad_input, part = final(back, cotangent.reshape(shape), factor)
    share = part.shape[0] // 2
    mine = lax.dynamic_slice_in_dim(part, core * share, share, 0)
    other = swap(lax.dynamic_slice_in_dim(part, (1 - core) * share, share, 0), "core", 1)
    low = jnp.where(core == 0, mine, other)
    high = jnp.where(core == 0, other, mine)
    grad_qkv = jnp.concatenate((low, high[:, :width]), axis=1)
    grad_out = high[:, width:]
    return (
        grad_input.reshape(tile_h, tile_w, width),
        grad_qkv,
        grad_out,
        table.reshape(heads, offsets),
        vectors[0],
        vectors[1],
    )


def solution(mesh):
    fine = Mesh(mesh.devices.reshape(2, 4, 2, 4, 2), AXES)
    tile = P(("x_lo", "y"), ("x_hi", "z", "core"), None)
    return jax.shard_map(
        local,
        mesh=fine,
        in_specs=(tile, tile, P(), P(), P(), P(), P()),
        out_specs=(tile, P(AXES, None), P(AXES, None), P(), P(), P()),
        check_vma=False,
    )
```

```python
import functools
import jax
import jax.numpy as jnp
from jax import lax
from jax.experimental import pallas as pl
from jax.experimental.pallas import tpu as pltpu
from jax.sharding import Mesh, PartitionSpec as P

GRID = 8
EPSILON = 1e-05
MEMBERS = GRID * GRID
PACK = 4
PARTS = 2
CHUNK = 256


def dot(a, b, ca, cb):
    return lax.dot_general(a, b, (((ca,), (cb,)), ((), ())), preferred_element_type=jnp.float32)


def put(ref, at, value):
    for b in range(ref.shape[0]):
        ref[b, at, :] = value[:, b * 128 : (b + 1) * 128]


def take(ref, at):
    return jnp.concatenate([ref[b, at, :] for b in range(ref.shape[0])], axis=1)


def forward_and_scores(
    pair_ref, wqkv_ref, wout_ref, bias_ref, gain_ref, shift_ref, gbias_ref,
    normed, gproj, att, dyp, hat, istd, proj, gatt, dyf, head_dim, fetches,
):
    width = gproj.shape[1] // 3
    rows, groups, chunk = gproj.shape[0], gproj.shape[0] // MEMBERS, CHUNK
    per, mem = chunk // MEMBERS, chunk // groups
    bf16, f32 = jnp.bfloat16, jnp.float32
    scale = head_dim ** (-0.5)

    def hat_step(c, carry):
        here = pl.ds(pl.multiple_of(c * chunk, chunk), chunk)
        pair = pair_ref[pl.ds(pl.multiple_of(c * mem, mem), mem)].astype(f32)
        x = pair[:, 0].reshape(chunk, width)
        centred = x - jnp.mean(x, axis=-1, keepdims=True)
        inv = lax.rsqrt(jnp.mean(centred * centred, axis=-1, keepdims=True) + EPSILON)
        put(hat, here, centred * inv)
        istd[here, :] = jnp.broadcast_to(inv, (chunk, 128))
        put(dyf, here, pair[:, 1].reshape(chunk, width))
        return carry

    lax.fori_loop(0, rows // chunk, hat_step, 0)
    for fetch in fetches:
        fetch.wait()

    def by_group(ref, c):
        return jnp.concatenate(
            [take(ref, pl.ds(c * per + g, MEMBERS, stride=groups)) for g in range(per)], axis=0
        )

    def norm_step(c, carry):
        here = pl.ds(pl.multiple_of(c * chunk, chunk), chunk)
        nb = (by_group(hat, c) * gain_ref[...] + shift_ref[...]).astype(bf16)
        dy = by_group(dyf, c).astype(bf16)
        dyp[here, :] = dy
        normed[here, :] = nb
        proj[here, :] = dot(nb, wqkv_ref[...], 1, 0).astype(bf16)
        gatt[here, :] = dot(dy, wout_ref[...], 1, 1).astype(bf16)
        return carry

    lax.fori_loop(0, rows // chunk, norm_step, 0)

    lane = lax.broadcasted_iota(jnp.int32, (MEMBERS, 128), 1) // head_dim

    def spread(a):
        zero = jnp.zeros_like(a)
        return jnp.concatenate([jnp.where(lane == h, a, zero) for h in range(PACK)], axis=0)

    def gather(a):
        out = a[:MEMBERS]
        for h in range(1, PACK):
            out = jnp.where(lane == h, a[h * MEMBERS : (h + 1) * MEMBERS], out)
        return out

    blocks = range(width // 128)

    def group_step(g, carry):
        here = pl.ds(pl.multiple_of(g * MEMBERS, MEMBERS), MEMBERS)
        cols = [slice(b * 128, (b + 1) * 128) for b in blocks]
        kcols = [slice(width + b * 128, width + (b + 1) * 128) for b in blocks]
        vcols = [slice(2 * width + b * 128, 2 * width + (b + 1) * 128) for b in blocks]
        ks = [proj[here, c] for c in kcols]
        vs = [proj[here, c] for c in vcols]
        none = jnp.zeros_like(ks[0])
        ws = [jnp.concatenate([spread(proj[here, c]), spread(gatt[here, c])], axis=1) for c in cols]
        both = [
            dot(
                jnp.concatenate(
                    [jnp.concatenate([k, none], axis=1), jnp.concatenate([none, v], axis=1)], axis=0
                ),
                w, 1, 1,
            )
            for k, v, w in zip(ks, vs, ws)
        ]
        pds = []
        for b in blocks:
            scores = both[b][:MEMBERS] * scale + bias_ref[b]
            gp = both[b][MEMBERS:]
            e = jnp.exp(scores - jnp.max(scores, axis=0, keepdims=True))
            p = e * (1.0 / jnp.sum(e, axis=0, keepdims=True))
            gs = p * (gp - jnp.sum(gp * p, axis=0, keepdims=True))
            gbias_ref[b] += gs
            pds.append(jnp.concatenate([p.astype(bf16), (gs * scale).astype(bf16)], axis=0))
        keyed = [dot(pd, w, 1, 0) for pd, w in zip(pds, ws)]
        queried = [
            dot(
                pd,
                jnp.concatenate(
                    [jnp.concatenate([v, none], axis=1), jnp.concatenate([none, k], axis=1)], axis=0
                ),
                0, 0,
            )
            for k, v, pd in zip(ks, vs, pds)
        ]
        for b in blocks:
            att[here, cols[b]] = gather(queried[b][:, :128]).astype(bf16)
            gproj[here, cols[b]] = gather(queried[b][:, 128:]).astype(bf16)
            gproj[here, kcols[b]] = keyed[b][MEMBERS:, :128].astype(bf16)
            gproj[here, vcols[b]] = keyed[b][:MEMBERS, 128:].astype(bf16)
        return carry

    lax.fori_loop(0, groups, group_step, 0)


def back_to_input(wqkv_ref, gain_ref, branch_ref, gproj, hat, istd, dyf):
    width = gproj.shape[1] // 3
    rows, groups, chunk = gproj.shape[0], gproj.shape[0] // MEMBERS, CHUNK
    per, mem = chunk // MEMBERS, chunk // groups
    bf16, f32 = jnp.bfloat16, jnp.float32

    def gn_step(c, carry):
        here = pl.ds(pl.multiple_of(c * chunk, chunk), chunk)
        gn = dot(gproj[here, :], wqkv_ref[...], 1, 1)
        for g in range(per):
            put(dyf, pl.ds(c * per + g, MEMBERS, stride=groups), gn[g * MEMBERS : (g + 1) * MEMBERS])
        return carry

    lax.fori_loop(0, rows // chunk, gn_step, 0)

    def back_step(c, carry):
        gg, gsh = carry
        here = pl.ds(pl.multiple_of(c * chunk, chunk), chunk)
        gn = take(dyf, here)
        normalized = take(hat, here)
        prod = gn * normalized
        gg = gg + jnp.sum(prod.reshape(chunk // 8, 8, width), axis=0)
        gsh = gsh + jnp.sum(gn.reshape(chunk // 8, 8, width), axis=0)
        gh = gn * gain_ref[...]
        m1 = jnp.mean(gh, axis=-1, keepdims=True)
        m2 = jnp.mean(prod * gain_ref[...], axis=-1, keepdims=True)
        inv = istd[here, :][:, :1]
        branch = (inv * (gh - m1 - normalized * m2)).astype(bf16)
        branch_ref[pl.ds(pl.multiple_of(c * mem, mem), mem)] = branch.reshape(mem, groups, width)
        return gg, gsh

    zero = jnp.zeros((8, width), f32)
    gg, gsh = lax.fori_loop(0, rows // chunk, back_step, (zero, zero))
    return jnp.sum(gg, axis=0, keepdims=True), jnp.sum(gsh, axis=0, keepdims=True)


def offset_sums(gbias_ref):
    f32, bf16 = jnp.float32, jnp.bfloat16
    blocks, members, lanes = gbias_ref.shape
    i = lax.broadcasted_iota(jnp.int32, (lanes, 2 * lanes), 0)
    o = lax.broadcasted_iota(jnp.int32, (lanes, 2 * lanes), 1)
    query = i % members
    place = (i // members) * 128 + query // GRID * 16 + query % GRID
    wide = (o == place).astype(f32).astype(bf16)
    frames = []
    for b in range(blocks):
        value = gbias_ref[b]
        high = value.astype(bf16)
        rest = value - high.astype(f32)
        low = rest.astype(bf16)
        lowest = (rest - low.astype(f32)).astype(bf16)
        spread = dot(jnp.concatenate([high, low, lowest], axis=0), wide, 1, 0)
        spread = spread[:members] + (spread[members : 2 * members] + spread[2 * members :])
        frames += [spread[None, :, h * 128 : (h + 1) * 128] for h in range(PACK)]
    frame = jnp.concatenate(frames, axis=0)
    heads = frame.shape[0]
    frame = jnp.concatenate([frame, jnp.zeros_like(frame)], axis=2).reshape(heads * members, 256)
    column = GRID - 1 - lax.broadcasted_iota(jnp.int32, frame.shape, 0) % GRID
    for bit in (1, 2, 4):
        frame = jnp.where((column & bit) != 0, pltpu.roll(frame, bit, 1), frame)
    frame = jnp.sum(frame.reshape(heads * GRID, GRID, 256), axis=1)
    row = GRID - 1 - lax.broadcasted_iota(jnp.int32, frame.shape, 0) % GRID
    for bit in (1, 2, 4):
        frame = jnp.where((row & bit) != 0, pltpu.roll(frame, 16 * bit, 1), frame)
    return jnp.sum(frame.reshape(heads, GRID, 256), axis=1)


def first_kernel(
    pair_ref, wqkv_hbm, wout_hbm, bias_ref, gain_ref, shift_ref,
    branch_ref, sums_hbm, gbias_hbm, gvec_ref,
    wqkv_ref, wout_ref, sums_ref, gbias_ref, normed, gproj, att, dyp, hat, istd, proj, gatt, dyf, sems, *, head_dim,
):
    width = wout_ref.shape[0]
    fetches = [
        pltpu.make_async_copy(wqkv_hbm, wqkv_ref, sems.at[0]),
        pltpu.make_async_copy(wout_hbm, wout_ref, sems.at[1]),
    ]
    for fetch in fetches:
        fetch.start()
    gbias_ref[...] = jnp.zeros_like(gbias_ref)
    forward_and_scores(
        pair_ref, wqkv_ref, wout_ref, bias_ref, gain_ref, shift_ref, gbias_ref,
        normed, gproj, att, dyp, hat, istd, proj, gatt, dyf, head_dim, fetches,
    )
    sums_ref[:, : 3 * width] = dot(normed[...], gproj[...], 0, 0)
    sums_ref[:, 3 * width :] = dot(att[...], dyp[...], 0, 0)
    stores = [
        pltpu.make_async_copy(sums_ref, sums_hbm, sems.at[2]),
        pltpu.make_async_copy(gbias_ref, gbias_hbm, sems.at[3]),
    ]
    for store in stores:
        store.start()
    gain_sum, shift_sum = back_to_input(wqkv_ref, gain_ref, branch_ref, gproj, hat, istd, dyf)
    gvec_ref[0:1, :] = gain_sum
    gvec_ref[1:2, :] = shift_sum
    for store in stores:
        store.wait()


def second_kernel(
    core_ref, pair_ref, wqkv_hbm, wout_hbm, bias_ref, gain_ref, shift_ref, sums_hbm, gbias_hbm,
    keep_ref, send_ref, gbias_ref, gproj, hat, istd,
    wqkv_ref, wout_ref, sums_ref, gbias_before, normed, att, dyp, proj, gatt, dyf, sems, *, head_dim,
):
    fetches = [
        pltpu.make_async_copy(wqkv_hbm, wqkv_ref, sems.at[0]),
        pltpu.make_async_copy(wout_hbm, wout_ref, sems.at[1]),
        pltpu.make_async_copy(gbias_hbm, gbias_before, sems.at[2]),
    ]
    late = pltpu.make_async_copy(sums_hbm, sums_ref, sems.at[3])
    for fetch in fetches:
        fetch.start()
    late.start()
    gbias_ref[...] = jnp.zeros_like(gbias_ref)
    forward_and_scores(
        pair_ref, wqkv_ref, wout_ref, bias_ref, gain_ref, shift_ref, gbias_ref,
        normed, gproj, att, dyp, hat, istd, proj, gatt, dyf, head_dim, fetches,
    )
    gbias_ref[...] += gbias_before[...]
    late.wait()
    half = sums_ref.shape[1] // 2
    gw = dot(normed[...], gproj[...], 0, 0)
    go = dot(att[...], dyp[...], 0, 0)
    low = gw[:, :half] + sums_ref[:, :half]
    high = jnp.concatenate([gw[:, half:], go], axis=1) + sums_ref[:, half:]

    @pl.when(core_ref[0] == 0)
    def _():
        keep_ref[...] = low
        send_ref[...] = high.astype(send_ref.dtype)

    @pl.when(core_ref[0] != 0)
    def _():
        keep_ref[...] = high
        send_ref[...] = low.astype(send_ref.dtype)


def third_kernel(
    wqkv_hbm, gain_ref, gproj, hat, istd, gbias_ref, gvec_ref, branch_ref, small_ref, wqkv_ref, dyf, sem, *, heads
):
    fetch = pltpu.make_async_copy(wqkv_hbm, wqkv_ref, sem)
    fetch.start()
    table = offset_sums(gbias_ref)
    small_ref[:heads, :] = table[:, :128]
    small_ref[heads : 2 * heads, :] = table[:, 128:]
    fetch.wait()
    sums = back_to_input(wqkv_ref, gain_ref, branch_ref, gproj, hat, istd, dyf)
    lanes = hat.shape[0]
    for i in range(2):
        total = sums[i] + gvec_ref[i : i + 1, :]
        for b in range(lanes):
            row = 2 * heads + i * lanes + b
            small_ref[row : row + 1, :] = total[:, b * 128 : (b + 1) * 128]


VMEM = pl.BlockSpec(memory_space=pltpu.VMEM)
SMEM = pl.BlockSpec(memory_space=pltpu.SMEM)
HBM = pl.BlockSpec(memory_space=pltpu.HBM)
MIB = 1024 * 1024


def shaped(*shape, dtype=jnp.float32):
    return jax.ShapeDtypeStruct(shape, dtype)


def cost(flops, size):
    return pl.CostEstimate(flops=flops, bytes_accessed=size, transcendentals=0)


def part_buffers(rows, width):
    bf16, f32 = jnp.bfloat16, jnp.float32
    tall, lanes = (rows, width), (width // 128, rows, 128)
    return [
        (tall, bf16), ((rows, 3 * width), bf16), (tall, bf16), (tall, bf16), (lanes, f32), ((rows, 128), f32),
        ((rows, 3 * width), bf16), (tall, bf16), (lanes, f32),
    ]


def first_part(pair, wqkv, wout, bias, gain, shift, head_dim):
    members, _, groups, width = pair.shape
    sums = (width, 4 * width)
    return pl.pallas_call(
        functools.partial(first_kernel, head_dim=head_dim),
        out_shape=(
            shaped(members, groups, width, dtype=pair.dtype), shaped(*sums), shaped(*bias.shape), shaped(2, width)
        ),
        in_specs=[VMEM, HBM, HBM, VMEM, VMEM, VMEM],
        out_specs=(VMEM, HBM, HBM, VMEM),
        scratch_shapes=[
            pltpu.VMEM(wqkv.shape, wqkv.dtype), pltpu.VMEM(wout.shape, wout.dtype),
            pltpu.VMEM(sums, jnp.float32), pltpu.VMEM(bias.shape, jnp.float32),
        ]
        + [pltpu.VMEM(*b) for b in part_buffers(groups * MEMBERS, width)]
        + [pltpu.SemaphoreType.DMA((4,))],
        compiler_params=pltpu.CompilerParams(vmem_limit_bytes=28 * MIB),
        cost_estimate=cost(10_000_000_000, 8 << 20),
        name="first_part",
    )(pair, wqkv, wout, bias, gain.reshape(1, width), shift.reshape(1, width))


def second_part(core, pair, wqkv, wout, bias, gain, shift, sums, gbias, head_dim):
    members, _, groups, width = pair.shape
    bf16, f32 = jnp.bfloat16, jnp.float32
    normed, gproj, att, dyp, hat, istd, proj, gatt, dyf = part_buffers(groups * MEMBERS, width)
    return pl.pallas_call(
        functools.partial(second_kernel, head_dim=head_dim),
        out_shape=(shaped(width, 2 * width), shaped(width, 2 * width, dtype=bf16), shaped(*bias.shape))
        + tuple(jax.ShapeDtypeStruct(*b) for b in (gproj, hat, istd)),
        in_specs=[SMEM, VMEM, HBM, HBM, VMEM, VMEM, VMEM, HBM, HBM],
        out_specs=(VMEM,) * 6,
        scratch_shapes=[
            pltpu.VMEM(wqkv.shape, wqkv.dtype), pltpu.VMEM(wout.shape, wout.dtype),
            pltpu.VMEM(sums.shape, f32), pltpu.VMEM(bias.shape, f32),
        ]
        + [pltpu.VMEM(*b) for b in (normed, att, dyp, proj, gatt, dyf)]
        + [pltpu.SemaphoreType.DMA((4,))],
        compiler_params=pltpu.CompilerParams(vmem_limit_bytes=28 * MIB),
        cost_estimate=cost(10_000_000_000, 8 << 20),
        name="second_part",
    )(core.reshape(1), pair, wqkv, wout, bias, gain.reshape(1, width), shift.reshape(1, width), sums, gbias)


def second_back(wqkv, gain, gproj, hat, istd, gbias, gvec, groups, heads):
    rows, width = istd.shape[0], gain.shape[0]
    return pl.pallas_call(
        functools.partial(third_kernel, heads=heads),
        out_shape=(
            shaped(MEMBERS, groups, width, dtype=gproj.dtype), shaped(2 * heads + 2 * width // 128, 128)
        ),
        in_specs=[HBM] + [VMEM] * 6,
        out_specs=(VMEM,) * 2,
        scratch_shapes=[
            pltpu.VMEM(wqkv.shape, wqkv.dtype), pltpu.VMEM(hat.shape, jnp.float32), pltpu.SemaphoreType.DMA
        ],
        compiler_params=pltpu.CompilerParams(vmem_limit_bytes=20 * MIB),
        cost_estimate=cost(4_000_000_000, 4 << 20),
        name="second_back",
    )(wqkv, gain.reshape(1, width), gproj, hat, istd, gbias, gvec)


def pair_kernel(x_ref, dy_ref, out_ref):
    out_ref[:, 0] = x_ref[0]
    out_ref[:, 1] = dy_ref[0]


def pair_of(x, dy, part):
    _, chips, groups, width = x.shape
    steps = 2
    source = pl.BlockSpec((1, chips // steps, groups, width), lambda i: (part, i, 0, 0))
    return pl.pallas_call(
        pair_kernel,
        grid=(steps,),
        out_shape=shaped(chips, 2, groups, width, dtype=x.dtype),
        in_specs=[source, source],
        out_specs=pl.BlockSpec((chips // steps, 2, groups, width), lambda i: (i, 0, 0, 0)),
        cost_estimate=cost(0, 2 << 20),
        name="pair",
    )(x, dy)


def outgoing_kernel(first_ref, second_ref, keep_ref, recv_ref, small_ref, out_ref):
    chips, _, groups, _ = out_ref.shape
    lanes = first_ref.shape[2] // 128
    for b in range(lanes):
        cols = slice(b * 128, (b + 1) * 128)
        out_ref[:, b] = first_ref[:, :, cols]
        out_ref[:, lanes + b] = second_ref[:, :, cols]
    for b in range(2 * lanes):
        cols = slice(b * 128, (b + 1) * 128)
        total = (keep_ref[:, cols] + recv_ref[:, cols].astype(jnp.float32)).astype(jnp.bfloat16)
        out_ref[:, 2 * lanes + b] = total.reshape(chips, groups, 128)
    for i in range(small_ref.shape[0] // groups):
        value = small_ref[i * groups : (i + 1) * groups, :].astype(jnp.bfloat16)
        out_ref[:, 4 * lanes + i] = jnp.broadcast_to(value[None], (chips, groups, 128))


def outgoing(first, second, keep, recv, small):
    chips, groups, width = first.shape
    slots = 4 * (width // 128) + small.shape[0] // groups
    return pl.pallas_call(
        outgoing_kernel,
        out_shape=shaped(chips, slots, groups, 128, dtype=first.dtype),
        in_specs=[VMEM] * 5,
        out_specs=VMEM,
        compiler_params=pltpu.CompilerParams(vmem_limit_bytes=20 * MIB),
        cost_estimate=cost(0, 6 << 20),
        name="outgoing",
    )(first, second, keep, recv, small)


def final_kernel(core_ref, got_ref, dy_ref, grad_ref, keep_ref, send_ref, *, factor):
    f32 = jnp.float32
    chips, slots, groups, _ = got_ref.shape
    lanes = dy_ref.shape[3] // 128
    for part in range(PARTS):
        for b in range(lanes):
            cols = slice(b * 128, (b + 1) * 128)
            branch = got_ref[:, part * lanes + b].astype(f32)
            grad_ref[part, :, :, cols] = (dy_ref[part, :, :, cols].astype(f32) + branch).astype(grad_ref.dtype)
    total = got_ref[0, 2 * lanes :].astype(f32)
    for chip in range(1, chips):
        total = total + got_ref[chip, 2 * lanes :].astype(f32)
    total = total * factor
    share = groups // 2
    for b in range(2 * lanes):
        rows = slice(b * share, (b + 1) * share)
        low, high = total[b, :share], total[b, share:]
        keep_ref[rows, :] = jnp.where(core_ref[0] == 0, low, high)
        send_ref[rows, :] = jnp.where(core_ref[0] == 0, high, low)
    for i in range(2 * lanes, slots - 2 * lanes):
        rows = slice(2 * lanes * share + (i - 2 * lanes) * groups, 2 * lanes * share + (i - 2 * lanes + 1) * groups)
        keep_ref[rows, :] = total[i]
        send_ref[rows, :] = total[i]


def final(core, got, dy, factor):
    chips, slots, groups, _ = got.shape
    lanes = dy.shape[3] // 128
    rows = 2 * lanes * (groups // 2) + (slots - 4 * lanes) * groups
    return pl.pallas_call(
        functools.partial(final_kernel, factor=factor),
        out_shape=(jax.ShapeDtypeStruct(dy.shape, dy.dtype), shaped(rows, 128), shaped(rows, 128)),
        in_specs=[SMEM, VMEM, VMEM],
        out_specs=(VMEM,) * 3,
        compiler_params=pltpu.CompilerParams(vmem_limit_bytes=16 * MIB),
        cost_estimate=cost(0, 6 << 20),
        name="final",
    )(core.reshape(1), got, dy)


def finish_kernel(core_ref, keep_ref, recv_ref, qkv_ref, out_ref, table_ref, gain_ref, shift_ref):
    width = out_ref.shape[1]
    lanes = width // 128
    share, heads = out_ref.shape[0], table_ref.shape[0]
    first = core_ref[0] == 0
    for b in range(4 * lanes):
        rows = slice(b % (2 * lanes) * share, (b % (2 * lanes) + 1) * share)
        mine, other = keep_ref[rows, :], recv_ref[rows, :]
        value = jnp.where(first, mine, other) if b < 2 * lanes else jnp.where(first, other, mine)
        if b < 3 * lanes:
            qkv_ref[:, b * 128 : (b + 1) * 128] = value
        else:
            out_ref[:, (b - 3 * lanes) * 128 : (b - 3 * lanes + 1) * 128] = value
    at = 2 * lanes * share
    small = keep_ref[at:, :] + recv_ref[at:, :]
    table = jnp.concatenate([small[:heads], small[heads : 2 * heads]], axis=1)
    side = 2 * GRID - 1
    for i in range(side):
        table_ref[:, i * side : (i + 1) * side] = table[:, i * 16 : i * 16 + side]
    for ref, row in ((gain_ref, 2 * heads), (shift_ref, 2 * heads + lanes)):
        for b in range(lanes):
            ref[:, b * 128 : (b + 1) * 128] = small[row + b : row + b + 1, :]


def finish(core, keep, recv, width, heads, offsets):
    share = (keep.shape[0] - 2 * heads - 2 * width // 128) // (2 * width // 128)
    return pl.pallas_call(
        finish_kernel,
        out_shape=(
            shaped(share, 3 * width), shaped(share, width), shaped(heads, offsets), shaped(1, width), shaped(1, width)
        ),
        in_specs=[SMEM, VMEM, VMEM],
        out_specs=(VMEM,) * 5,
        name="finish",
    )(core.reshape(1), keep, recv)


AXES = ("x_lo", "y", "x_hi", "z", "core")
CHIPS = AXES[:4]


def relative_onehot(members):
    span = 2 * GRID - 1
    second = jnp.arange(members, dtype=jnp.int32)[:, None]
    first = jnp.arange(members, dtype=jnp.int32)[None, :]
    row_delta = first // GRID - second // GRID + GRID - 1
    col_delta = first % GRID - second % GRID + GRID - 1
    rel_index = row_delta * span + col_delta
    offsets = jnp.arange(span * span, dtype=jnp.int32)
    return (rel_index[:, :, None] == offsets).astype(jnp.float32)


def swap(a, axis, mask):
    size = lax.axis_size(axis)
    return lax.ppermute(a, axis, [(i, i ^ mask) for i in range(size)])


def local(block_input, cotangent, qkv_weight, out_weight, bias_table, norm_gain, norm_shift):
    tile_h, tile_w, width = block_input.shape
    heads, offsets = bias_table.shape
    chips = lax.axis_size(CHIPS)
    devices = chips * lax.axis_size("core")
    owned = tile_h * tile_w // chips // PARTS
    core = lax.axis_index("core")
    onehot = relative_onehot(MEMBERS)
    bias = jnp.einsum(
        "bhr,kqr->bkhq",
        bias_table.reshape(heads // PACK, PACK, offsets),
        onehot,
        precision=lax.Precision.HIGHEST,
    ).reshape(heads // PACK, MEMBERS, PACK * MEMBERS)
    shape = (PARTS, chips, owned, width)
    x, dy = block_input.reshape(shape), cotangent.reshape(shape)
    sent = [pair_of(x, dy, part) for part in range(PARTS)]
    exchange = functools.partial(lax.all_to_all, axis_name=CHIPS, split_axis=0, concat_axis=0, tiled=True)
    got = [exchange(sent[0])]
    got[0], sent[1], bias = lax.optimization_barrier((got[0], sent[1], bias))
    got.append(exchange(sent[1]))
    head_dim = width // heads
    common = (qkv_weight, out_weight, bias, norm_gain, norm_shift)
    first, sums, gbias, gvec = first_part(got[0], *common, head_dim)
    keep, send, gbias, gproj, hat, istd = second_part(core, got[1], *common, sums, gbias, head_dim)
    recv = swap(send, "core", 1)
    second, small = second_back(qkv_weight, norm_gain, gproj, hat, istd, gbias, gvec, owned, heads)
    back = outgoing(first, second, keep, recv, small)
    back = exchange(back)
    factor = float(tile_h * tile_w * devices) ** (-0.5)
    grad_input, mine, theirs = final(core, back, dy, factor)
    grad_qkv, grad_out, table, gain, shift = finish(core, mine, swap(theirs, "core", 1), width, heads, offsets)
    return (
        grad_input.reshape(tile_h, tile_w, width),
        grad_qkv,
        grad_out,
        table,
        gain.reshape(width),
        shift.reshape(width),
    )


def solution(mesh):
    fine = Mesh(mesh.devices.reshape(2, 4, 2, 4, 2), AXES)
    tile = P(("x_lo", "y"), ("x_hi", "z", "core"), None)
    return jax.shard_map(
        local,
        mesh=fine,
        in_specs=(tile, tile, P(), P(), P(), P(), P()),
        out_specs=(tile, P(AXES, None), P(AXES, None), P(), P(), P()),
        check_vma=False,
    )
```

```python
import functools
import jax
import jax.numpy as jnp
from jax import lax
from jax.experimental import pallas as pl
from jax.experimental.pallas import tpu as pltpu
from jax.sharding import Mesh, PartitionSpec as P

GRID = 8
EPSILON = 1e-05
MEMBERS = GRID * GRID
PACK = 4
CHUNK = 256


def dot(a, b, ca, cb):
    return lax.dot_general(a, b, (((ca,), (cb,)), ((), ())), preferred_element_type=jnp.float32)


def put(ref, at, value):
    for b in range(ref.shape[0]):
        ref[b, at, :] = value[:, b * 128 : (b + 1) * 128]


def take(ref, at):
    return jnp.concatenate([ref[b, at, :] for b in range(ref.shape[0])], axis=1)


def forward_and_scores(
    pair_ref, wqkv_ref, wout_ref, bias_ref, gain_ref, shift_ref, gbias_ref,
    normed, gproj, att, dyp, hat, istd, proj, gatt, dyf, head_dim,
):
    width = gproj.shape[1] // 3
    rows, groups, chunk = gproj.shape[0], gproj.shape[0] // MEMBERS, CHUNK
    per, mem = chunk // MEMBERS, chunk // groups
    bf16, f32 = jnp.bfloat16, jnp.float32
    scale = head_dim ** (-0.5)

    def hat_step(c, carry):
        here = pl.ds(pl.multiple_of(c * chunk, chunk), chunk)
        pair = pair_ref[pl.ds(pl.multiple_of(c * mem, mem), mem)].astype(f32)
        x = pair[:, 0].reshape(chunk, width)
        centred = x - jnp.mean(x, axis=-1, keepdims=True)
        inv = lax.rsqrt(jnp.mean(centred * centred, axis=-1, keepdims=True) + EPSILON)
        put(hat, here, centred * inv)
        istd[here, :] = jnp.broadcast_to(inv, (chunk, 128))
        put(dyf, here, pair[:, 1].reshape(chunk, width))
        return carry

    lax.fori_loop(0, rows // chunk, hat_step, 0)

    def by_group(ref, c):
        return jnp.concatenate(
            [take(ref, pl.ds(c * per + g, MEMBERS, stride=groups)) for g in range(per)], axis=0
        )

    def norm_step(c, carry):
        here = pl.ds(pl.multiple_of(c * chunk, chunk), chunk)
        nb = (by_group(hat, c) * gain_ref[...] + shift_ref[...]).astype(bf16)
        dy = by_group(dyf, c).astype(bf16)
        dyp[here, :] = dy
        normed[here, :] = nb
        proj[here, :] = dot(nb, wqkv_ref[...], 1, 0).astype(bf16)
        gatt[here, :] = dot(dy, wout_ref[...], 1, 1).astype(bf16)
        return carry

    lax.fori_loop(0, rows // chunk, norm_step, 0, unroll=True)

    lane = lax.broadcasted_iota(jnp.int32, (MEMBERS, 128), 1) // head_dim

    def spread(a):
        zero = jnp.zeros_like(a)
        return jnp.concatenate([jnp.where(lane == h, a, zero) for h in range(PACK)], axis=0)

    def gather(a):
        out = a[:MEMBERS]
        for h in range(1, PACK):
            out = jnp.where(lane == h, a[h * MEMBERS : (h + 1) * MEMBERS], out)
        return out

    blocks = range(width // 128)

    def group_step(g, carry):
        here = pl.ds(pl.multiple_of(g * MEMBERS, MEMBERS), MEMBERS)
        cols = [slice(b * 128, (b + 1) * 128) for b in blocks]
        kcols = [slice(width + b * 128, width + (b + 1) * 128) for b in blocks]
        vcols = [slice(2 * width + b * 128, 2 * width + (b + 1) * 128) for b in blocks]
        ks = [proj[here, c] for c in kcols]
        vs = [proj[here, c] for c in vcols]
        none = jnp.zeros_like(ks[0])
        ws = [jnp.concatenate([spread(proj[here, c]), spread(gatt[here, c])], axis=1) for c in cols]
        both = [
            dot(
                jnp.concatenate(
                    [jnp.concatenate([k, none], axis=1), jnp.concatenate([none, v], axis=1)], axis=0
                ),
                w, 1, 1,
            )
            for k, v, w in zip(ks, vs, ws)
        ]
        pds = []
        for b in blocks:
            scores = both[b][:MEMBERS] * scale + bias_ref[b]
            gp = both[b][MEMBERS:]
            e = jnp.exp(scores - jnp.max(scores, axis=0, keepdims=True))
            p = e * (1.0 / jnp.sum(e, axis=0, keepdims=True))
            gs = p * (gp - jnp.sum(gp * p, axis=0, keepdims=True))
            gbias_ref[b] += gs
            pds.append(jnp.concatenate([p.astype(bf16), (gs * scale).astype(bf16)], axis=0))
        keyed = [dot(pd, w, 1, 0) for pd, w in zip(pds, ws)]
        queried = [
            dot(
                pd,
                jnp.concatenate(
                    [jnp.concatenate([v, none], axis=1), jnp.concatenate([none, k], axis=1)], axis=0
                ),
                0, 0,
            )
            for k, v, pd in zip(ks, vs, pds)
        ]
        for b in blocks:
            att[here, cols[b]] = gather(queried[b][:, :128]).astype(bf16)
            gproj[here, cols[b]] = gather(queried[b][:, 128:]).astype(bf16)
            gproj[here, kcols[b]] = keyed[b][MEMBERS:, :128].astype(bf16)
            gproj[here, vcols[b]] = keyed[b][:MEMBERS, 128:].astype(bf16)
        return carry

    lax.fori_loop(0, groups, group_step, 0, unroll=4)


def back_to_input(wqkv_ref, gain_ref, branch_ref, gproj, hat, istd, dyf):
    width = gproj.shape[1] // 3
    rows, groups, chunk = gproj.shape[0], gproj.shape[0] // MEMBERS, CHUNK
    per, mem = chunk // MEMBERS, chunk // groups
    bf16, f32 = jnp.bfloat16, jnp.float32

    def gn_step(c, carry):
        here = pl.ds(pl.multiple_of(c * chunk, chunk), chunk)
        gn = dot(gproj[here, :], wqkv_ref[...], 1, 1)
        for g in range(per):
            put(dyf, pl.ds(c * per + g, MEMBERS, stride=groups), gn[g * MEMBERS : (g + 1) * MEMBERS])
        return carry

    lax.fori_loop(0, rows // chunk, gn_step, 0, unroll=True)

    def back_step(c, carry):
        gg, gsh = carry
        here = pl.ds(pl.multiple_of(c * chunk, chunk), chunk)
        gn = take(dyf, here)
        normalized = take(hat, here)
        prod = gn * normalized
        gg = gg + jnp.sum(prod.reshape(chunk // 8, 8, width), axis=0)
        gsh = gsh + jnp.sum(gn.reshape(chunk // 8, 8, width), axis=0)
        gh = gn * gain_ref[...]
        m1 = jnp.mean(gh, axis=-1, keepdims=True)
        m2 = jnp.mean(prod * gain_ref[...], axis=-1, keepdims=True)
        inv = istd[here, :][:, :1]
        branch = (inv * (gh - m1 - normalized * m2)).astype(bf16)
        branch_ref[pl.ds(pl.multiple_of(c * mem, mem), mem)] = branch.reshape(mem, groups, width)
        return gg, gsh

    zero = jnp.zeros((8, width), f32)
    gg, gsh = lax.fori_loop(0, rows // chunk, back_step, (zero, zero))
    return jnp.sum(gg, axis=0, keepdims=True), jnp.sum(gsh, axis=0, keepdims=True)


def offset_sums(gbias_ref):
    f32, bf16 = jnp.float32, jnp.bfloat16
    blocks, members, lanes = gbias_ref.shape
    i = lax.broadcasted_iota(jnp.int32, (lanes, 2 * lanes), 0)
    o = lax.broadcasted_iota(jnp.int32, (lanes, 2 * lanes), 1)
    query = i % members
    place = (i // members) * 128 + query // GRID * 16 + query % GRID
    wide = (o == place).astype(f32).astype(bf16)
    frames = []
    for b in range(blocks):
        value = gbias_ref[b]
        high = value.astype(bf16)
        rest = value - high.astype(f32)
        low = rest.astype(bf16)
        lowest = (rest - low.astype(f32)).astype(bf16)
        spread = dot(jnp.concatenate([high, low, lowest], axis=0), wide, 1, 0)
        spread = spread[:members] + (spread[members : 2 * members] + spread[2 * members :])
        frames += [spread[None, :, h * 128 : (h + 1) * 128] for h in range(PACK)]
    frame = jnp.concatenate(frames, axis=0)
    heads = frame.shape[0]
    frame = jnp.concatenate([frame, jnp.zeros_like(frame)], axis=2).reshape(heads * members, 256)
    column = GRID - 1 - lax.broadcasted_iota(jnp.int32, frame.shape, 0) % GRID
    for bit in (1, 2, 4):
        frame = jnp.where((column & bit) != 0, pltpu.roll(frame, bit, 1), frame)
    frame = jnp.sum(frame.reshape(heads * GRID, GRID, 256), axis=1)
    row = GRID - 1 - lax.broadcasted_iota(jnp.int32, frame.shape, 0) % GRID
    for bit in (1, 2, 4):
        frame = jnp.where((row & bit) != 0, pltpu.roll(frame, 16 * bit, 1), frame)
    return jnp.sum(frame.reshape(heads, GRID, 256), axis=1)


def scores_kernel(
    core_ref, pair_ref, wqkv_ref, wout_ref, bias_ref, gain_ref, shift_ref,
    keep_ref, send_ref, table_ref, gproj, hat, istd,
    gbias_ref, normed, att, dyp, proj, gatt, dyf, *, head_dim,
):
    gbias_ref[...] = jnp.zeros_like(gbias_ref)
    forward_and_scores(
        pair_ref, wqkv_ref, wout_ref, bias_ref, gain_ref, shift_ref, gbias_ref,
        normed, gproj, att, dyp, hat, istd, proj, gatt, dyf, head_dim,
    )
    width = wout_ref.shape[0]
    half = 2 * width
    first = core_ref[0] == 0
    table = offset_sums(gbias_ref)
    heads = table.shape[0] // 2
    table_ref[...] = jnp.where(first, table[:heads], table[heads:])
    send_ref[width:, :] = jnp.zeros((send_ref.shape[0] - width, half), send_ref.dtype)
    send_ref[width : width + heads, :256] = jnp.where(first, table[heads:], table[:heads]).astype(send_ref.dtype)

    @pl.when(first)
    def _():
        keep_ref[...] = dot(normed[...], gproj[:, :half], 0, 0)
        send_ref[:width, :width] = dot(normed[...], gproj[:, half:], 0, 0).astype(send_ref.dtype)
        send_ref[:width, width:] = dot(att[...], dyp[...], 0, 0).astype(send_ref.dtype)

    @pl.when(jnp.logical_not(first))
    def _():
        send_ref[:width, :] = dot(normed[...], gproj[:, :half], 0, 0).astype(send_ref.dtype)
        keep_ref[:, :width] = dot(normed[...], gproj[:, half:], 0, 0)
        keep_ref[:, width:] = dot(att[...], dyp[...], 0, 0)


def back_kernel(wqkv_ref, gain_ref, gproj, hat, istd, branch_ref, gvec_ref, dyf):
    sums = back_to_input(wqkv_ref, gain_ref, branch_ref, gproj, hat, istd, dyf)
    lanes = hat.shape[0]
    for i in range(2):
        for b in range(lanes):
            gvec_ref[i * lanes + b : i * lanes + b + 1, :] = sums[i][:, b * 128 : (b + 1) * 128]


VMEM = pl.BlockSpec(memory_space=pltpu.VMEM)
SMEM = pl.BlockSpec(memory_space=pltpu.SMEM)
MIB = 1024 * 1024


def shaped(*shape, dtype=jnp.float32):
    return jax.ShapeDtypeStruct(shape, dtype)


def cost(flops, size):
    return pl.CostEstimate(flops=flops, bytes_accessed=size, transcendentals=0)


def part_buffers(rows, width):
    bf16, f32 = jnp.bfloat16, jnp.float32
    tall, lanes = (rows, width), (width // 128, rows, 128)
    return [
        (tall, bf16), ((rows, 3 * width), bf16), (tall, bf16), (tall, bf16), (lanes, f32), ((rows, 128), f32),
        ((rows, 3 * width), bf16), (tall, bf16), (lanes, f32),
    ]


def local_scores(core, pair, wqkv, wout, bias, gain, shift, head_dim):
    members, _, groups, width = pair.shape
    bf16, f32 = jnp.bfloat16, jnp.float32
    normed, gproj, att, dyp, hat, istd, proj, gatt, dyf = part_buffers(groups * MEMBERS, width)
    half_heads = width // head_dim // 2
    return pl.pallas_call(
        functools.partial(scores_kernel, head_dim=head_dim),
        out_shape=(
            shaped(width, 2 * width), shaped(width + 16, 2 * width, dtype=bf16), shaped(half_heads, 256)
        )
        + tuple(jax.ShapeDtypeStruct(*b) for b in (gproj, hat, istd)),
        in_specs=[SMEM] + [VMEM] * 6,
        out_specs=(VMEM,) * 6,
        scratch_shapes=[pltpu.VMEM(bias.shape, f32)]
        + [pltpu.VMEM(*b) for b in (normed, att, dyp, proj, gatt, dyf)],
        compiler_params=pltpu.CompilerParams(vmem_limit_bytes=28 * MIB),
        cost_estimate=cost(20_000_000_000, 8 << 20),
        name="scores",
    )(core.reshape(1), pair, wqkv, wout, bias, gain.reshape(1, width), shift.reshape(1, width))


def local_back(wqkv, gain, gproj, hat, istd, groups):
    width = gain.shape[0]
    return pl.pallas_call(
        back_kernel,
        out_shape=(shaped(MEMBERS, groups, width, dtype=gproj.dtype), shaped(2 * width // 128, 128)),
        in_specs=[VMEM] * 5,
        out_specs=(VMEM,) * 2,
        scratch_shapes=[pltpu.VMEM(hat.shape, jnp.float32)],
        compiler_params=pltpu.CompilerParams(vmem_limit_bytes=16 * MIB),
        cost_estimate=cost(6_000_000_000, 4 << 20),
        name="back",
    )(wqkv, gain.reshape(1, width), gproj, hat, istd)


def pair_kernel(x_ref, dy_ref, out_ref):
    out_ref[:, 0] = x_ref[...]
    out_ref[:, 1] = dy_ref[...]


def pair_of(x, dy):
    chips, groups, width = x.shape
    step = chips // 4
    source = pl.BlockSpec((step, groups, width), lambda i: (i, 0, 0))
    return pl.pallas_call(
        pair_kernel,
        grid=(chips // step,),
        out_shape=shaped(chips, 2, groups, width, dtype=x.dtype),
        in_specs=[source, source],
        out_specs=pl.BlockSpec((step, 2, groups, width), lambda i: (i, 0, 0, 0)),
        cost_estimate=cost(0, 4 << 20),
        name="pair",
    )(x, dy)


def outgoing_kernel(branch_ref, keep_ref, recv_ref, table_ref, gvec_ref, out_ref):
    chips, _, share, _ = out_ref.shape
    _, groups, width = branch_ref.shape
    f32, bf16 = jnp.float32, jnp.bfloat16
    slot = 0
    for b in range(width // 128):
        for t in range(groups // share):
            out_ref[:, slot] = branch_ref[:, t * share : (t + 1) * share, b * 128 : (b + 1) * 128]
            slot += 1
    for b in range(2 * width // 128):
        cols = slice(b * 128, (b + 1) * 128)
        total = (keep_ref[:, cols] + recv_ref[:width, cols].astype(f32)).astype(bf16)
        out_ref[:, slot] = total.reshape(chips, share, 128)
        slot += 1
    table = table_ref[...] + recv_ref[width : width + share, :256].astype(f32)
    for value in (table[:, :128], table[:, 128:], gvec_ref[...]):
        out_ref[:, slot] = jnp.broadcast_to(value.astype(bf16)[None], (chips, share, 128))
        slot += 1


def outgoing(branch, keep, recv, table, gvec):
    chips, groups, width = branch.shape
    share = width // chips
    slots = groups // share * width // 128 + 2 * width // 128 + 3
    return pl.pallas_call(
        outgoing_kernel,
        out_shape=shaped(chips, slots, share, 128, dtype=branch.dtype),
        in_specs=[VMEM] * 5,
        out_specs=VMEM,
        compiler_params=pltpu.CompilerParams(vmem_limit_bytes=16 * MIB),
        cost_estimate=cost(0, 6 << 20),
        name="outgoing",
    )(branch, keep, recv, table, gvec)


def sums_kernel(core_ref, got_ref, keep_ref, send_ref, *, begin, factor):
    f32 = jnp.float32
    chips, slots, share, _ = got_ref.shape
    total = got_ref[0, begin:].astype(f32)
    for chip in range(1, chips):
        total = total + got_ref[chip, begin:].astype(f32)
    total = total * factor
    part = share // 2
    weights = slots - begin - 3
    for b in range(weights):
        rows = slice(b * part, (b + 1) * part)
        low, high = total[b, :part], total[b, part:]
        keep_ref[rows, :] = jnp.where(core_ref[0] == 0, low, high)
        send_ref[rows, :] = jnp.where(core_ref[0] == 0, high, low)
    for i in range(3):
        rows = slice(weights * part + i * share, weights * part + (i + 1) * share)
        keep_ref[rows, :] = total[weights + i]
        send_ref[rows, :] = total[weights + i]


def sums_of(core, got, begin, factor):
    chips, slots, share, _ = got.shape
    rows = (slots - begin - 3) * share // 2 + 3 * share
    return pl.pallas_call(
        functools.partial(sums_kernel, begin=begin, factor=factor),
        out_shape=(shaped(rows, 128), shaped(rows, 128)),
        in_specs=[SMEM, VMEM],
        out_specs=(VMEM,) * 2,
        compiler_params=pltpu.CompilerParams(vmem_limit_bytes=16 * MIB),
        cost_estimate=cost(0, 2 << 20),
        name="sums",
    )(core.reshape(1), got)


def input_kernel(got_ref, dy_ref, grad_ref):
    _, groups, width = dy_ref.shape
    share = got_ref.shape[2]
    f32 = jnp.float32
    slot = 0
    for b in range(width // 128):
        cols = slice(b * 128, (b + 1) * 128)
        for t in range(groups // share):
            rows = slice(t * share, (t + 1) * share)
            branch = got_ref[:, slot].astype(f32)
            grad_ref[:, rows, cols] = (dy_ref[:, rows, cols].astype(f32) + branch).astype(grad_ref.dtype)
            slot += 1


def input_gradient(got, dy):
    return pl.pallas_call(
        input_kernel,
        out_shape=jax.ShapeDtypeStruct(dy.shape, dy.dtype),
        in_specs=[VMEM] * 2,
        out_specs=VMEM,
        compiler_params=pltpu.CompilerParams(vmem_limit_bytes=16 * MIB),
        cost_estimate=cost(0, 4 << 20),
        name="input_gradient",
    )(got, dy)


def finish_kernel(core_ref, keep_ref, recv_ref, qkv_ref, out_ref, table_ref, gain_ref, shift_ref):
    width = out_ref.shape[1]
    lanes = width // 128
    part, heads = out_ref.shape[0], table_ref.shape[0] // 2
    first = core_ref[0] == 0

    def ordered(mine, other):
        return jnp.where(first, mine, other), jnp.where(first, other, mine)

    for b in range(2 * lanes):
        rows = slice(b * part, (b + 1) * part)
        low, high = ordered(keep_ref[rows, :], recv_ref[rows, :])
        qkv_ref[:, b * 128 : (b + 1) * 128] = low
        if b < lanes:
            qkv_ref[:, 2 * width + b * 128 : 2 * width + (b + 1) * 128] = high
        else:
            out_ref[:, (b - lanes) * 128 : (b - lanes + 1) * 128] = high
    at = 2 * lanes * part
    halves = [jnp.concatenate([ref[at : at + heads], ref[at + heads : at + 2 * heads]], axis=1) for ref in (keep_ref, recv_ref)]
    table = jnp.concatenate(ordered(*halves), axis=0)
    side = 2 * GRID - 1
    place = lax.broadcasted_iota(jnp.int32, (256, side * side), 0)
    offset = lax.broadcasted_iota(jnp.int32, (256, side * side), 1)
    pick = (place == offset // side * 16 + offset % side).astype(jnp.float32)
    table_ref[...] = lax.dot_general(
        table, pick, (((1,), (0,)), ((), ())), precision=lax.Precision.HIGHEST, preferred_element_type=jnp.float32
    )
    at += 2 * heads
    vectors = keep_ref[at:, :] + recv_ref[at:, :]
    for ref, row in ((gain_ref, 0), (shift_ref, lanes)):
        for b in range(lanes):
            ref[:, b * 128 : (b + 1) * 128] = vectors[row + b : row + b + 1]


def finish(core, keep, recv, part, width, heads, offsets):
    return pl.pallas_call(
        finish_kernel,
        out_shape=(
            shaped(part, 3 * width), shaped(part, width), shaped(heads, offsets), shaped(1, width), shaped(1, width)
        ),
        in_specs=[SMEM, VMEM, VMEM],
        out_specs=(VMEM,) * 5,
        name="finish",
    )(core.reshape(1), keep, recv)


AXES = ("x_lo", "y", "x_hi", "z", "core")
CHIPS = AXES[:4]


def relative_onehot(members):
    span = 2 * GRID - 1
    second = jnp.arange(members, dtype=jnp.int32)[:, None]
    first = jnp.arange(members, dtype=jnp.int32)[None, :]
    row_delta = first // GRID - second // GRID + GRID - 1
    col_delta = first % GRID - second % GRID + GRID - 1
    rel_index = row_delta * span + col_delta
    offsets = jnp.arange(span * span, dtype=jnp.int32)
    return (rel_index[:, :, None] == offsets).astype(jnp.float32)


def swap(a, axis, mask):
    size = lax.axis_size(axis)
    return lax.ppermute(a, axis, [(i, i ^ mask) for i in range(size)])


def local(block_input, cotangent, qkv_weight, out_weight, bias_table, norm_gain, norm_shift):
    tile_h, tile_w, width = block_input.shape
    heads, offsets = bias_table.shape
    chips = lax.axis_size(CHIPS)
    devices = chips * lax.axis_size("core")
    owned = tile_h * tile_w // chips
    core = lax.axis_index("core")
    onehot = relative_onehot(MEMBERS)
    bias = jnp.einsum(
        "bhr,kqr->bkhq",
        bias_table.reshape(heads // PACK, PACK, offsets),
        onehot,
        precision=lax.Precision.HIGHEST,
    ).reshape(heads // PACK, MEMBERS, PACK * MEMBERS)
    x = block_input.reshape(chips, owned, width)
    dy = cotangent.reshape(chips, owned, width)
    exchange = functools.partial(lax.all_to_all, axis_name=CHIPS, split_axis=0, concat_axis=0, tiled=True)
    got = exchange(pair_of(x, dy))
    keep, send, table, gproj, hat, istd = local_scores(
        core, got, qkv_weight, out_weight, bias, norm_gain, norm_shift, width // heads
    )
    recv = swap(send, "core", 1)
    branch, gvec = local_back(qkv_weight, norm_gain, gproj, hat, istd, owned)
    got = exchange(outgoing(branch, keep, recv, table, gvec))
    factor = float(tile_h * tile_w * devices) ** (-0.5)
    share = width // chips
    mine, theirs = sums_of(core, got, owned // share * width // 128, factor)
    recv = swap(theirs, "core", 1)
    grad_input = input_gradient(got, dy)
    grad_qkv, grad_out, table, gain, shift = finish(core, mine, recv, share // 2, width, heads, offsets)
    return (
        grad_input.reshape(tile_h, tile_w, width),
        grad_qkv,
        grad_out,
        table,
        gain.reshape(width),
        shift.reshape(width),
    )


def solution(mesh):
    fine = Mesh(mesh.devices.reshape(2, 4, 2, 4, 2), AXES)
    tile = P(("x_lo", "y"), ("x_hi", "z", "core"), None)
    return jax.shard_map(
        local,
        mesh=fine,
        in_specs=(tile, tile, P(), P(), P(), P(), P()),
        out_specs=(tile, P(AXES, None), P(AXES, None), P(), P(), P()),
        check_vma=False,
    )
```

```python
import functools
import jax
import jax.numpy as jnp
from jax import lax
from jax.experimental import pallas as pl
from jax.experimental.pallas import tpu as pltpu
from jax.sharding import Mesh, PartitionSpec as P

GRID = 8
EPSILON = 1e-05
MEMBERS = GRID * GRID
PACK = 4
CHUNK = 256


def dot(a, b, ca, cb):
    return lax.dot_general(a, b, (((ca,), (cb,)), ((), ())), preferred_element_type=jnp.float32)


def put(ref, at, value):
    for b in range(ref.shape[0]):
        ref[b, at, :] = value[:, b * 128 : (b + 1) * 128]


def take(ref, at):
    return jnp.concatenate([ref[b, at, :] for b in range(ref.shape[0])], axis=1)


def by_group(ref, c, per, groups):
    return jnp.concatenate([take(ref, pl.ds(c * per + g, MEMBERS, stride=groups)) for g in range(per)], axis=0)


def spread(a, lane):
    zero = jnp.zeros_like(a)
    return jnp.concatenate([jnp.where(lane == h, a, zero) for h in range(PACK)], axis=0)


def gather(a, lane):
    out = a[:MEMBERS]
    for h in range(1, PACK):
        out = jnp.where(lane == h, a[h * MEMBERS : (h + 1) * MEMBERS], out)
    return out


def by_query(weights, values):
    none = jnp.zeros_like(values[0])
    out = []
    for b in range(0, len(weights), 2):
        pair = jnp.concatenate(
            [
                jnp.concatenate([values[b], none], axis=1),
                jnp.concatenate([none, values[b + 1]], axis=1),
            ],
            axis=0,
        )
        both = dot(jnp.concatenate(weights[b : b + 2], axis=0), pair, 0, 0)
        out += [both[:, :128], both[:, 128:]]
    return out


def head_lanes(head_dim):
    return lax.broadcasted_iota(jnp.int32, (MEMBERS, 128), 1) // head_dim


def column_blocks(width):
    blocks = range(width // 128)
    return [[slice(i * width + b * 128, i * width + (b + 1) * 128) for b in blocks] for i in range(3)]


def forward_kernel(
    x_ref, wqkv_ref, bias_ref, gain_ref, shift_ref, normed, proj, hat, istd, prob_ref, att, *, head_dim
):
    _, groups, width = x_ref.shape
    rows, chunk = groups * MEMBERS, CHUNK
    per, mem = chunk // MEMBERS, chunk // groups
    bf16, f32 = jnp.bfloat16, jnp.float32
    scale = head_dim ** (-0.5)

    def hat_step(c, carry):
        here = pl.ds(pl.multiple_of(c * chunk, chunk), chunk)
        x = x_ref[pl.ds(pl.multiple_of(c * mem, mem), mem)].astype(f32).reshape(chunk, width)
        centred = x - jnp.mean(x, axis=-1, keepdims=True)
        inv = lax.rsqrt(jnp.mean(centred * centred, axis=-1, keepdims=True) + EPSILON)
        put(hat, here, centred * inv)
        istd[here, :] = jnp.broadcast_to(inv, (chunk, 128))
        return carry

    lax.fori_loop(0, rows // chunk, hat_step, 0)

    def norm_step(c, carry):
        here = pl.ds(pl.multiple_of(c * chunk, chunk), chunk)
        nb = (by_group(hat, c, per, groups) * gain_ref[...] + shift_ref[...]).astype(bf16)
        normed[here, :] = nb
        proj[here, :] = dot(nb, wqkv_ref[...], 1, 0).astype(bf16)
        return carry

    lax.fori_loop(0, rows // chunk, norm_step, 0, unroll=True)

    lane = head_lanes(head_dim)
    qcols, kcols, vcols = column_blocks(width)

    def group_step(g, carry):
        here = pl.ds(pl.multiple_of(g * MEMBERS, MEMBERS), MEMBERS)
        probs = []
        scores = [dot(proj[here, k], spread(proj[here, q], lane), 1, 1) for q, k in zip(qcols, kcols)]
        for b, score in enumerate(scores):
            score = score * scale + bias_ref[b]
            e = jnp.exp(score - jnp.max(score, axis=0, keepdims=True))
            p = e * (1.0 / jnp.sum(e, axis=0, keepdims=True))
            prob_ref[b, here, :] = p
            probs.append(p.astype(bf16))
        attended = by_query(probs, [proj[here, c] for c in vcols])
        for b, value in enumerate(attended):
            att[here, qcols[b]] = gather(value, lane).astype(bf16)
        return carry

    lax.fori_loop(0, groups, group_step, 0, unroll=4)


def scores_kernel(
    core_ref, dy_ref, wout_ref, normed, proj, prob_ref, att,
    keep_ref, send_ref, table_ref, gproj, gbias_ref, dyp, gatt, dyf, *, head_dim,
):
    _, groups, width = dy_ref.shape
    rows, chunk = groups * MEMBERS, CHUNK
    per, mem = chunk // MEMBERS, chunk // groups
    bf16, f32 = jnp.bfloat16, jnp.float32
    scale = head_dim ** (-0.5)

    def float_step(c, carry):
        here = pl.ds(pl.multiple_of(c * chunk, chunk), chunk)
        put(dyf, here, dy_ref[pl.ds(pl.multiple_of(c * mem, mem), mem)].astype(f32).reshape(chunk, width))
        return carry

    lax.fori_loop(0, rows // chunk, float_step, 0)

    def cotangent_step(c, carry):
        here = pl.ds(pl.multiple_of(c * chunk, chunk), chunk)
        dy = by_group(dyf, c, per, groups).astype(bf16)
        dyp[here, :] = dy
        gatt[here, :] = dot(dy, wout_ref[...], 1, 1).astype(bf16)
        return carry

    lax.fori_loop(0, rows // chunk, cotangent_step, 0, unroll=True)

    gbias_ref[...] = jnp.zeros_like(gbias_ref)
    lane = head_lanes(head_dim)
    qcols, kcols, vcols = column_blocks(width)
    blocks = range(width // 128)

    def group_step(g, carry):
        here = pl.ds(pl.multiple_of(g * MEMBERS, MEMBERS), MEMBERS)
        gas = [spread(gatt[here, c], lane) for c in qcols]
        gps = [dot(proj[here, c], ga, 1, 1) for c, ga in zip(vcols, gas)]
        ws = [jnp.concatenate([spread(proj[here, c], lane), ga], axis=1) for c, ga in zip(qcols, gas)]
        probs, grads = [], []
        for b in blocks:
            p = prob_ref[b, here, :]
            gs = p * (gps[b] - jnp.sum(gps[b] * p, axis=0, keepdims=True))
            gbias_ref[b] += gs
            probs.append(p.astype(bf16))
            grads.append((gs * scale).astype(bf16))
        keyed = [dot(jnp.concatenate([p, gs], axis=0), w, 1, 0) for p, gs, w in zip(probs, grads, ws)]
        queried = by_query(grads, [proj[here, c] for c in kcols])
        for b in blocks:
            gproj[here, qcols[b]] = gather(queried[b], lane).astype(bf16)
            gproj[here, kcols[b]] = keyed[b][MEMBERS:, :128].astype(bf16)
            gproj[here, vcols[b]] = keyed[b][:MEMBERS, 128:].astype(bf16)
        return carry

    lax.fori_loop(0, groups, group_step, 0, unroll=4)

    half = 2 * width
    first = core_ref[0] == 0
    table = offset_sums(gbias_ref)
    heads = table.shape[0] // 2
    table_ref[...] = jnp.where(first, table[:heads], table[heads:])
    send_ref[width:, :] = jnp.zeros((send_ref.shape[0] - width, half), send_ref.dtype)
    send_ref[width : width + heads, :256] = jnp.where(first, table[heads:], table[:heads]).astype(send_ref.dtype)

    @pl.when(first)
    def _():
        keep_ref[...] = dot(normed[...], gproj[:, :half], 0, 0)
        send_ref[:width, :width] = dot(normed[...], gproj[:, half:], 0, 0).astype(send_ref.dtype)
        send_ref[:width, width:] = dot(att[...], dyp[...], 0, 0).astype(send_ref.dtype)

    @pl.when(jnp.logical_not(first))
    def _():
        send_ref[:width, :] = dot(normed[...], gproj[:, :half], 0, 0).astype(send_ref.dtype)
        keep_ref[:, :width] = dot(normed[...], gproj[:, half:], 0, 0)
        keep_ref[:, width:] = dot(att[...], dyp[...], 0, 0)


def back_to_input(wqkv_ref, gain_ref, branch_ref, gproj, hat, istd, dyf):
    width = gproj.shape[1] // 3
    rows, groups, chunk = gproj.shape[0], gproj.shape[0] // MEMBERS, CHUNK
    per, mem = chunk // MEMBERS, chunk // groups
    bf16, f32 = jnp.bfloat16, jnp.float32

    def gn_step(c, carry):
        here = pl.ds(pl.multiple_of(c * chunk, chunk), chunk)
        gn = dot(gproj[here, :], wqkv_ref[...], 1, 1)
        for g in range(per):
            put(dyf, pl.ds(c * per + g, MEMBERS, stride=groups), gn[g * MEMBERS : (g + 1) * MEMBERS])
        return carry

    lax.fori_loop(0, rows // chunk, gn_step, 0, unroll=True)

    def back_step(c, carry):
        gg, gsh = carry
        here = pl.ds(pl.multiple_of(c * chunk, chunk), chunk)
        gn = take(dyf, here)
        normalized = take(hat, here)
        prod = gn * normalized
        gg = gg + jnp.sum(prod.reshape(chunk // 8, 8, width), axis=0)
        gsh = gsh + jnp.sum(gn.reshape(chunk // 8, 8, width), axis=0)
        gh = gn * gain_ref[...]
        m1 = jnp.mean(gh, axis=-1, keepdims=True)
        m2 = jnp.mean(prod * gain_ref[...], axis=-1, keepdims=True)
        inv = istd[here, :][:, :1]
        branch = (inv * (gh - m1 - normalized * m2)).astype(bf16)
        branch_ref[pl.ds(pl.multiple_of(c * mem, mem), mem)] = branch.reshape(mem, groups, width)
        return gg, gsh

    zero = jnp.zeros((8, width), f32)
    gg, gsh = lax.fori_loop(0, rows // chunk, back_step, (zero, zero))
    return jnp.sum(gg, axis=0, keepdims=True), jnp.sum(gsh, axis=0, keepdims=True)


def offset_sums(gbias_ref):
    f32, bf16 = jnp.float32, jnp.bfloat16
    blocks, members, lanes = gbias_ref.shape
    i = lax.broadcasted_iota(jnp.int32, (lanes, 2 * lanes), 0)
    o = lax.broadcasted_iota(jnp.int32, (lanes, 2 * lanes), 1)
    query = GRID * GRID - 1 - i % members
    wide = (o == i // members * 128 + query // GRID * 16 + query % GRID).astype(f32).astype(bf16)
    spreads = []
    for b in range(blocks):
        value = gbias_ref[b]
        high = value.astype(bf16)
        rest = value - high.astype(f32)
        low = rest.astype(bf16)
        lowest = (rest - low.astype(f32)).astype(bf16)
        parts = dot(jnp.concatenate([high, low, lowest], axis=0), wide, 1, 0)
        spreads.append(parts[:members] + (parts[members : 2 * members] + parts[2 * members :]))
    sums = []
    for b in range(blocks):
        for h in range(PACK):
            frame = spreads[b][:, h * 128 : (h + 1) * 128]
            total = None
            for row in range(GRID):
                piece = frame[row * GRID : (row + 1) * GRID]
                piece = jnp.concatenate([piece, jnp.zeros_like(piece)], axis=1)
                piece = pltpu.roll(piece, row * 16, 1, stride=1, stride_axis=0)
                total = piece if total is None else total + piece
            sums.append(jnp.sum(total, axis=0, keepdims=True))
    return jnp.concatenate(sums, axis=0)


def back_kernel(wqkv_ref, gain_ref, gproj, hat, istd, branch_ref, gvec_ref, dyf):
    sums = back_to_input(wqkv_ref, gain_ref, branch_ref, gproj, hat, istd, dyf)
    lanes = hat.shape[0]
    for i in range(2):
        for b in range(lanes):
            gvec_ref[i * lanes + b : i * lanes + b + 1, :] = sums[i][:, b * 128 : (b + 1) * 128]


VMEM = pl.BlockSpec(memory_space=pltpu.VMEM)
SMEM = pl.BlockSpec(memory_space=pltpu.SMEM)
MIB = 1024 * 1024


def shaped(*shape, dtype=jnp.float32):
    return jax.ShapeDtypeStruct(shape, dtype)


def cost(flops, size):
    return pl.CostEstimate(flops=flops, bytes_accessed=size, transcendentals=0)


def local_forward(x, wqkv, bias, gain, shift, head_dim):
    members, groups, width = x.shape
    rows, bf16 = groups * MEMBERS, jnp.bfloat16
    blocks = width // 128
    return pl.pallas_call(
        functools.partial(forward_kernel, head_dim=head_dim),
        out_shape=(
            shaped(rows, width, dtype=bf16), shaped(rows, 3 * width, dtype=bf16),
            shaped(blocks, rows, 128), shaped(rows, 128), shaped(blocks, rows, PACK * MEMBERS),
            shaped(rows, width, dtype=bf16),
        ),
        in_specs=[VMEM] * 5,
        out_specs=(VMEM,) * 6,
        compiler_params=pltpu.CompilerParams(vmem_limit_bytes=24 * MIB),
        cost_estimate=cost(10_000_000_000, 8 << 20),
        name="forward",
    )(x, wqkv, bias, gain.reshape(1, width), shift.reshape(1, width))


def local_scores(core, dy, wout, normed, proj, prob, att, head_dim):
    members, groups, width = dy.shape
    rows, bf16, f32 = groups * MEMBERS, jnp.bfloat16, jnp.float32
    half_heads = width // head_dim // 2
    tall = pltpu.VMEM((rows, width), bf16)
    return pl.pallas_call(
        functools.partial(scores_kernel, head_dim=head_dim),
        out_shape=(
            shaped(width, 2 * width), shaped(width + 16, 2 * width, dtype=bf16), shaped(half_heads, 256),
            shaped(rows, 3 * width, dtype=bf16),
        ),
        in_specs=[SMEM] + [VMEM] * 6,
        out_specs=(VMEM,) * 4,
        scratch_shapes=[
            pltpu.VMEM((width // 128, MEMBERS, PACK * MEMBERS), f32), tall, tall,
            pltpu.VMEM((width // 128, rows, 128), f32),
        ],
        compiler_params=pltpu.CompilerParams(vmem_limit_bytes=28 * MIB),
        cost_estimate=cost(20_000_000_000, 8 << 20),
        name="scores",
    )(core.reshape(1), dy, wout, normed, proj, prob, att)


def local_back(wqkv, gain, gproj, hat, istd, groups):
    width = gain.shape[0]
    return pl.pallas_call(
        back_kernel,
        out_shape=(shaped(MEMBERS, groups, width, dtype=gproj.dtype), shaped(2 * width // 128, 128)),
        in_specs=[VMEM] * 5,
        out_specs=(VMEM,) * 2,
        scratch_shapes=[pltpu.VMEM(hat.shape, jnp.float32)],
        compiler_params=pltpu.CompilerParams(vmem_limit_bytes=16 * MIB),
        cost_estimate=cost(6_000_000_000, 4 << 20),
        name="back",
    )(wqkv, gain.reshape(1, width), gproj, hat, istd)


def outgoing_kernel(branch_ref, keep_ref, recv_ref, table_ref, gvec_ref, out_ref):
    chips, _, share, _ = out_ref.shape
    _, groups, width = branch_ref.shape
    f32, bf16 = jnp.float32, jnp.bfloat16
    slot = 0
    for b in range(width // 128):
        for t in range(groups // share):
            out_ref[:, slot] = branch_ref[:, t * share : (t + 1) * share, b * 128 : (b + 1) * 128]
            slot += 1
    for b in range(2 * width // 128):
        cols = slice(b * 128, (b + 1) * 128)
        total = (keep_ref[:, cols] + recv_ref[:width, cols].astype(f32)).astype(bf16)
        out_ref[:, slot] = total.reshape(chips, share, 128)
        slot += 1
    table = table_ref[...] + recv_ref[width : width + share, :256].astype(f32)
    for value in (table[:, :128], table[:, 128:], gvec_ref[...]):
        out_ref[:, slot] = jnp.broadcast_to(value.astype(bf16)[None], (chips, share, 128))
        slot += 1


def outgoing(branch, keep, recv, table, gvec):
    chips, groups, width = branch.shape
    share = width // chips
    slots = groups // share * width // 128 + 2 * width // 128 + 3
    return pl.pallas_call(
        outgoing_kernel,
        out_shape=shaped(chips, slots, share, 128, dtype=branch.dtype),
        in_specs=[VMEM] * 5,
        out_specs=VMEM,
        compiler_params=pltpu.CompilerParams(vmem_limit_bytes=16 * MIB),
        cost_estimate=cost(0, 6 << 20),
        name="outgoing",
    )(branch, keep, recv, table, gvec)


def sums_kernel(core_ref, got_ref, keep_ref, send_ref, *, begin, factor):
    f32 = jnp.float32
    chips, slots, share, _ = got_ref.shape
    total = got_ref[0, begin:].astype(f32)
    for chip in range(1, chips):
        total = total + got_ref[chip, begin:].astype(f32)
    total = total * factor
    part = share // 2
    weights = slots - begin - 3
    for b in range(weights):
        rows = slice(b * part, (b + 1) * part)
        low, high = total[b, :part], total[b, part:]
        keep_ref[rows, :] = jnp.where(core_ref[0] == 0, low, high)
        send_ref[rows, :] = jnp.where(core_ref[0] == 0, high, low)
    for i in range(3):
        rows = slice(weights * part + i * share, weights * part + (i + 1) * share)
        keep_ref[rows, :] = total[weights + i]
        send_ref[rows, :] = total[weights + i]


def sums_of(core, got, begin, factor):
    chips, slots, share, _ = got.shape
    rows = (slots - begin - 3) * share // 2 + 3 * share
    return pl.pallas_call(
        functools.partial(sums_kernel, begin=begin, factor=factor),
        out_shape=(shaped(rows, 128), shaped(rows, 128)),
        in_specs=[SMEM, VMEM],
        out_specs=(VMEM,) * 2,
        compiler_params=pltpu.CompilerParams(vmem_limit_bytes=16 * MIB),
        cost_estimate=cost(0, 2 << 20),
        name="sums",
    )(core.reshape(1), got)


def input_kernel(got_ref, dy_ref, grad_ref):
    _, groups, width = dy_ref.shape
    share = got_ref.shape[2]
    f32 = jnp.float32
    slot = 0
    for b in range(width // 128):
        cols = slice(b * 128, (b + 1) * 128)
        for t in range(groups // share):
            rows = slice(t * share, (t + 1) * share)
            branch = got_ref[:, slot].astype(f32)
            grad_ref[:, rows, cols] = (dy_ref[:, rows, cols].astype(f32) + branch).astype(grad_ref.dtype)
            slot += 1


def input_gradient(got, dy):
    return pl.pallas_call(
        input_kernel,
        out_shape=jax.ShapeDtypeStruct(dy.shape, dy.dtype),
        in_specs=[VMEM] * 2,
        out_specs=VMEM,
        compiler_params=pltpu.CompilerParams(vmem_limit_bytes=16 * MIB),
        cost_estimate=cost(0, 4 << 20),
        name="input_gradient",
    )(got, dy)


def finish_kernel(core_ref, keep_ref, recv_ref, qkv_ref, out_ref, table_ref, gain_ref, shift_ref):
    width = out_ref.shape[1]
    lanes = width // 128
    part, heads = out_ref.shape[0], table_ref.shape[0] // 2
    first = core_ref[0] == 0

    def ordered(mine, other):
        return jnp.where(first, mine, other), jnp.where(first, other, mine)

    for b in range(2 * lanes):
        rows = slice(b * part, (b + 1) * part)
        low, high = ordered(keep_ref[rows, :], recv_ref[rows, :])
        qkv_ref[:, b * 128 : (b + 1) * 128] = low
        if b < lanes:
            qkv_ref[:, 2 * width + b * 128 : 2 * width + (b + 1) * 128] = high
        else:
            out_ref[:, (b - lanes) * 128 : (b - lanes + 1) * 128] = high
    at = 2 * lanes * part
    halves = [jnp.concatenate([ref[at : at + heads], ref[at + heads : at + 2 * heads]], axis=1) for ref in (keep_ref, recv_ref)]
    table = jnp.concatenate(ordered(*halves), axis=0)
    side = 2 * GRID - 1
    place = lax.broadcasted_iota(jnp.int32, (256, side * side), 0)
    offset = lax.broadcasted_iota(jnp.int32, (256, side * side), 1)
    row, column = side - 1 - offset // side, side - 1 - offset % side
    pick = (place == row * 16 + column).astype(jnp.float32)
    table_ref[...] = lax.dot_general(
        table, pick, (((1,), (0,)), ((), ())), precision=lax.Precision.HIGHEST, preferred_element_type=jnp.float32
    )
    at += 2 * heads
    vectors = keep_ref[at:, :] + recv_ref[at:, :]
    for ref, row in ((gain_ref, 0), (shift_ref, lanes)):
        for b in range(lanes):
            ref[:, b * 128 : (b + 1) * 128] = vectors[row + b : row + b + 1]


def finish(core, keep, recv, part, width, heads, offsets):
    return pl.pallas_call(
        finish_kernel,
        out_shape=(
            shaped(part, 3 * width), shaped(part, width), shaped(heads, offsets), shaped(1, width), shaped(1, width)
        ),
        in_specs=[SMEM, VMEM, VMEM],
        out_specs=(VMEM,) * 5,
        name="finish",
    )(core.reshape(1), keep, recv)


AXES = ("x_lo", "y", "x_hi", "z", "core")
CHIPS = AXES[:4]


def relative_onehot(members):
    span = 2 * GRID - 1
    second = jnp.arange(members, dtype=jnp.int32)[:, None]
    first = jnp.arange(members, dtype=jnp.int32)[None, :]
    row_delta = first // GRID - second // GRID + GRID - 1
    col_delta = first % GRID - second % GRID + GRID - 1
    rel_index = row_delta * span + col_delta
    offsets = jnp.arange(span * span, dtype=jnp.int32)
    return (rel_index[:, :, None] == offsets).astype(jnp.float32)


def swap(a, axis, mask):
    size = lax.axis_size(axis)
    return lax.ppermute(a, axis, [(i, i ^ mask) for i in range(size)])


def local(block_input, cotangent, qkv_weight, out_weight, bias_table, norm_gain, norm_shift):
    tile_h, tile_w, width = block_input.shape
    heads, offsets = bias_table.shape
    chips = lax.axis_size(CHIPS)
    devices = chips * lax.axis_size("core")
    owned = tile_h * tile_w // chips
    core = lax.axis_index("core")
    onehot = relative_onehot(MEMBERS)
    bias = jnp.einsum(
        "bhr,kqr->bkhq",
        bias_table.reshape(heads // PACK, PACK, offsets),
        onehot,
        precision=lax.Precision.HIGHEST,
    ).reshape(heads // PACK, MEMBERS, PACK * MEMBERS)
    x = block_input.reshape(chips, owned, width)
    dy = cotangent.reshape(chips, owned, width)
    exchange = functools.partial(lax.all_to_all, axis_name=CHIPS, split_axis=0, concat_axis=0, tiled=True)
    got = exchange(x)
    got, bias, dy_sent = lax.optimization_barrier((got, bias, dy))
    normed, proj, hat, istd, prob, att = local_forward(got, qkv_weight, bias, norm_gain, norm_shift, width // heads)
    keep, send, table, gproj = local_scores(
        core, exchange(dy_sent), out_weight, normed, proj, prob, att, width // heads
    )
    recv = swap(send, "core", 1)
    branch, gvec = local_back(qkv_weight, norm_gain, gproj, hat, istd, owned)
    got = exchange(outgoing(branch, keep, recv, table, gvec))
    factor = float(tile_h * tile_w * devices) ** (-0.5)
    share = width // chips
    mine, theirs = sums_of(core, got, owned // share * width // 128, factor)
    recv = swap(theirs, "core", 1)
    grad_input = input_gradient(got, dy)
    grad_qkv, grad_out, table, gain, shift = finish(core, mine, recv, share // 2, width, heads, offsets)
    return (
        grad_input.reshape(tile_h, tile_w, width),
        grad_qkv,
        grad_out,
        table,
        gain.reshape(width),
        shift.reshape(width),
    )


def solution(mesh):
    fine = Mesh(mesh.devices.reshape(2, 4, 2, 4, 2), AXES)
    tile = P(("x_lo", "y"), ("x_hi", "z", "core"), None)
    return jax.shard_map(
        local,
        mesh=fine,
        in_specs=(tile, tile, P(), P(), P(), P(), P()),
        out_specs=(tile, P(AXES, None), P(AXES, None), P(), P(), P()),
        check_vma=False,
    )
```

```python
import functools
import jax
import jax.numpy as jnp
from jax import lax
from jax.experimental import pallas as pl
from jax.experimental.pallas import tpu as pltpu
from jax.sharding import Mesh, PartitionSpec as P

GRID = 8
EPSILON = 1e-05
MEMBERS = GRID * GRID
PACK = 4
CHUNK = 256


def dot(a, b, ca, cb):
    return lax.dot_general(a, b, (((ca,), (cb,)), ((), ())), preferred_element_type=jnp.float32)


def put(ref, at, value):
    for b in range(ref.shape[0]):
        ref[b, at, :] = value[:, b * 128 : (b + 1) * 128]


def take(ref, at):
    return jnp.concatenate([ref[b, at, :] for b in range(ref.shape[0])], axis=1)


def forward_and_scores(
    pair_ref, wqkv_ref, wout_ref, bias_ref, gain_ref, shift_ref, gbias_ref,
    normed, gproj, att, dyp, hat, istd, proj, gatt, dyf, head_dim, fetches,
):
    width = gproj.shape[1] // 3
    rows, groups, chunk = gproj.shape[0], gproj.shape[0] // MEMBERS, CHUNK
    per, mem = chunk // MEMBERS, chunk // groups
    bf16, f32 = jnp.bfloat16, jnp.float32
    scale = head_dim ** (-0.5)

    def hat_step(c, carry):
        here = pl.ds(pl.multiple_of(c * chunk, chunk), chunk)
        pair = pair_ref[pl.ds(pl.multiple_of(c * mem, mem), mem)].astype(f32)
        x = pair[:, 0].reshape(chunk, width)
        centred = x - jnp.mean(x, axis=-1, keepdims=True)
        inv = lax.rsqrt(jnp.mean(centred * centred, axis=-1, keepdims=True) + EPSILON)
        put(hat, here, centred * inv)
        istd[here, :] = jnp.broadcast_to(inv, (chunk, 128))
        put(dyf, here, pair[:, 1].reshape(chunk, width))
        return carry

    lax.fori_loop(0, rows // chunk, hat_step, 0)
    for fetch in fetches:
        fetch.wait()

    def by_group(ref, c):
        return jnp.concatenate(
            [take(ref, pl.ds(c * per + g, MEMBERS, stride=groups)) for g in range(per)], axis=0
        )

    def norm_step(c, carry):
        here = pl.ds(pl.multiple_of(c * chunk, chunk), chunk)
        nb = (by_group(hat, c) * gain_ref[...] + shift_ref[...]).astype(bf16)
        dy = by_group(dyf, c).astype(bf16)
        dyp[here, :] = dy
        normed[here, :] = nb
        proj[here, :] = dot(nb, wqkv_ref[...], 1, 0).astype(bf16)
        gatt[here, :] = dot(dy, wout_ref[...], 1, 1).astype(bf16)
        return carry

    lax.fori_loop(0, rows // chunk, norm_step, 0, unroll=True)

    lane = lax.broadcasted_iota(jnp.int32, (MEMBERS, 128), 1) // head_dim

    def spread(a):
        zero = jnp.zeros_like(a)
        return jnp.concatenate([jnp.where(lane == h, a, zero) for h in range(PACK)], axis=0)

    def gather(a):
        out = a[:MEMBERS]
        for h in range(1, PACK):
            out = jnp.where(lane == h, a[h * MEMBERS : (h + 1) * MEMBERS], out)
        return out

    blocks = range(width // 128)

    def group_step(g, carry):
        here = pl.ds(pl.multiple_of(g * MEMBERS, MEMBERS), MEMBERS)
        cols = [slice(b * 128, (b + 1) * 128) for b in blocks]
        kcols = [slice(width + b * 128, width + (b + 1) * 128) for b in blocks]
        vcols = [slice(2 * width + b * 128, 2 * width + (b + 1) * 128) for b in blocks]
        ks = [proj[here, c] for c in kcols]
        vs = [proj[here, c] for c in vcols]
        none = jnp.zeros_like(ks[0])
        ws = [jnp.concatenate([spread(proj[here, c]), spread(gatt[here, c])], axis=1) for c in cols]
        both = [
            dot(
                jnp.concatenate(
                    [jnp.concatenate([k, none], axis=1), jnp.concatenate([none, v], axis=1)], axis=0
                ),
                w, 1, 1,
            )
            for k, v, w in zip(ks, vs, ws)
        ]
        pds = []
        for b in blocks:
            scores = both[b][:MEMBERS] * scale + bias_ref[b]
            gp = both[b][MEMBERS:]
            e = jnp.exp(scores - jnp.max(scores, axis=0, keepdims=True))
            p = e * (1.0 / jnp.sum(e, axis=0, keepdims=True))
            gs = p * (gp - jnp.sum(gp * p, axis=0, keepdims=True))
            gbias_ref[b] += gs
            pds.append(jnp.concatenate([p.astype(bf16), (gs * scale).astype(bf16)], axis=0))
        keyed = [dot(pd, w, 1, 0) for pd, w in zip(pds, ws)]
        queried = [
            dot(
                pd,
                jnp.concatenate(
                    [jnp.concatenate([v, none], axis=1), jnp.concatenate([none, k], axis=1)], axis=0
                ),
                0, 0,
            )
            for k, v, pd in zip(ks, vs, pds)
        ]
        for b in blocks:
            att[here, cols[b]] = gather(queried[b][:, :128]).astype(bf16)
            gproj[here, cols[b]] = gather(queried[b][:, 128:]).astype(bf16)
            gproj[here, kcols[b]] = keyed[b][MEMBERS:, :128].astype(bf16)
            gproj[here, vcols[b]] = keyed[b][:MEMBERS, 128:].astype(bf16)
        return carry

    lax.fori_loop(0, groups, group_step, 0, unroll=4)


def back_to_input(wqkv_ref, gain_ref, branch_ref, gproj, hat, istd, dyf):
    width = gproj.shape[1] // 3
    rows, groups, chunk = gproj.shape[0], gproj.shape[0] // MEMBERS, CHUNK
    per, mem = chunk // MEMBERS, chunk // groups
    bf16, f32 = jnp.bfloat16, jnp.float32

    def gn_step(c, carry):
        here = pl.ds(pl.multiple_of(c * chunk, chunk), chunk)
        gn = dot(gproj[here, :], wqkv_ref[...], 1, 1)
        for g in range(per):
            put(dyf, pl.ds(c * per + g, MEMBERS, stride=groups), gn[g * MEMBERS : (g + 1) * MEMBERS])
        return carry

    lax.fori_loop(0, rows // chunk, gn_step, 0, unroll=True)

    def back_step(c, carry):
        gg, gsh = carry
        here = pl.ds(pl.multiple_of(c * chunk, chunk), chunk)
        gn = take(dyf, here)
        normalized = take(hat, here)
        prod = gn * normalized
        gg = gg + jnp.sum(prod.reshape(chunk // 8, 8, width), axis=0)
        gsh = gsh + jnp.sum(gn.reshape(chunk // 8, 8, width), axis=0)
        gh = gn * gain_ref[...]
        m1 = jnp.mean(gh, axis=-1, keepdims=True)
        m2 = jnp.mean(prod * gain_ref[...], axis=-1, keepdims=True)
        inv = istd[here, :][:, :1]
        branch = (inv * (gh - m1 - normalized * m2)).astype(bf16)
        branch_ref[pl.ds(pl.multiple_of(c * mem, mem), mem)] = branch.reshape(mem, groups, width)
        return gg, gsh

    zero = jnp.zeros((8, width), f32)
    gg, gsh = lax.fori_loop(0, rows // chunk, back_step, (zero, zero))
    return jnp.sum(gg, axis=0, keepdims=True), jnp.sum(gsh, axis=0, keepdims=True)


def offset_sums(gbias_ref):
    f32, bf16 = jnp.float32, jnp.bfloat16
    blocks, members, lanes = gbias_ref.shape
    i = lax.broadcasted_iota(jnp.int32, (lanes, 2 * lanes), 0)
    o = lax.broadcasted_iota(jnp.int32, (lanes, 2 * lanes), 1)
    query = GRID * GRID - 1 - i % members
    wide = (o == i // members * 128 + query // GRID * 16 + query % GRID).astype(f32).astype(bf16)
    spreads = []
    for b in range(blocks):
        value = gbias_ref[b]
        high = value.astype(bf16)
        rest = value - high.astype(f32)
        low = rest.astype(bf16)
        lowest = (rest - low.astype(f32)).astype(bf16)
        parts = dot(jnp.concatenate([high, low, lowest], axis=0), wide, 1, 0)
        spreads.append(parts[:members] + (parts[members : 2 * members] + parts[2 * members :]))
    sums = []
    for b in range(blocks):
        for h in range(PACK):
            frame = spreads[b][:, h * 128 : (h + 1) * 128]
            total = None
            for row in range(GRID):
                piece = frame[row * GRID : (row + 1) * GRID]
                piece = jnp.concatenate([piece, jnp.zeros_like(piece)], axis=1)
                piece = pltpu.roll(piece, row * 16, 1, stride=1, stride_axis=0)
                total = piece if total is None else total + piece
            sums.append(jnp.sum(total, axis=0, keepdims=True))
    return jnp.concatenate(sums, axis=0)


def scores_kernel(
    core_ref, pair_ref, wqkv_hbm, wout_hbm, bias_ref, gain_ref, shift_ref,
    keep_ref, send_ref, table_ref, gproj, hat, istd, wqkv_ref,
    wout_ref, gbias_ref, normed, att, dyp, proj, gatt, dyf, sems, *, head_dim,
):
    fetches = [
        pltpu.make_async_copy(wqkv_hbm, wqkv_ref, sems.at[0]),
        pltpu.make_async_copy(wout_hbm, wout_ref, sems.at[1]),
    ]
    for fetch in fetches:
        fetch.start()
    gbias_ref[...] = jnp.zeros_like(gbias_ref)
    forward_and_scores(
        pair_ref, wqkv_ref, wout_ref, bias_ref, gain_ref, shift_ref, gbias_ref,
        normed, gproj, att, dyp, hat, istd, proj, gatt, dyf, head_dim, fetches,
    )
    width = wout_ref.shape[0]
    half = 2 * width
    first = core_ref[0] == 0
    table = offset_sums(gbias_ref)
    heads = table.shape[0] // 2
    table_ref[...] = jnp.where(first, table[:heads], table[heads:])
    send_ref[width:, :] = jnp.zeros((send_ref.shape[0] - width, half), send_ref.dtype)
    send_ref[width : width + heads, :256] = jnp.where(first, table[heads:], table[:heads]).astype(send_ref.dtype)

    @pl.when(first)
    def _():
        keep_ref[...] = dot(normed[...], gproj[:, :half], 0, 0)
        send_ref[:width, :width] = dot(normed[...], gproj[:, half:], 0, 0).astype(send_ref.dtype)
        send_ref[:width, width:] = dot(att[...], dyp[...], 0, 0).astype(send_ref.dtype)

    @pl.when(jnp.logical_not(first))
    def _():
        send_ref[:width, :] = dot(normed[...], gproj[:, :half], 0, 0).astype(send_ref.dtype)
        keep_ref[:, :width] = dot(normed[...], gproj[:, half:], 0, 0)
        keep_ref[:, width:] = dot(att[...], dyp[...], 0, 0)


def back_kernel(wqkv_ref, gain_ref, gproj, hat, istd, branch_ref, gvec_ref, dyf):
    sums = back_to_input(wqkv_ref, gain_ref, branch_ref, gproj, hat, istd, dyf)
    lanes = hat.shape[0]
    for i in range(2):
        for b in range(lanes):
            gvec_ref[i * lanes + b : i * lanes + b + 1, :] = sums[i][:, b * 128 : (b + 1) * 128]


VMEM = pl.BlockSpec(memory_space=pltpu.VMEM)
SMEM = pl.BlockSpec(memory_space=pltpu.SMEM)
HBM = pl.BlockSpec(memory_space=pltpu.HBM)
MIB = 1024 * 1024


def in_hbm(a):
    return pltpu.with_memory_space_constraint(a, pltpu.HBM)


def shaped(*shape, dtype=jnp.float32):
    return jax.ShapeDtypeStruct(shape, dtype)


def cost(flops, size):
    return pl.CostEstimate(flops=flops, bytes_accessed=size, transcendentals=0)


def part_buffers(rows, width):
    bf16, f32 = jnp.bfloat16, jnp.float32
    tall, lanes = (rows, width), (width // 128, rows, 128)
    return [
        (tall, bf16), ((rows, 3 * width), bf16), (tall, bf16), (tall, bf16), (lanes, f32), ((rows, 128), f32),
        ((rows, 3 * width), bf16), (tall, bf16), (lanes, f32),
    ]


def local_scores(core, pair, wqkv, wout, bias, gain, shift, head_dim):
    members, _, groups, width = pair.shape
    bf16, f32 = jnp.bfloat16, jnp.float32
    normed, gproj, att, dyp, hat, istd, proj, gatt, dyf = part_buffers(groups * MEMBERS, width)
    half_heads = width // head_dim // 2
    return pl.pallas_call(
        functools.partial(scores_kernel, head_dim=head_dim),
        out_shape=(
            shaped(width, 2 * width), shaped(width + 16, 2 * width, dtype=bf16), shaped(half_heads, 256)
        )
        + tuple(jax.ShapeDtypeStruct(*b) for b in (gproj, hat, istd))
        + (jax.ShapeDtypeStruct(wqkv.shape, wqkv.dtype),),
        in_specs=[SMEM, VMEM, HBM, HBM] + [VMEM] * 3,
        out_specs=(VMEM,) * 7,
        scratch_shapes=[pltpu.VMEM(wout.shape, wout.dtype), pltpu.VMEM(bias.shape, f32)]
        + [pltpu.VMEM(*b) for b in (normed, att, dyp, proj, gatt, dyf)]
        + [pltpu.SemaphoreType.DMA((2,))],
        compiler_params=pltpu.CompilerParams(vmem_limit_bytes=28 * MIB),
        cost_estimate=cost(20_000_000_000, 8 << 20),
        name="scores",
    )(core.reshape(1), pair, in_hbm(wqkv), in_hbm(wout), bias, gain.reshape(1, width), shift.reshape(1, width))


def local_back(wqkv, gain, gproj, hat, istd, groups):
    width = gain.shape[0]
    return pl.pallas_call(
        back_kernel,
        out_shape=(shaped(MEMBERS, groups, width, dtype=gproj.dtype), shaped(2 * width // 128, 128)),
        in_specs=[VMEM] * 5,
        out_specs=(VMEM,) * 2,
        scratch_shapes=[pltpu.VMEM(hat.shape, jnp.float32)],
        compiler_params=pltpu.CompilerParams(vmem_limit_bytes=16 * MIB),
        cost_estimate=cost(6_000_000_000, 4 << 20),
        name="back",
    )(wqkv, gain.reshape(1, width), gproj, hat, istd)


def pair_kernel(x_ref, dy_ref, out_ref):
    out_ref[:, 0] = x_ref[...]
    out_ref[:, 1] = dy_ref[...]


def pair_of(x, dy):
    chips, groups, width = x.shape
    step = chips // 2
    source = pl.BlockSpec((step, groups, width), lambda i: (i, 0, 0))
    return pl.pallas_call(
        pair_kernel,
        grid=(chips // step,),
        out_shape=shaped(chips, 2, groups, width, dtype=x.dtype),
        in_specs=[source, source],
        out_specs=pl.BlockSpec((step, 2, groups, width), lambda i: (i, 0, 0, 0)),
        cost_estimate=cost(0, 4 << 20),
        name="pair",
    )(x, dy)


def outgoing_kernel(branch_ref, keep_ref, recv_ref, table_ref, gvec_ref, out_ref):
    chips, _, share, _ = out_ref.shape
    _, groups, width = branch_ref.shape
    f32, bf16 = jnp.float32, jnp.bfloat16
    slot = 0
    for b in range(width // 128):
        for t in range(groups // share):
            out_ref[:, slot] = branch_ref[:, t * share : (t + 1) * share, b * 128 : (b + 1) * 128]
            slot += 1
    for b in range(2 * width // 128):
        cols = slice(b * 128, (b + 1) * 128)
        total = (keep_ref[:, cols] + recv_ref[:width, cols].astype(f32)).astype(bf16)
        out_ref[:, slot] = total.reshape(chips, share, 128)
        slot += 1
    table = table_ref[...] + recv_ref[width : width + share, :256].astype(f32)
    for value in (table[:, :128], table[:, 128:], gvec_ref[...]):
        out_ref[:, slot] = jnp.broadcast_to(value.astype(bf16)[None], (chips, share, 128))
        slot += 1


def outgoing(branch, keep, recv, table, gvec):
    chips, groups, width = branch.shape
    share = width // chips
    slots = groups // share * width // 128 + 2 * width // 128 + 3
    return pl.pallas_call(
        outgoing_kernel,
        out_shape=shaped(chips, slots, share, 128, dtype=branch.dtype),
        in_specs=[VMEM] * 5,
        out_specs=VMEM,
        compiler_params=pltpu.CompilerParams(vmem_limit_bytes=16 * MIB),
        cost_estimate=cost(0, 6 << 20),
        name="outgoing",
    )(branch, keep, recv, table, gvec)


def sums_kernel(core_ref, got_ref, keep_ref, send_ref, *, begin, factor):
    f32 = jnp.float32
    chips, slots, share, _ = got_ref.shape
    total = got_ref[0, begin:].astype(f32)
    for chip in range(1, chips):
        total = total + got_ref[chip, begin:].astype(f32)
    total = total * factor
    part = share // 2
    weights = slots - begin - 3
    for b in range(weights):
        rows = slice(b * part, (b + 1) * part)
        low, high = total[b, :part], total[b, part:]
        keep_ref[rows, :] = jnp.where(core_ref[0] == 0, low, high)
        send_ref[rows, :] = jnp.where(core_ref[0] == 0, high, low)
    for i in range(3):
        rows = slice(weights * part + i * share, weights * part + (i + 1) * share)
        keep_ref[rows, :] = total[weights + i]
        send_ref[rows, :] = total[weights + i]


def sums_of(core, got, begin, factor):
    chips, slots, share, _ = got.shape
    rows = (slots - begin - 3) * share // 2 + 3 * share
    return pl.pallas_call(
        functools.partial(sums_kernel, begin=begin, factor=factor),
        out_shape=(shaped(rows, 128), shaped(rows, 128)),
        in_specs=[SMEM, VMEM],
        out_specs=(VMEM,) * 2,
        compiler_params=pltpu.CompilerParams(vmem_limit_bytes=16 * MIB),
        cost_estimate=cost(0, 2 << 20),
        name="sums",
    )(core.reshape(1), got)


def input_kernel(got_ref, dy_ref, grad_ref):
    _, groups, width = dy_ref.shape
    share = got_ref.shape[2]
    f32 = jnp.float32
    slot = 0
    for b in range(width // 128):
        cols = slice(b * 128, (b + 1) * 128)
        for t in range(groups // share):
            rows = slice(t * share, (t + 1) * share)
            branch = got_ref[:, slot].astype(f32)
            grad_ref[:, rows, cols] = (dy_ref[:, rows, cols].astype(f32) + branch).astype(grad_ref.dtype)
            slot += 1


def input_gradient(got, dy):
    return pl.pallas_call(
        input_kernel,
        out_shape=jax.ShapeDtypeStruct(dy.shape, dy.dtype),
        in_specs=[VMEM] * 2,
        out_specs=VMEM,
        compiler_params=pltpu.CompilerParams(vmem_limit_bytes=16 * MIB),
        cost_estimate=cost(0, 4 << 20),
        name="input_gradient",
    )(got, dy)


def finish_kernel(core_ref, keep_ref, recv_ref, qkv_ref, out_ref, table_ref, gain_ref, shift_ref):
    width = out_ref.shape[1]
    lanes = width // 128
    part, heads = out_ref.shape[0], table_ref.shape[0] // 2
    first = core_ref[0] == 0

    def ordered(mine, other):
        return jnp.where(first, mine, other), jnp.where(first, other, mine)

    for b in range(2 * lanes):
        rows = slice(b * part, (b + 1) * part)
        low, high = ordered(keep_ref[rows, :], recv_ref[rows, :])
        qkv_ref[:, b * 128 : (b + 1) * 128] = low
        if b < lanes:
            qkv_ref[:, 2 * width + b * 128 : 2 * width + (b + 1) * 128] = high
        else:
            out_ref[:, (b - lanes) * 128 : (b - lanes + 1) * 128] = high
    at = 2 * lanes * part
    halves = [jnp.concatenate([ref[at : at + heads], ref[at + heads : at + 2 * heads]], axis=1) for ref in (keep_ref, recv_ref)]
    table = jnp.concatenate(ordered(*halves), axis=0)
    side = 2 * GRID - 1
    place = lax.broadcasted_iota(jnp.int32, (256, side * side), 0)
    offset = lax.broadcasted_iota(jnp.int32, (256, side * side), 1)
    row, column = side - 1 - offset // side, side - 1 - offset % side
    pick = (place == row * 16 + column).astype(jnp.float32)
    table_ref[...] = lax.dot_general(
        table, pick, (((1,), (0,)), ((), ())), precision=lax.Precision.HIGHEST, preferred_element_type=jnp.float32
    )
    at += 2 * heads
    vectors = keep_ref[at:, :] + recv_ref[at:, :]
    for ref, row in ((gain_ref, 0), (shift_ref, lanes)):
        for b in range(lanes):
            ref[:, b * 128 : (b + 1) * 128] = vectors[row + b : row + b + 1]


def finish(core, keep, recv, part, width, heads, offsets):
    return pl.pallas_call(
        finish_kernel,
        out_shape=(
            shaped(part, 3 * width), shaped(part, width), shaped(heads, offsets), shaped(1, width), shaped(1, width)
        ),
        in_specs=[SMEM, VMEM, VMEM],
        out_specs=(VMEM,) * 5,
        compiler_params=pltpu.CompilerParams(vmem_limit_bytes=8 * MIB),
        name="finish",
    )(core.reshape(1), keep, recv)


AXES = ("x_lo", "y", "x_hi", "z", "core")
CHIPS = AXES[:4]


def relative_onehot(members):
    span = 2 * GRID - 1
    second = jnp.arange(members, dtype=jnp.int32)[:, None]
    first = jnp.arange(members, dtype=jnp.int32)[None, :]
    row_delta = first // GRID - second // GRID + GRID - 1
    col_delta = first % GRID - second % GRID + GRID - 1
    rel_index = row_delta * span + col_delta
    offsets = jnp.arange(span * span, dtype=jnp.int32)
    return (rel_index[:, :, None] == offsets).astype(jnp.float32)


def swap(a, axis, mask):
    size = lax.axis_size(axis)
    return lax.ppermute(a, axis, [(i, i ^ mask) for i in range(size)])


def local(block_input, cotangent, qkv_weight, out_weight, bias_table, norm_gain, norm_shift):
    tile_h, tile_w, width = block_input.shape
    heads, offsets = bias_table.shape
    chips = lax.axis_size(CHIPS)
    devices = chips * lax.axis_size("core")
    owned = tile_h * tile_w // chips
    core = lax.axis_index("core")
    onehot = relative_onehot(MEMBERS)
    bias = jnp.einsum(
        "bhr,kqr->bkhq",
        bias_table.reshape(heads // PACK, PACK, offsets),
        onehot,
        precision=lax.Precision.HIGHEST,
    ).reshape(heads // PACK, MEMBERS, PACK * MEMBERS)
    x = block_input.reshape(chips, owned, width)
    dy = cotangent.reshape(chips, owned, width)
    exchange = functools.partial(lax.all_to_all, axis_name=CHIPS, split_axis=0, concat_axis=0, tiled=True)
    got = exchange(pair_of(x, dy))
    keep, send, table, gproj, hat, istd, qkv_copy = local_scores(
        core, got, qkv_weight, out_weight, bias, norm_gain, norm_shift, width // heads
    )
    recv = swap(send, "core", 1)
    branch, gvec = local_back(qkv_copy, norm_gain, gproj, hat, istd, owned)
    got = exchange(outgoing(branch, keep, recv, table, gvec))
    factor = float(tile_h * tile_w * devices) ** (-0.5)
    share = width // chips
    mine, theirs = sums_of(core, got, owned // share * width // 128, factor)
    recv = swap(theirs, "core", 1)
    grad_input = input_gradient(got, dy)
    grad_qkv, grad_out, table, gain, shift = finish(core, mine, recv, share // 2, width, heads, offsets)
    return (
        grad_input.reshape(tile_h, tile_w, width),
        grad_qkv,
        grad_out,
        table,
        gain.reshape(width),
        shift.reshape(width),
    )


def solution(mesh):
    fine = Mesh(mesh.devices.reshape(2, 4, 2, 4, 2), AXES)
    tile = P(("x_lo", "y"), ("x_hi", "z", "core"), None)
    return jax.shard_map(
        local,
        mesh=fine,
        in_specs=(tile, tile, P(), P(), P(), P(), P()),
        out_specs=(tile, P(AXES, None), P(AXES, None), P(), P(), P()),
        check_vma=False,
    )
```

```python
import functools
import jax
import jax.numpy as jnp
from jax import lax
from jax.experimental import pallas as pl
from jax.experimental.pallas import tpu as pltpu
from jax.sharding import Mesh, PartitionSpec as P

GRID = 8
EPSILON = 1e-05
MEMBERS = GRID * GRID
PACK = 4
CHUNK = 256


def dot(a, b, ca, cb):
    return lax.dot_general(a, b, (((ca,), (cb,)), ((), ())), preferred_element_type=jnp.float32)


def put(ref, at, value):
    for b in range(ref.shape[0]):
        ref[b, at, :] = value[:, b * 128 : (b + 1) * 128]


def take(ref, at):
    return jnp.concatenate([ref[b, at, :] for b in range(ref.shape[0])], axis=1)


def forward_and_scores(
    pair_ref, wqkv_ref, wout_ref, bias_ref, gain_ref, shift_ref, gbias_ref,
    normed, gproj, att, dyp, hat, istd, proj, gatt, dyf, head_dim, fetches,
):
    width = gproj.shape[1] // 3
    rows, groups, chunk = gproj.shape[0], gproj.shape[0] // MEMBERS, CHUNK
    per, mem = chunk // MEMBERS, chunk // groups
    bf16, f32 = jnp.bfloat16, jnp.float32
    scale = head_dim ** (-0.5)

    def hat_step(c, carry):
        here = pl.ds(pl.multiple_of(c * chunk, chunk), chunk)
        pair = pair_ref[pl.ds(pl.multiple_of(c * mem, mem), mem)].astype(f32)
        x = pair[:, 0].reshape(chunk, width)
        centred = x - jnp.mean(x, axis=-1, keepdims=True)
        inv = lax.rsqrt(jnp.mean(centred * centred, axis=-1, keepdims=True) + EPSILON)
        put(hat, here, centred * inv)
        istd[here, :] = jnp.broadcast_to(inv, (chunk, 128))
        put(dyf, here, pair[:, 1].reshape(chunk, width))
        return carry

    lax.fori_loop(0, rows // chunk, hat_step, 0)
    for fetch in fetches:
        fetch.wait()

    def by_group(ref, c):
        return jnp.concatenate(
            [take(ref, pl.ds(c * per + g, MEMBERS, stride=groups)) for g in range(per)], axis=0
        )

    def norm_step(c, carry):
        here = pl.ds(pl.multiple_of(c * chunk, chunk), chunk)
        nb = (by_group(hat, c) * gain_ref[...] + shift_ref[...]).astype(bf16)
        dy = by_group(dyf, c).astype(bf16)
        dyp[here, :] = dy
        normed[here, :] = nb
        proj[here, :] = dot(nb, wqkv_ref[...], 1, 0).astype(bf16)
        gatt[here, :] = dot(dy, wout_ref[...], 1, 1).astype(bf16)
        return carry

    lax.fori_loop(0, rows // chunk, norm_step, 0, unroll=True)

    lane = lax.broadcasted_iota(jnp.int32, (MEMBERS, 128), 1) // head_dim

    def spread(a):
        zero = jnp.zeros_like(a)
        return jnp.concatenate([jnp.where(lane == h, a, zero) for h in range(PACK)], axis=0)

    def gather(a):
        out = a[:MEMBERS]
        for h in range(1, PACK):
            out = jnp.where(lane == h, a[h * MEMBERS : (h + 1) * MEMBERS], out)
        return out

    blocks = range(width // 128)

    qcols = [slice(b * 128, (b + 1) * 128) for b in blocks]
    kcols = [slice(width + b * 128, width + (b + 1) * 128) for b in blocks]
    vcols = [slice(2 * width + b * 128, 2 * width + (b + 1) * 128) for b in blocks]

    def stacked(top, low):
        none = jnp.zeros_like(top)
        return jnp.concatenate(
            [jnp.concatenate([top, none], axis=1), jnp.concatenate([none, low], axis=1)], axis=0
        )

    def products(g):
        here = slice(g * MEMBERS, (g + 1) * MEMBERS)
        ws = [jnp.concatenate([spread(proj[here, c]), spread(gatt[here, c])], axis=1) for c in qcols]
        return ws, [dot(stacked(proj[here, k], proj[here, v]), w, 1, 1) for k, v, w in zip(kcols, vcols, ws)]

    def softmax(b, both):
        scores = both[:MEMBERS] * scale + bias_ref[b]
        gp = both[MEMBERS:]
        e = jnp.exp(scores - jnp.max(scores, axis=0, keepdims=True))
        p = e * (1.0 / jnp.sum(e, axis=0, keepdims=True))
        gs = p * (gp - jnp.sum(gp * p, axis=0, keepdims=True))
        gbias_ref[b] += gs
        return jnp.concatenate([p.astype(bf16), (gs * scale).astype(bf16)], axis=0)

    def store(g, keyed, queried):
        here = slice(g * MEMBERS, (g + 1) * MEMBERS)
        for b in blocks:
            att[here, qcols[b]] = gather(queried[b][:, :128]).astype(bf16)
            gproj[here, qcols[b]] = gather(queried[b][:, 128:]).astype(bf16)
            gproj[here, kcols[b]] = keyed[b][MEMBERS:, :128].astype(bf16)
            gproj[here, vcols[b]] = keyed[b][:MEMBERS, 128:].astype(bf16)

    ahead, behind = products(0), None
    for g in range(groups):
        here = slice(g * MEMBERS, (g + 1) * MEMBERS)
        ws, both = ahead
        keyed, queried, ws_next, both_next = [], [], [], []
        more = products(g + 1) if g + 1 < groups else ([], [])
        ws_next, both_next = more
        for b in blocks:
            pd = softmax(b, both[b])
            keyed.append(dot(pd, ws[b], 1, 0))
            queried.append(dot(pd, stacked(proj[here, vcols[b]], proj[here, kcols[b]]), 0, 0))
        if behind is not None:
            store(g - 1, *behind)
        behind = (keyed, queried)
        ahead = (ws_next, both_next)
    store(groups - 1, *behind)


def back_to_input(wqkv_ref, gain_ref, branch_ref, gproj, hat, istd, dyf):
    width = gproj.shape[1] // 3
    rows, groups, chunk = gproj.shape[0], gproj.shape[0] // MEMBERS, CHUNK
    per, mem = chunk // MEMBERS, chunk // groups
    bf16, f32 = jnp.bfloat16, jnp.float32

    def gn_step(c, carry):
        here = pl.ds(pl.multiple_of(c * chunk, chunk), chunk)
        gn = dot(gproj[here, :], wqkv_ref[...], 1, 1)
        for g in range(per):
            put(dyf, pl.ds(c * per + g, MEMBERS, stride=groups), gn[g * MEMBERS : (g + 1) * MEMBERS])
        return carry

    lax.fori_loop(0, rows // chunk, gn_step, 0, unroll=True)

    def back_step(c, carry):
        gg, gsh = carry
        here = pl.ds(pl.multiple_of(c * chunk, chunk), chunk)
        gn = take(dyf, here)
        normalized = take(hat, here)
        prod = gn * normalized
        gg = gg + jnp.sum(prod.reshape(chunk // 8, 8, width), axis=0)
        gsh = gsh + jnp.sum(gn.reshape(chunk // 8, 8, width), axis=0)
        gh = gn * gain_ref[...]
        m1 = jnp.mean(gh, axis=-1, keepdims=True)
        m2 = jnp.mean(prod * gain_ref[...], axis=-1, keepdims=True)
        inv = istd[here, :][:, :1]
        branch = (inv * (gh - m1 - normalized * m2)).astype(bf16)
        branch_ref[pl.ds(pl.multiple_of(c * mem, mem), mem)] = branch.reshape(mem, groups, width)
        return gg, gsh

    zero = jnp.zeros((8, width), f32)
    gg, gsh = lax.fori_loop(0, rows // chunk, back_step, (zero, zero))
    return jnp.sum(gg, axis=0, keepdims=True), jnp.sum(gsh, axis=0, keepdims=True)


def offset_sums(gbias_ref):
    f32, bf16 = jnp.float32, jnp.bfloat16
    blocks, members, lanes = gbias_ref.shape
    i = lax.broadcasted_iota(jnp.int32, (lanes, 2 * lanes), 0)
    o = lax.broadcasted_iota(jnp.int32, (lanes, 2 * lanes), 1)
    query = GRID * GRID - 1 - i % members
    wide = (o == i // members * 128 + query // GRID * 16 + query % GRID).astype(f32).astype(bf16)
    spreads = []
    for b in range(blocks):
        value = gbias_ref[b]
        high = value.astype(bf16)
        rest = value - high.astype(f32)
        low = rest.astype(bf16)
        lowest = (rest - low.astype(f32)).astype(bf16)
        parts = dot(jnp.concatenate([high, low, lowest], axis=0), wide, 1, 0)
        spreads.append(parts[:members] + (parts[members : 2 * members] + parts[2 * members :]))
    sums = []
    for b in range(blocks):
        for h in range(PACK):
            frame = spreads[b][:, h * 128 : (h + 1) * 128]
            total = None
            for row in range(GRID):
                piece = frame[row * GRID : (row + 1) * GRID]
                piece = jnp.concatenate([piece, jnp.zeros_like(piece)], axis=1)
                piece = pltpu.roll(piece, row * 16, 1, stride=1, stride_axis=0)
                total = piece if total is None else total + piece
            sums.append(jnp.sum(total, axis=0, keepdims=True))
    return jnp.concatenate(sums, axis=0)


def scores_kernel(
    core_ref, pair_ref, wqkv_hbm, wout_hbm, bias_ref, gain_ref, shift_ref,
    keep_ref, send_ref, table_ref, gproj, hat, istd, wqkv_ref,
    wout_ref, gbias_ref, normed, att, dyp, proj, gatt, dyf, sems, *, head_dim,
):
    fetches = [
        pltpu.make_async_copy(wqkv_hbm, wqkv_ref, sems.at[0]),
        pltpu.make_async_copy(wout_hbm, wout_ref, sems.at[1]),
    ]
    for fetch in fetches:
        fetch.start()
    gbias_ref[...] = jnp.zeros_like(gbias_ref)
    forward_and_scores(
        pair_ref, wqkv_ref, wout_ref, bias_ref, gain_ref, shift_ref, gbias_ref,
        normed, gproj, att, dyp, hat, istd, proj, gatt, dyf, head_dim, fetches,
    )
    width = wout_ref.shape[0]
    half = 2 * width
    first = core_ref[0] == 0
    table = offset_sums(gbias_ref)
    heads = table.shape[0] // 2
    table_ref[...] = jnp.where(first, table[:heads], table[heads:])
    send_ref[width:, :] = jnp.zeros((send_ref.shape[0] - width, half), send_ref.dtype)
    send_ref[width : width + heads, :256] = jnp.where(first, table[heads:], table[:heads]).astype(send_ref.dtype)

    @pl.when(first)
    def _():
        keep_ref[...] = dot(normed[...], gproj[:, :half], 0, 0)
        send_ref[:width, :width] = dot(normed[...], gproj[:, half:], 0, 0).astype(send_ref.dtype)
        send_ref[:width, width:] = dot(att[...], dyp[...], 0, 0).astype(send_ref.dtype)

    @pl.when(jnp.logical_not(first))
    def _():
        send_ref[:width, :] = dot(normed[...], gproj[:, :half], 0, 0).astype(send_ref.dtype)
        keep_ref[:, :width] = dot(normed[...], gproj[:, half:], 0, 0)
        keep_ref[:, width:] = dot(att[...], dyp[...], 0, 0)


def back_kernel(wqkv_ref, gain_ref, gproj, hat, istd, branch_ref, gvec_ref, dyf):
    sums = back_to_input(wqkv_ref, gain_ref, branch_ref, gproj, hat, istd, dyf)
    lanes = hat.shape[0]
    for i in range(2):
        for b in range(lanes):
            gvec_ref[i * lanes + b : i * lanes + b + 1, :] = sums[i][:, b * 128 : (b + 1) * 128]


VMEM = pl.BlockSpec(memory_space=pltpu.VMEM)
SMEM = pl.BlockSpec(memory_space=pltpu.SMEM)
HBM = pl.BlockSpec(memory_space=pltpu.HBM)
MIB = 1024 * 1024


def in_hbm(a):
    return pltpu.with_memory_space_constraint(a, pltpu.HBM)


def shaped(*shape, dtype=jnp.float32):
    return jax.ShapeDtypeStruct(shape, dtype)


def cost(flops, size):
    return pl.CostEstimate(flops=flops, bytes_accessed=size, transcendentals=0)


def part_buffers(rows, width):
    bf16, f32 = jnp.bfloat16, jnp.float32
    tall, lanes = (rows, width), (width // 128, rows, 128)
    return [
        (tall, bf16), ((rows, 3 * width), bf16), (tall, bf16), (tall, bf16), (lanes, f32), ((rows, 128), f32),
        ((rows, 3 * width), bf16), (tall, bf16), (lanes, f32),
    ]


def local_scores(core, pair, wqkv, wout, bias, gain, shift, head_dim):
    members, _, groups, width = pair.shape
    bf16, f32 = jnp.bfloat16, jnp.float32
    normed, gproj, att, dyp, hat, istd, proj, gatt, dyf = part_buffers(groups * MEMBERS, width)
    half_heads = width // head_dim // 2
    return pl.pallas_call(
        functools.partial(scores_kernel, head_dim=head_dim),
        out_shape=(
            shaped(width, 2 * width), shaped(width + 16, 2 * width, dtype=bf16), shaped(half_heads, 256)
        )
        + tuple(jax.ShapeDtypeStruct(*b) for b in (gproj, hat, istd))
        + (jax.ShapeDtypeStruct(wqkv.shape, wqkv.dtype),),
        in_specs=[SMEM, VMEM, HBM, HBM] + [VMEM] * 3,
        out_specs=(VMEM,) * 7,
        scratch_shapes=[pltpu.VMEM(wout.shape, wout.dtype), pltpu.VMEM(bias.shape, f32)]
        + [pltpu.VMEM(*b) for b in (normed, att, dyp, proj, gatt, dyf)]
        + [pltpu.SemaphoreType.DMA((2,))],
        compiler_params=pltpu.CompilerParams(vmem_limit_bytes=28 * MIB),
        cost_estimate=cost(20_000_000_000, 8 << 20),
        name="scores",
    )(core.reshape(1), pair, in_hbm(wqkv), in_hbm(wout), bias, gain.reshape(1, width), shift.reshape(1, width))


def local_back(wqkv, gain, gproj, hat, istd, groups):
    width = gain.shape[0]
    return pl.pallas_call(
        back_kernel,
        out_shape=(shaped(MEMBERS, groups, width, dtype=gproj.dtype), shaped(2 * width // 128, 128)),
        in_specs=[VMEM] * 5,
        out_specs=(VMEM,) * 2,
        scratch_shapes=[pltpu.VMEM(hat.shape, jnp.float32)],
        compiler_params=pltpu.CompilerParams(vmem_limit_bytes=16 * MIB),
        cost_estimate=cost(6_000_000_000, 4 << 20),
        name="back",
    )(wqkv, gain.reshape(1, width), gproj, hat, istd)


def pair_kernel(x_ref, dy_ref, out_ref):
    out_ref[:, 0] = x_ref[...]
    out_ref[:, 1] = dy_ref[...]


def pair_of(x, dy):
    chips, groups, width = x.shape
    step = chips // 2
    source = pl.BlockSpec((step, groups, width), lambda i: (i, 0, 0))
    return pl.pallas_call(
        pair_kernel,
        grid=(chips // step,),
        out_shape=shaped(chips, 2, groups, width, dtype=x.dtype),
        in_specs=[source, source],
        out_specs=pl.BlockSpec((step, 2, groups, width), lambda i: (i, 0, 0, 0)),
        cost_estimate=cost(0, 4 << 20),
        name="pair",
    )(x, dy)


def outgoing_kernel(branch_ref, keep_ref, recv_ref, table_ref, gvec_ref, out_ref):
    chips, _, share, _ = out_ref.shape
    _, groups, width = branch_ref.shape
    f32, bf16 = jnp.float32, jnp.bfloat16
    slot = 0
    for b in range(width // 128):
        for t in range(groups // share):
            out_ref[:, slot] = branch_ref[:, t * share : (t + 1) * share, b * 128 : (b + 1) * 128]
            slot += 1
    for b in range(2 * width // 128):
        cols = slice(b * 128, (b + 1) * 128)
        total = (keep_ref[:, cols] + recv_ref[:width, cols].astype(f32)).astype(bf16)
        out_ref[:, slot] = total.reshape(chips, share, 128)
        slot += 1
    table = table_ref[...] + recv_ref[width : width + share, :256].astype(f32)
    for value in (table[:, :128], table[:, 128:], gvec_ref[...]):
        out_ref[:, slot] = jnp.broadcast_to(value.astype(bf16)[None], (chips, share, 128))
        slot += 1


def outgoing(branch, keep, recv, table, gvec):
    chips, groups, width = branch.shape
    share = width // chips
    slots = groups // share * width // 128 + 2 * width // 128 + 3
    return pl.pallas_call(
        outgoing_kernel,
        out_shape=shaped(chips, slots, share, 128, dtype=branch.dtype),
        in_specs=[VMEM] * 5,
        out_specs=VMEM,
        compiler_params=pltpu.CompilerParams(vmem_limit_bytes=16 * MIB),
        cost_estimate=cost(0, 6 << 20),
        name="outgoing",
    )(branch, keep, recv, table, gvec)


def sums_kernel(core_ref, got_ref, keep_ref, send_ref, *, begin, factor):
    f32 = jnp.float32
    chips, slots, share, _ = got_ref.shape
    total = got_ref[0, begin:].astype(f32)
    for chip in range(1, chips):
        total = total + got_ref[chip, begin:].astype(f32)
    total = total * factor
    part = share // 2
    weights = slots - begin - 3
    for b in range(weights):
        rows = slice(b * part, (b + 1) * part)
        low, high = total[b, :part], total[b, part:]
        keep_ref[rows, :] = jnp.where(core_ref[0] == 0, low, high)
        send_ref[rows, :] = jnp.where(core_ref[0] == 0, high, low)
    for i in range(3):
        rows = slice(weights * part + i * share, weights * part + (i + 1) * share)
        keep_ref[rows, :] = total[weights + i]
        send_ref[rows, :] = total[weights + i]


def sums_of(core, got, begin, factor):
    chips, slots, share, _ = got.shape
    rows = (slots - begin - 3) * share // 2 + 3 * share
    return pl.pallas_call(
        functools.partial(sums_kernel, begin=begin, factor=factor),
        out_shape=(shaped(rows, 128), shaped(rows, 128)),
        in_specs=[SMEM, VMEM],
        out_specs=(VMEM,) * 2,
        compiler_params=pltpu.CompilerParams(vmem_limit_bytes=16 * MIB),
        cost_estimate=cost(0, 2 << 20),
        name="sums",
    )(core.reshape(1), got)


def input_kernel(got_ref, dy_ref, grad_ref):
    _, groups, width = dy_ref.shape
    share = got_ref.shape[2]
    f32 = jnp.float32
    slot = 0
    for b in range(width // 128):
        cols = slice(b * 128, (b + 1) * 128)
        for t in range(groups // share):
            rows = slice(t * share, (t + 1) * share)
            branch = got_ref[:, slot].astype(f32)
            grad_ref[:, rows, cols] = (dy_ref[:, rows, cols].astype(f32) + branch).astype(grad_ref.dtype)
            slot += 1


def input_gradient(got, dy):
    return pl.pallas_call(
        input_kernel,
        out_shape=jax.ShapeDtypeStruct(dy.shape, dy.dtype),
        in_specs=[VMEM] * 2,
        out_specs=VMEM,
        compiler_params=pltpu.CompilerParams(vmem_limit_bytes=16 * MIB),
        cost_estimate=cost(0, 4 << 20),
        name="input_gradient",
    )(got, dy)


def finish_kernel(core_ref, keep_ref, recv_ref, qkv_ref, out_ref, table_ref, gain_ref, shift_ref):
    width = out_ref.shape[1]
    lanes = width // 128
    part, heads = out_ref.shape[0], table_ref.shape[0] // 2
    first = core_ref[0] == 0

    def ordered(mine, other):
        return jnp.where(first, mine, other), jnp.where(first, other, mine)

    for b in range(2 * lanes):
        rows = slice(b * part, (b + 1) * part)
        low, high = ordered(keep_ref[rows, :], recv_ref[rows, :])
        qkv_ref[:, b * 128 : (b + 1) * 128] = low
        if b < lanes:
            qkv_ref[:, 2 * width + b * 128 : 2 * width + (b + 1) * 128] = high
        else:
            out_ref[:, (b - lanes) * 128 : (b - lanes + 1) * 128] = high
    at = 2 * lanes * part
    halves = [jnp.concatenate([ref[at : at + heads], ref[at + heads : at + 2 * heads]], axis=1) for ref in (keep_ref, recv_ref)]
    table = jnp.concatenate(ordered(*halves), axis=0)
    side = 2 * GRID - 1
    place = lax.broadcasted_iota(jnp.int32, (256, side * side), 0)
    offset = lax.broadcasted_iota(jnp.int32, (256, side * side), 1)
    row, column = side - 1 - offset // side, side - 1 - offset % side
    pick = (place == row * 16 + column).astype(jnp.float32)
    table_ref[...] = lax.dot_general(
        table, pick, (((1,), (0,)), ((), ())), precision=lax.Precision.HIGHEST, preferred_element_type=jnp.float32
    )
    at += 2 * heads
    vectors = keep_ref[at:, :] + recv_ref[at:, :]
    for ref, row in ((gain_ref, 0), (shift_ref, lanes)):
        for b in range(lanes):
            ref[:, b * 128 : (b + 1) * 128] = vectors[row + b : row + b + 1]


def finish(core, keep, recv, part, width, heads, offsets):
    return pl.pallas_call(
        finish_kernel,
        out_shape=(
            shaped(part, 3 * width), shaped(part, width), shaped(heads, offsets), shaped(1, width), shaped(1, width)
        ),
        in_specs=[SMEM, VMEM, VMEM],
        out_specs=(VMEM,) * 5,
        compiler_params=pltpu.CompilerParams(vmem_limit_bytes=8 * MIB),
        name="finish",
    )(core.reshape(1), keep, recv)


AXES = ("x_lo", "y", "x_hi", "z", "core")
CHIPS = AXES[:4]


def relative_onehot(members):
    span = 2 * GRID - 1
    second = jnp.arange(members, dtype=jnp.int32)[:, None]
    first = jnp.arange(members, dtype=jnp.int32)[None, :]
    row_delta = first // GRID - second // GRID + GRID - 1
    col_delta = first % GRID - second % GRID + GRID - 1
    rel_index = row_delta * span + col_delta
    offsets = jnp.arange(span * span, dtype=jnp.int32)
    return (rel_index[:, :, None] == offsets).astype(jnp.float32)


def swap(a, axis, mask):
    size = lax.axis_size(axis)
    return lax.ppermute(a, axis, [(i, i ^ mask) for i in range(size)])


def local(block_input, cotangent, qkv_weight, out_weight, bias_table, norm_gain, norm_shift):
    tile_h, tile_w, width = block_input.shape
    heads, offsets = bias_table.shape
    chips = lax.axis_size(CHIPS)
    devices = chips * lax.axis_size("core")
    owned = tile_h * tile_w // chips
    core = lax.axis_index("core")
    onehot = relative_onehot(MEMBERS)
    bias = jnp.einsum(
        "bhr,kqr->bkhq",
        bias_table.reshape(heads // PACK, PACK, offsets),
        onehot,
        precision=lax.Precision.HIGHEST,
    ).reshape(heads // PACK, MEMBERS, PACK * MEMBERS)
    x = block_input.reshape(chips, owned, width)
    dy = cotangent.reshape(chips, owned, width)
    exchange = functools.partial(lax.all_to_all, axis_name=CHIPS, split_axis=0, concat_axis=0, tiled=True)
    got = exchange(pair_of(x, dy))
    keep, send, table, gproj, hat, istd, qkv_copy = local_scores(
        core, got, qkv_weight, out_weight, bias, norm_gain, norm_shift, width // heads
    )
    recv = swap(send, "core", 1)
    branch, gvec = local_back(qkv_copy, norm_gain, gproj, hat, istd, owned)
    got = exchange(outgoing(branch, keep, recv, table, gvec))
    factor = float(tile_h * tile_w * devices) ** (-0.5)
    share = width // chips
    mine, theirs = sums_of(core, got, owned // share * width // 128, factor)
    recv = swap(theirs, "core", 1)
    grad_input = input_gradient(got, dy)
    grad_qkv, grad_out, table, gain, shift = finish(core, mine, recv, share // 2, width, heads, offsets)
    return (
        grad_input.reshape(tile_h, tile_w, width),
        grad_qkv,
        grad_out,
        table,
        gain.reshape(width),
        shift.reshape(width),
    )


def solution(mesh):
    fine = Mesh(mesh.devices.reshape(2, 4, 2, 4, 2), AXES)
    tile = P(("x_lo", "y"), ("x_hi", "z", "core"), None)
    return jax.shard_map(
        local,
        mesh=fine,
        in_specs=(tile, tile, P(), P(), P(), P(), P()),
        out_specs=(tile, P(AXES, None), P(AXES, None), P(), P(), P()),
        check_vma=False,
    )
```

```python
import functools
import jax
import jax.numpy as jnp
from jax import lax
from jax.experimental import pallas as pl
from jax.experimental.pallas import tpu as pltpu
from jax.sharding import Mesh, PartitionSpec as P

GRID = 8
EPSILON = 1e-05
MEMBERS = GRID * GRID
PACK = 4
CHUNK = 256


def dot(a, b, ca, cb):
    return lax.dot_general(a, b, (((ca,), (cb,)), ((), ())), preferred_element_type=jnp.float32)


def put(ref, at, value):
    for b in range(ref.shape[0]):
        ref[b, at, :] = value[:, b * 128 : (b + 1) * 128]


def take(ref, at):
    return jnp.concatenate([ref[b, at, :] for b in range(ref.shape[0])], axis=1)


def forward_and_scores(
    pair_ref, wqkv_ref, wout_ref, bias_ref, gain_ref, shift_ref, gbias_ref,
    normed, gproj, att, dyp, hat, istd, proj, gatt, dyf, head_dim, fetches,
):
    width = gproj.shape[1] // 3
    rows, groups, chunk = gproj.shape[0], gproj.shape[0] // MEMBERS, CHUNK
    per, mem = chunk // MEMBERS, chunk // groups
    bf16, f32 = jnp.bfloat16, jnp.float32
    scale = head_dim ** (-0.5)

    def hat_step(c, carry):
        here = pl.ds(pl.multiple_of(c * chunk, chunk), chunk)
        pair = pair_ref[pl.ds(pl.multiple_of(c * mem, mem), mem)].astype(f32)
        x = pair[:, 0].reshape(chunk, width)
        centred = x - jnp.mean(x, axis=-1, keepdims=True)
        inv = lax.rsqrt(jnp.mean(centred * centred, axis=-1, keepdims=True) + EPSILON)
        put(hat, here, centred * inv)
        istd[here, :] = jnp.broadcast_to(inv, (chunk, 128))
        put(dyf, here, pair[:, 1].reshape(chunk, width))
        return carry

    lax.fori_loop(0, rows // chunk, hat_step, 0)
    for fetch in fetches:
        fetch.wait()

    def by_group(ref, c):
        return jnp.concatenate(
            [take(ref, pl.ds(c * per + g, MEMBERS, stride=groups)) for g in range(per)], axis=0
        )

    def norm_step(c, carry):
        here = pl.ds(pl.multiple_of(c * chunk, chunk), chunk)
        nb = (by_group(hat, c) * gain_ref[...] + shift_ref[...]).astype(bf16)
        dy = by_group(dyf, c).astype(bf16)
        dyp[here, :] = dy
        normed[here, :] = nb
        proj[here, :] = dot(nb, wqkv_ref[...], 1, 0).astype(bf16)
        gatt[here, :] = dot(dy, wout_ref[...], 1, 1).astype(bf16)
        return carry

    lax.fori_loop(0, rows // chunk, norm_step, 0, unroll=True)

    lane = lax.broadcasted_iota(jnp.int32, (MEMBERS, 128), 1) // head_dim

    def spread(a):
        zero = jnp.zeros_like(a)
        return jnp.concatenate([jnp.where(lane == h, a, zero) for h in range(PACK)], axis=0)

    def gather(a):
        out = a[:MEMBERS]
        for h in range(1, PACK):
            out = jnp.where(lane == h, a[h * MEMBERS : (h + 1) * MEMBERS], out)
        return out

    blocks = range(width // 128)

    qcols = [slice(b * 128, (b + 1) * 128) for b in blocks]
    kcols = [slice(width + b * 128, width + (b + 1) * 128) for b in blocks]
    vcols = [slice(2 * width + b * 128, 2 * width + (b + 1) * 128) for b in blocks]

    def stacked(top, low):
        none = jnp.zeros_like(top)
        return jnp.concatenate(
            [jnp.concatenate([top, none], axis=1), jnp.concatenate([none, low], axis=1)], axis=0
        )

    def products(g):
        here = slice(g * MEMBERS, (g + 1) * MEMBERS)
        ws = [jnp.concatenate([spread(proj[here, c]), spread(gatt[here, c])], axis=1) for c in qcols]
        return ws, [dot(stacked(proj[here, k], proj[here, v]), w, 1, 1) for k, v, w in zip(kcols, vcols, ws)]

    def softmax(b, both):
        scores = both[:MEMBERS] * scale + bias_ref[b]
        gp = both[MEMBERS:]
        e = jnp.exp(scores - jnp.max(scores, axis=0, keepdims=True))
        p = e * (1.0 / jnp.sum(e, axis=0, keepdims=True))
        gs = p * (gp - jnp.sum(gp * p, axis=0, keepdims=True))
        gbias_ref[b] += gs
        return jnp.concatenate([p.astype(bf16), (gs * scale).astype(bf16)], axis=0)

    def store(g, keyed, queried):
        here = slice(g * MEMBERS, (g + 1) * MEMBERS)
        for b in blocks:
            att[here, qcols[b]] = gather(queried[b][:, :128]).astype(bf16)
            gproj[here, qcols[b]] = gather(queried[b][:, 128:]).astype(bf16)
            gproj[here, kcols[b]] = keyed[b][MEMBERS:, :128].astype(bf16)
            gproj[here, vcols[b]] = keyed[b][:MEMBERS, 128:].astype(bf16)

    ahead, behind = products(0), None
    for g in range(groups):
        here = slice(g * MEMBERS, (g + 1) * MEMBERS)
        ws, both = ahead
        keyed, queried, ws_next, both_next = [], [], [], []
        more = products(g + 1) if g + 1 < groups else ([], [])
        ws_next, both_next = more
        for b in blocks:
            pd = softmax(b, both[b])
            keyed.append(dot(pd, ws[b], 1, 0))
            queried.append(dot(pd, stacked(proj[here, vcols[b]], proj[here, kcols[b]]), 0, 0))
        if behind is not None:
            store(g - 1, *behind)
        behind = (keyed, queried)
        ahead = (ws_next, both_next)
    store(groups - 1, *behind)


def back_to_input(wqkv_ref, gain_ref, branch_ref, gproj, hat, istd, dyf):
    width = gproj.shape[1] // 3
    rows, groups, chunk = gproj.shape[0], gproj.shape[0] // MEMBERS, CHUNK
    per, mem = chunk // MEMBERS, chunk // groups
    bf16, f32 = jnp.bfloat16, jnp.float32

    def gn_step(c, carry):
        here = pl.ds(pl.multiple_of(c * chunk, chunk), chunk)
        gn = dot(gproj[here, :], wqkv_ref[...], 1, 1)
        for g in range(per):
            put(dyf, pl.ds(c * per + g, MEMBERS, stride=groups), gn[g * MEMBERS : (g + 1) * MEMBERS])
        return carry

    lax.fori_loop(0, rows // chunk, gn_step, 0, unroll=True)

    def back_step(c, carry):
        gg, gsh = carry
        here = pl.ds(pl.multiple_of(c * chunk, chunk), chunk)
        gn = take(dyf, here)
        normalized = take(hat, here)
        prod = gn * normalized
        gg = gg + jnp.sum(prod.reshape(chunk // 8, 8, width), axis=0)
        gsh = gsh + jnp.sum(gn.reshape(chunk // 8, 8, width), axis=0)
        gh = gn * gain_ref[...]
        m1 = jnp.mean(gh, axis=-1, keepdims=True)
        m2 = jnp.mean(prod * gain_ref[...], axis=-1, keepdims=True)
        inv = istd[here, :][:, :1]
        branch = (inv * (gh - m1 - normalized * m2)).astype(bf16)
        branch_ref[pl.ds(pl.multiple_of(c * mem, mem), mem)] = branch.reshape(mem, groups, width)
        return gg, gsh

    zero = jnp.zeros((8, width), f32)
    gg, gsh = lax.fori_loop(0, rows // chunk, back_step, (zero, zero), unroll=True)
    return jnp.sum(gg, axis=0, keepdims=True), jnp.sum(gsh, axis=0, keepdims=True)


def offset_sums(gbias_ref):
    f32, bf16 = jnp.float32, jnp.bfloat16
    blocks, members, lanes = gbias_ref.shape
    i = lax.broadcasted_iota(jnp.int32, (lanes, 2 * lanes), 0)
    o = lax.broadcasted_iota(jnp.int32, (lanes, 2 * lanes), 1)
    query = GRID * GRID - 1 - i % members
    wide = (o == i // members * 128 + query // GRID * 16 + query % GRID).astype(f32).astype(bf16)
    spreads = []
    for b in range(blocks):
        value = gbias_ref[b]
        high = value.astype(bf16)
        rest = value - high.astype(f32)
        low = rest.astype(bf16)
        lowest = (rest - low.astype(f32)).astype(bf16)
        parts = dot(jnp.concatenate([high, low, lowest], axis=0), wide, 1, 0)
        spreads.append(parts[:members] + (parts[members : 2 * members] + parts[2 * members :]))
    sums = []
    for b in range(blocks):
        for h in range(PACK):
            frame = spreads[b][:, h * 128 : (h + 1) * 128]
            total = None
            for row in range(GRID):
                piece = frame[row * GRID : (row + 1) * GRID]
                piece = jnp.concatenate([piece, jnp.zeros_like(piece)], axis=1)
                piece = pltpu.roll(piece, row * 16, 1, stride=1, stride_axis=0)
                total = piece if total is None else total + piece
            sums.append(jnp.sum(total, axis=0, keepdims=True))
    return jnp.concatenate(sums, axis=0)


def scores_kernel(
    core_ref, pair_ref, wqkv_hbm, wout_hbm, bias_ref, gain_ref, shift_ref,
    keep_ref, send_ref, table_ref, gproj, hat, istd, wqkv_ref,
    wout_ref, gbias_ref, normed, att, dyp, proj, gatt, dyf, sems, *, head_dim,
):
    fetches = [
        pltpu.make_async_copy(wqkv_hbm, wqkv_ref, sems.at[0]),
        pltpu.make_async_copy(wout_hbm, wout_ref, sems.at[1]),
    ]
    for fetch in fetches:
        fetch.start()
    gbias_ref[...] = jnp.zeros_like(gbias_ref)
    forward_and_scores(
        pair_ref, wqkv_ref, wout_ref, bias_ref, gain_ref, shift_ref, gbias_ref,
        normed, gproj, att, dyp, hat, istd, proj, gatt, dyf, head_dim, fetches,
    )
    width = wout_ref.shape[0]
    half = 2 * width
    first = core_ref[0] == 0
    table = offset_sums(gbias_ref)
    heads = table.shape[0] // 2
    table_ref[...] = jnp.where(first, table[:heads], table[heads:])
    send_ref[width:, :] = jnp.zeros((send_ref.shape[0] - width, half), send_ref.dtype)
    send_ref[width : width + heads, :256] = jnp.where(first, table[heads:], table[:heads]).astype(send_ref.dtype)

    turned = normed[...].T
    for piece in range(4):
        cols = slice(piece * 256, (piece + 1) * 256)
        low = dot(turned, gproj[:, cols], 1, 0)
        if piece < 2:
            high = dot(turned, gproj[:, half + piece * 256 : half + (piece + 1) * 256], 1, 0)
        else:
            high = dot(att[...], dyp[:, (piece - 2) * 256 : (piece - 1) * 256], 0, 0)
        keep_ref[:, cols] = jnp.where(first, low, high)
        send_ref[:width, cols] = jnp.where(first, high, low).astype(send_ref.dtype)


def back_kernel(wqkv_ref, gain_ref, gproj, hat, istd, branch_ref, gvec_ref, dyf):
    sums = back_to_input(wqkv_ref, gain_ref, branch_ref, gproj, hat, istd, dyf)
    lanes = hat.shape[0]
    for i in range(2):
        for b in range(lanes):
            gvec_ref[i * lanes + b : i * lanes + b + 1, :] = sums[i][:, b * 128 : (b + 1) * 128]


VMEM = pl.BlockSpec(memory_space=pltpu.VMEM)
SMEM = pl.BlockSpec(memory_space=pltpu.SMEM)
HBM = pl.BlockSpec(memory_space=pltpu.HBM)
MIB = 1024 * 1024


def in_hbm(a):
    return pltpu.with_memory_space_constraint(a, pltpu.HBM)


def shaped(*shape, dtype=jnp.float32):
    return jax.ShapeDtypeStruct(shape, dtype)


def cost(flops, size):
    return pl.CostEstimate(flops=flops, bytes_accessed=size, transcendentals=0)


def part_buffers(rows, width):
    bf16, f32 = jnp.bfloat16, jnp.float32
    tall, lanes = (rows, width), (width // 128, rows, 128)
    return [
        (tall, bf16), ((rows, 3 * width), bf16), (tall, bf16), (tall, bf16), (lanes, f32), ((rows, 128), f32),
        ((rows, 3 * width), bf16), (tall, bf16), (lanes, f32),
    ]


def local_scores(core, pair, wqkv, wout, bias, gain, shift, head_dim):
    members, _, groups, width = pair.shape
    bf16, f32 = jnp.bfloat16, jnp.float32
    normed, gproj, att, dyp, hat, istd, proj, gatt, dyf = part_buffers(groups * MEMBERS, width)
    half_heads = width // head_dim // 2
    return pl.pallas_call(
        functools.partial(scores_kernel, head_dim=head_dim),
        out_shape=(
            shaped(width, 2 * width), shaped(width + 16, 2 * width, dtype=bf16), shaped(half_heads, 256)
        )
        + tuple(jax.ShapeDtypeStruct(*b) for b in (gproj, hat, istd))
        + (jax.ShapeDtypeStruct(wqkv.shape, wqkv.dtype),),
        in_specs=[SMEM, VMEM, HBM, HBM] + [VMEM] * 3,
        out_specs=(VMEM,) * 7,
        scratch_shapes=[pltpu.VMEM(wout.shape, wout.dtype), pltpu.VMEM(bias.shape, f32)]
        + [pltpu.VMEM(*b) for b in (normed, att, dyp, proj, gatt, dyf)]
        + [pltpu.SemaphoreType.DMA((2,))],
        compiler_params=pltpu.CompilerParams(vmem_limit_bytes=28 * MIB),
        cost_estimate=cost(20_000_000_000, 8 << 20),
        name="scores",
    )(core.reshape(1), pair, in_hbm(wqkv), in_hbm(wout), bias, gain.reshape(1, width), shift.reshape(1, width))


def local_back(wqkv, gain, gproj, hat, istd, groups):
    width = gain.shape[0]
    return pl.pallas_call(
        back_kernel,
        out_shape=(shaped(MEMBERS, groups, width, dtype=gproj.dtype), shaped(2 * width // 128, 128)),
        in_specs=[VMEM] * 5,
        out_specs=(VMEM,) * 2,
        scratch_shapes=[pltpu.VMEM(hat.shape, jnp.float32)],
        compiler_params=pltpu.CompilerParams(vmem_limit_bytes=16 * MIB),
        cost_estimate=cost(6_000_000_000, 4 << 20),
        name="back",
    )(wqkv, gain.reshape(1, width), gproj, hat, istd)


def pair_kernel(x_ref, dy_ref, out_ref):
    out_ref[:, 0] = x_ref[...]
    out_ref[:, 1] = dy_ref[...]


def pair_of(x, dy):
    chips, groups, width = x.shape
    step = chips // 2
    source = pl.BlockSpec((step, groups, width), lambda i: (i, 0, 0))
    return pl.pallas_call(
        pair_kernel,
        grid=(chips // step,),
        out_shape=shaped(chips, 2, groups, width, dtype=x.dtype),
        in_specs=[source, source],
        out_specs=pl.BlockSpec((step, 2, groups, width), lambda i: (i, 0, 0, 0)),
        cost_estimate=cost(0, 4 << 20),
        name="pair",
    )(x, dy)


def outgoing_kernel(branch_ref, keep_ref, recv_ref, table_ref, gvec_ref, out_ref):
    chips, _, share, _ = out_ref.shape
    _, groups, width = branch_ref.shape
    f32, bf16 = jnp.float32, jnp.bfloat16
    slot = 0
    for b in range(width // 128):
        for t in range(groups // share):
            out_ref[:, slot] = branch_ref[:, t * share : (t + 1) * share, b * 128 : (b + 1) * 128]
            slot += 1
    for b in range(2 * width // 128):
        cols = slice(b * 128, (b + 1) * 128)
        total = (keep_ref[:, cols] + recv_ref[:width, cols].astype(f32)).astype(bf16)
        out_ref[:, slot] = total.reshape(chips, share, 128)
        slot += 1
    table = table_ref[...] + recv_ref[width : width + share, :256].astype(f32)
    for value in (table[:, :128], table[:, 128:], gvec_ref[...]):
        out_ref[:, slot] = jnp.broadcast_to(value.astype(bf16)[None], (chips, share, 128))
        slot += 1


def outgoing(branch, keep, recv, table, gvec):
    chips, groups, width = branch.shape
    share = width // chips
    slots = groups // share * width // 128 + 2 * width // 128 + 3
    return pl.pallas_call(
        outgoing_kernel,
        out_shape=shaped(chips, slots, share, 128, dtype=branch.dtype),
        in_specs=[VMEM] * 5,
        out_specs=VMEM,
        compiler_params=pltpu.CompilerParams(vmem_limit_bytes=16 * MIB),
        cost_estimate=cost(0, 6 << 20),
        name="outgoing",
    )(branch, keep, recv, table, gvec)


def sums_kernel(core_ref, got_ref, keep_ref, send_ref, *, begin, factor):
    f32 = jnp.float32
    chips, slots, share, _ = got_ref.shape
    total = got_ref[0, begin:].astype(f32)
    for chip in range(1, chips):
        total = total + got_ref[chip, begin:].astype(f32)
    total = total * factor
    part = share // 2
    weights = slots - begin - 3
    for b in range(weights):
        rows = slice(b * part, (b + 1) * part)
        low, high = total[b, :part], total[b, part:]
        keep_ref[rows, :] = jnp.where(core_ref[0] == 0, low, high)
        send_ref[rows, :] = jnp.where(core_ref[0] == 0, high, low)
    for i in range(3):
        rows = slice(weights * part + i * share, weights * part + (i + 1) * share)
        keep_ref[rows, :] = total[weights + i]
        send_ref[rows, :] = total[weights + i]


def sums_of(core, got, begin, factor):
    chips, slots, share, _ = got.shape
    rows = (slots - begin - 3) * share // 2 + 3 * share
    return pl.pallas_call(
        functools.partial(sums_kernel, begin=begin, factor=factor),
        out_shape=(shaped(rows, 128), shaped(rows, 128)),
        in_specs=[SMEM, VMEM],
        out_specs=(VMEM,) * 2,
        compiler_params=pltpu.CompilerParams(vmem_limit_bytes=16 * MIB),
        cost_estimate=cost(0, 2 << 20),
        name="sums",
    )(core.reshape(1), got)


def input_kernel(got_ref, dy_ref, grad_ref):
    step, groups, width = dy_ref.shape
    share = got_ref.shape[2]
    f32 = jnp.float32
    chips = pl.ds(pl.multiple_of(pl.program_id(0) * step, step), step)
    slot = 0
    for b in range(width // 128):
        cols = slice(b * 128, (b + 1) * 128)
        for t in range(groups // share):
            rows = slice(t * share, (t + 1) * share)
            branch = got_ref[chips, slot].astype(f32)
            grad_ref[:, rows, cols] = (dy_ref[:, rows, cols].astype(f32) + branch).astype(grad_ref.dtype)
            slot += 1


def input_gradient(got, dy):
    chips, groups, width = dy.shape
    block = pl.BlockSpec((chips // 2, groups, width), lambda i: (i, 0, 0))
    return pl.pallas_call(
        input_kernel,
        grid=(2,),
        out_shape=jax.ShapeDtypeStruct(dy.shape, dy.dtype),
        in_specs=[VMEM, block],
        out_specs=block,
        compiler_params=pltpu.CompilerParams(vmem_limit_bytes=16 * MIB),
        cost_estimate=cost(0, 4 << 20),
        name="input_gradient",
    )(got, in_hbm(dy))


def finish_kernel(core_ref, keep_ref, recv_ref, qkv_ref, out_ref, table_ref, gain_ref, shift_ref):
    width = out_ref.shape[1]
    lanes = width // 128
    part, heads = out_ref.shape[0], table_ref.shape[0] // 2
    first = core_ref[0] == 0

    def ordered(mine, other):
        return jnp.where(first, mine, other), jnp.where(first, other, mine)

    for b in range(2 * lanes):
        rows = slice(b * part, (b + 1) * part)
        low, high = ordered(keep_ref[rows, :], recv_ref[rows, :])
        qkv_ref[:, b * 128 : (b + 1) * 128] = low
        if b < lanes:
            qkv_ref[:, 2 * width + b * 128 : 2 * width + (b + 1) * 128] = high
        else:
            out_ref[:, (b - lanes) * 128 : (b - lanes + 1) * 128] = high
    at = 2 * lanes * part
    halves = [jnp.concatenate([ref[at : at + heads], ref[at + heads : at + 2 * heads]], axis=1) for ref in (keep_ref, recv_ref)]
    table = jnp.concatenate(ordered(*halves), axis=0)
    side = 2 * GRID - 1
    place = lax.broadcasted_iota(jnp.int32, (256, side * side), 0)
    offset = lax.broadcasted_iota(jnp.int32, (256, side * side), 1)
    row, column = side - 1 - offset // side, side - 1 - offset % side
    pick = (place == row * 16 + column).astype(jnp.float32)
    table_ref[...] = lax.dot_general(
        table, pick, (((1,), (0,)), ((), ())), precision=lax.Precision.HIGHEST, preferred_element_type=jnp.float32
    )
    at += 2 * heads
    vectors = keep_ref[at:, :] + recv_ref[at:, :]
    for ref, row in ((gain_ref, 0), (shift_ref, lanes)):
        for b in range(lanes):
            ref[:, b * 128 : (b + 1) * 128] = vectors[row + b : row + b + 1]


def finish(core, keep, recv, part, width, heads, offsets):
    return pl.pallas_call(
        finish_kernel,
        out_shape=(
            shaped(part, 3 * width), shaped(part, width), shaped(heads, offsets), shaped(1, width), shaped(1, width)
        ),
        in_specs=[SMEM, VMEM, VMEM],
        out_specs=(VMEM,) * 5,
        compiler_params=pltpu.CompilerParams(vmem_limit_bytes=8 * MIB),
        name="finish",
    )(core.reshape(1), keep, recv)


AXES = ("x_lo", "y", "x_hi", "z", "core")
CHIPS = AXES[:4]


def relative_onehot(members):
    span = 2 * GRID - 1
    second = jnp.arange(members, dtype=jnp.int32)[:, None]
    first = jnp.arange(members, dtype=jnp.int32)[None, :]
    row_delta = first // GRID - second // GRID + GRID - 1
    col_delta = first % GRID - second % GRID + GRID - 1
    rel_index = row_delta * span + col_delta
    offsets = jnp.arange(span * span, dtype=jnp.int32)
    return (rel_index[:, :, None] == offsets).astype(jnp.float32)


def swap(a, axis, mask):
    size = lax.axis_size(axis)
    return lax.ppermute(a, axis, [(i, i ^ mask) for i in range(size)])


def local(block_input, cotangent, qkv_weight, out_weight, bias_table, norm_gain, norm_shift):
    tile_h, tile_w, width = block_input.shape
    heads, offsets = bias_table.shape
    chips = lax.axis_size(CHIPS)
    devices = chips * lax.axis_size("core")
    owned = tile_h * tile_w // chips
    core = lax.axis_index("core")
    onehot = relative_onehot(MEMBERS)
    bias = jnp.einsum(
        "bhr,kqr->bkhq",
        bias_table.reshape(heads // PACK, PACK, offsets),
        onehot,
        precision=lax.Precision.HIGHEST,
    ).reshape(heads // PACK, MEMBERS, PACK * MEMBERS)
    x = block_input.reshape(chips, owned, width)
    dy = cotangent.reshape(chips, owned, width)
    exchange = functools.partial(lax.all_to_all, axis_name=CHIPS, split_axis=0, concat_axis=0, tiled=True)
    got = exchange(pair_of(x, dy))
    keep, send, table, gproj, hat, istd, qkv_copy = local_scores(
        core, got, qkv_weight, out_weight, bias, norm_gain, norm_shift, width // heads
    )
    recv = swap(send, "core", 1)
    branch, gvec = local_back(qkv_copy, norm_gain, gproj, hat, istd, owned)
    got = exchange(outgoing(branch, keep, recv, table, gvec))
    factor = float(tile_h * tile_w * devices) ** (-0.5)
    share = width // chips
    mine, theirs = sums_of(core, got, owned // share * width // 128, factor)
    recv = swap(theirs, "core", 1)
    grad_input = input_gradient(got, dy)
    grad_qkv, grad_out, table, gain, shift = finish(core, mine, recv, share // 2, width, heads, offsets)
    return (
        grad_input.reshape(tile_h, tile_w, width),
        grad_qkv,
        grad_out,
        table,
        gain.reshape(width),
        shift.reshape(width),
    )


def solution(mesh):
    fine = Mesh(mesh.devices.reshape(2, 4, 2, 4, 2), AXES)
    tile = P(("x_lo", "y"), ("x_hi", "z", "core"), None)
    return jax.shard_map(
        local,
        mesh=fine,
        in_specs=(tile, tile, P(), P(), P(), P(), P()),
        out_specs=(tile, P(AXES, None), P(AXES, None), P(), P(), P()),
        check_vma=False,
    )
```

```python
import functools
import jax
import jax.numpy as jnp
from jax import lax
from jax.experimental import pallas as pl
from jax.experimental.pallas import tpu as pltpu
from jax.sharding import Mesh, PartitionSpec as P

GRID = 8
EPSILON = 1e-05
MEMBERS = GRID * GRID
PACK = 4
CHUNK = 256


def dot(a, b, ca, cb):
    return lax.dot_general(a, b, (((ca,), (cb,)), ((), ())), preferred_element_type=jnp.float32)


def put(ref, at, value):
    for b in range(ref.shape[0]):
        ref[b, at, :] = value[:, b * 128 : (b + 1) * 128]


def take(ref, at):
    return jnp.concatenate([ref[b, at, :] for b in range(ref.shape[0])], axis=1)


def forward_and_scores(
    pair_ref, wqkv_ref, wout_ref, bias_ref, gain_ref, shift_ref, gbias_ref,
    normed, gproj, att, dyp, hat, istd, proj, gatt, dyf, head_dim, fetches,
):
    width = gproj.shape[1] // 3
    rows, groups, chunk = gproj.shape[0], gproj.shape[0] // MEMBERS, CHUNK
    per, mem = chunk // MEMBERS, chunk // groups
    bf16, f32 = jnp.bfloat16, jnp.float32
    scale = head_dim ** (-0.5)

    def hat_step(c, carry):
        here = pl.ds(pl.multiple_of(c * chunk, chunk), chunk)
        pair = pair_ref[pl.ds(pl.multiple_of(c * mem, mem), mem)].astype(f32)
        x = pair[:, 0].reshape(chunk, width)
        centred = x - jnp.mean(x, axis=-1, keepdims=True)
        inv = lax.rsqrt(jnp.mean(centred * centred, axis=-1, keepdims=True) + EPSILON)
        put(hat, here, centred * inv)
        istd[here, :] = jnp.broadcast_to(inv, (chunk, 128))
        put(dyf, here, pair[:, 1].reshape(chunk, width))
        return carry

    lax.fori_loop(0, rows // chunk, hat_step, 0)
    for fetch in fetches:
        fetch.wait()

    def by_group(ref, c):
        return jnp.concatenate(
            [take(ref, pl.ds(c * per + g, MEMBERS, stride=groups)) for g in range(per)], axis=0
        )

    def norm_step(c, carry):
        here = pl.ds(pl.multiple_of(c * chunk, chunk), chunk)
        nb = (by_group(hat, c) * gain_ref[...] + shift_ref[...]).astype(bf16)
        dy = by_group(dyf, c).astype(bf16)
        dyp[here, :] = dy
        normed[here, :] = nb
        proj[here, :] = dot(nb, wqkv_ref[...], 1, 0).astype(bf16)
        gatt[here, :] = dot(dy, wout_ref[...], 1, 1).astype(bf16)
        return carry

    lax.fori_loop(0, rows // chunk, norm_step, 0, unroll=True)

    lane = lax.broadcasted_iota(jnp.int32, (MEMBERS, 128), 1) // head_dim

    def spread(a):
        zero = jnp.zeros_like(a)
        return jnp.concatenate([jnp.where(lane == h, a, zero) for h in range(PACK)], axis=0)

    def gather(a):
        out = a[:MEMBERS]
        for h in range(1, PACK):
            out = jnp.where(lane == h, a[h * MEMBERS : (h + 1) * MEMBERS], out)
        return out

    blocks = range(width // 128)

    qcols = [slice(b * 128, (b + 1) * 128) for b in blocks]
    kcols = [slice(width + b * 128, width + (b + 1) * 128) for b in blocks]
    vcols = [slice(2 * width + b * 128, 2 * width + (b + 1) * 128) for b in blocks]

    def stacked(top, low):
        none = jnp.zeros_like(top)
        return jnp.concatenate(
            [jnp.concatenate([top, none], axis=1), jnp.concatenate([none, low], axis=1)], axis=0
        )

    def products(g):
        here = slice(g * MEMBERS, (g + 1) * MEMBERS)
        ws = [jnp.concatenate([spread(proj[here, c]), spread(gatt[here, c])], axis=1) for c in qcols]
        return ws, [dot(stacked(proj[here, k], proj[here, v]), w, 1, 1) for k, v, w in zip(kcols, vcols, ws)]

    def softmax(b, both):
        scores = both[:MEMBERS] * scale + bias_ref[b]
        gp = both[MEMBERS:]
        e = jnp.exp(scores - jnp.max(scores, axis=0, keepdims=True))
        p = e * (1.0 / jnp.sum(e, axis=0, keepdims=True))
        gs = p * (gp - jnp.sum(gp * p, axis=0, keepdims=True))
        gbias_ref[b] += gs
        return jnp.concatenate([p.astype(bf16), (gs * scale).astype(bf16)], axis=0)

    def store(g, keyed, queried):
        here = slice(g * MEMBERS, (g + 1) * MEMBERS)
        for b in blocks:
            att[here, qcols[b]] = gather(queried[b][:, :128]).astype(bf16)
            gproj[here, qcols[b]] = gather(queried[b][:, 128:]).astype(bf16)
            gproj[here, kcols[b]] = keyed[b][MEMBERS:, :128].astype(bf16)
            gproj[here, vcols[b]] = keyed[b][:MEMBERS, 128:].astype(bf16)

    ahead, behind = products(0), None
    for g in range(groups):
        here = slice(g * MEMBERS, (g + 1) * MEMBERS)
        ws, both = ahead
        keyed, queried, ws_next, both_next = [], [], [], []
        more = products(g + 1) if g + 1 < groups else ([], [])
        ws_next, both_next = more
        for b in blocks:
            pd = softmax(b, both[b])
            keyed.append(dot(pd, ws[b], 1, 0))
            queried.append(dot(pd, stacked(proj[here, vcols[b]], proj[here, kcols[b]]), 0, 0))
        if behind is not None:
            store(g - 1, *behind)
        behind = (keyed, queried)
        ahead = (ws_next, both_next)
    store(groups - 1, *behind)


def back_to_input(wqkv_ref, gain_ref, branch_ref, gproj, hat, istd, dyf):
    width = gproj.shape[1] // 3
    rows, groups, chunk = gproj.shape[0], gproj.shape[0] // MEMBERS, CHUNK
    per, mem = chunk // MEMBERS, chunk // groups
    bf16, f32 = jnp.bfloat16, jnp.float32

    def gn_step(c, carry):
        here = pl.ds(pl.multiple_of(c * chunk, chunk), chunk)
        gn = dot(gproj[here, :], wqkv_ref[...], 1, 1)
        for g in range(per):
            put(dyf, pl.ds(c * per + g, MEMBERS, stride=groups), gn[g * MEMBERS : (g + 1) * MEMBERS])
        return carry

    lax.fori_loop(0, rows // chunk, gn_step, 0, unroll=True)

    def back_step(c, carry):
        gg, gsh = carry
        here = pl.ds(pl.multiple_of(c * chunk, chunk), chunk)
        gn = take(dyf, here)
        normalized = take(hat, here)
        prod = gn * normalized
        gg = gg + jnp.sum(prod.reshape(chunk // 8, 8, width), axis=0)
        gsh = gsh + jnp.sum(gn.reshape(chunk // 8, 8, width), axis=0)
        gh = gn * gain_ref[...]
        m1 = jnp.mean(gh, axis=-1, keepdims=True)
        m2 = jnp.mean(prod * gain_ref[...], axis=-1, keepdims=True)
        inv = istd[here, :][:, :1]
        branch = (inv * (gh - m1 - normalized * m2)).astype(bf16)
        branch_ref[pl.ds(pl.multiple_of(c * mem, mem), mem)] = branch.reshape(mem, groups, width)
        return gg, gsh

    zero = jnp.zeros((8, width), f32)
    gg, gsh = lax.fori_loop(0, rows // chunk, back_step, (zero, zero), unroll=True)
    return jnp.sum(gg, axis=0, keepdims=True), jnp.sum(gsh, axis=0, keepdims=True)


def offset_sums(gbias_ref):
    f32, bf16 = jnp.float32, jnp.bfloat16
    blocks, members, lanes = gbias_ref.shape
    i = lax.broadcasted_iota(jnp.int32, (lanes, 2 * lanes), 0)
    o = lax.broadcasted_iota(jnp.int32, (lanes, 2 * lanes), 1)
    query = GRID * GRID - 1 - i % members
    wide = (o == i // members * 128 + query // GRID * 16 + query % GRID).astype(f32).astype(bf16)
    spreads = []
    for b in range(blocks):
        value = gbias_ref[b]
        high = value.astype(bf16)
        rest = value - high.astype(f32)
        low = rest.astype(bf16)
        lowest = (rest - low.astype(f32)).astype(bf16)
        parts = dot(jnp.concatenate([high, low, lowest], axis=0), wide, 1, 0)
        spreads.append(parts[:members] + (parts[members : 2 * members] + parts[2 * members :]))
    sums = []
    for b in range(blocks):
        for h in range(PACK):
            frame = spreads[b][:, h * 128 : (h + 1) * 128]
            total = None
            for row in range(GRID):
                piece = frame[row * GRID : (row + 1) * GRID]
                piece = jnp.concatenate([piece, jnp.zeros_like(piece)], axis=1)
                piece = pltpu.roll(piece, row * 16, 1, stride=1, stride_axis=0)
                total = piece if total is None else total + piece
            sums.append(jnp.sum(total, axis=0, keepdims=True))
    return jnp.concatenate(sums, axis=0)


def scores_kernel(
    core_ref, pair_ref, wqkv_hbm, wout_hbm, bias_ref, gain_ref, shift_ref,
    keep_ref, send_ref, table_ref, gproj, hat, istd, wqkv_ref,
    wout_ref, gbias_ref, normed, att, dyp, proj, gatt, dyf, sems, *, head_dim,
):
    fetches = [
        pltpu.make_async_copy(wqkv_hbm, wqkv_ref, sems.at[0]),
        pltpu.make_async_copy(wout_hbm, wout_ref, sems.at[1]),
    ]
    for fetch in fetches:
        fetch.start()
    gbias_ref[...] = jnp.zeros_like(gbias_ref)
    forward_and_scores(
        pair_ref, wqkv_ref, wout_ref, bias_ref, gain_ref, shift_ref, gbias_ref,
        normed, gproj, att, dyp, hat, istd, proj, gatt, dyf, head_dim, fetches,
    )
    width = wout_ref.shape[0]
    half = 2 * width
    first = core_ref[0] == 0
    table = offset_sums(gbias_ref)
    heads = table.shape[0] // 2
    table_ref[...] = jnp.where(first, table[:heads], table[heads:])
    send_ref[width:, :] = jnp.zeros((send_ref.shape[0] - width, half), send_ref.dtype)
    send_ref[width : width + heads, :256] = jnp.where(first, table[heads:], table[:heads]).astype(send_ref.dtype)

    turned = normed[...].T
    for piece in range(4):
        cols = slice(piece * 256, (piece + 1) * 256)
        low = dot(turned, gproj[:, cols], 1, 0)
        if piece < 2:
            high = dot(turned, gproj[:, half + piece * 256 : half + (piece + 1) * 256], 1, 0)
        else:
            high = dot(att[...], dyp[:, (piece - 2) * 256 : (piece - 1) * 256], 0, 0)
        keep_ref[:, cols] = jnp.where(first, low, high)
        send_ref[:width, cols] = jnp.where(first, high, low).astype(send_ref.dtype)


def back_kernel(wqkv_ref, gain_ref, gproj, hat, istd, branch_ref, gvec_ref, dyf):
    sums = back_to_input(wqkv_ref, gain_ref, branch_ref, gproj, hat, istd, dyf)
    lanes = hat.shape[0]
    for i in range(2):
        for b in range(lanes):
            gvec_ref[i * lanes + b : i * lanes + b + 1, :] = sums[i][:, b * 128 : (b + 1) * 128]


VMEM = pl.BlockSpec(memory_space=pltpu.VMEM)
SMEM = pl.BlockSpec(memory_space=pltpu.SMEM)
HBM = pl.BlockSpec(memory_space=pltpu.HBM)
MIB = 1024 * 1024


def in_hbm(a):
    return pltpu.with_memory_space_constraint(a, pltpu.HBM)


def shaped(*shape, dtype=jnp.float32):
    return jax.ShapeDtypeStruct(shape, dtype)


def cost(flops, size):
    return pl.CostEstimate(flops=flops, bytes_accessed=size, transcendentals=0)


def part_buffers(rows, width):
    bf16, f32 = jnp.bfloat16, jnp.float32
    tall, lanes = (rows, width), (width // 128, rows, 128)
    return [
        (tall, bf16), ((rows, 3 * width), bf16), (tall, bf16), (tall, bf16), (lanes, f32), ((rows, 128), f32),
        ((rows, 3 * width), bf16), (tall, bf16), (lanes, f32),
    ]


def local_scores(core, pair, wqkv, wout, bias, gain, shift, head_dim):
    members, _, groups, width = pair.shape
    bf16, f32 = jnp.bfloat16, jnp.float32
    normed, gproj, att, dyp, hat, istd, proj, gatt, dyf = part_buffers(groups * MEMBERS, width)
    half_heads = width // head_dim // 2
    return pl.pallas_call(
        functools.partial(scores_kernel, head_dim=head_dim),
        out_shape=(
            shaped(width, 2 * width), shaped(width + 16, 2 * width, dtype=bf16), shaped(half_heads, 256)
        )
        + tuple(jax.ShapeDtypeStruct(*b) for b in (gproj, hat, istd))
        + (jax.ShapeDtypeStruct(wqkv.shape, wqkv.dtype),),
        in_specs=[SMEM, VMEM, HBM, HBM] + [VMEM] * 3,
        out_specs=(VMEM,) * 7,
        scratch_shapes=[pltpu.VMEM(wout.shape, wout.dtype), pltpu.VMEM(bias.shape, f32)]
        + [pltpu.VMEM(*b) for b in (normed, att, dyp, proj, gatt, dyf)]
        + [pltpu.SemaphoreType.DMA((2,))],
        compiler_params=pltpu.CompilerParams(vmem_limit_bytes=28 * MIB),
        cost_estimate=cost(20_000_000_000, 8 << 20),
        name="scores",
    )(core.reshape(1), pair, in_hbm(wqkv), in_hbm(wout), bias, gain.reshape(1, width), shift.reshape(1, width))


def local_back(wqkv, gain, gproj, hat, istd, groups):
    width = gain.shape[0]
    return pl.pallas_call(
        back_kernel,
        out_shape=(shaped(MEMBERS, groups, width, dtype=gproj.dtype), shaped(2 * width // 128, 128)),
        in_specs=[VMEM] * 5,
        out_specs=(VMEM,) * 2,
        scratch_shapes=[pltpu.VMEM(hat.shape, jnp.float32)],
        compiler_params=pltpu.CompilerParams(vmem_limit_bytes=16 * MIB),
        cost_estimate=cost(6_000_000_000, 4 << 20),
        name="back",
    )(wqkv, gain.reshape(1, width), gproj, hat, istd)


def pair_kernel(x_ref, dy_ref, out_ref):
    out_ref[:, 0] = x_ref[...]
    out_ref[:, 1] = dy_ref[...]


def pair_of(x, dy):
    chips, groups, width = x.shape
    step = chips // 2
    source = pl.BlockSpec((step, groups, width), lambda i: (i, 0, 0))
    return pl.pallas_call(
        pair_kernel,
        grid=(chips // step,),
        out_shape=shaped(chips, 2, groups, width, dtype=x.dtype),
        in_specs=[source, source],
        out_specs=pl.BlockSpec((step, 2, groups, width), lambda i: (i, 0, 0, 0)),
        cost_estimate=cost(0, 4 << 20),
        name="pair",
    )(x, dy)


def outgoing_kernel(branch_ref, keep_ref, recv_ref, table_ref, gvec_ref, out_ref):
    chips, _, share, _ = out_ref.shape
    _, groups, width = branch_ref.shape
    f32, bf16 = jnp.float32, jnp.bfloat16
    slot = 0
    for b in range(width // 128):
        for t in range(groups // share):
            out_ref[:, slot] = branch_ref[:, t * share : (t + 1) * share, b * 128 : (b + 1) * 128]
            slot += 1
    for b in range(2 * width // 128):
        cols = slice(b * 128, (b + 1) * 128)
        total = (keep_ref[:, cols] + recv_ref[:width, cols].astype(f32)).astype(bf16)
        out_ref[:, slot] = total.reshape(chips, share, 128)
        slot += 1
    table = table_ref[...] + recv_ref[width : width + share, :256].astype(f32)
    for value in (table[:, :128], table[:, 128:], gvec_ref[...]):
        out_ref[:, slot] = jnp.broadcast_to(value.astype(bf16)[None], (chips, share, 128))
        slot += 1


def outgoing(branch, keep, recv, table, gvec):
    chips, groups, width = branch.shape
    share = width // chips
    slots = groups // share * width // 128 + 2 * width // 128 + 3
    return pl.pallas_call(
        outgoing_kernel,
        out_shape=shaped(chips, slots, share, 128, dtype=branch.dtype),
        in_specs=[VMEM] * 5,
        out_specs=VMEM,
        compiler_params=pltpu.CompilerParams(vmem_limit_bytes=16 * MIB),
        cost_estimate=cost(0, 6 << 20),
        name="outgoing",
    )(branch, keep, recv, table, gvec)


def sums_kernel(core_ref, got_ref, keep_ref, send_ref, *, begin, factor):
    f32 = jnp.float32
    chips, slots, share, _ = got_ref.shape
    total = got_ref[0, begin:].astype(f32)
    for chip in range(1, chips):
        total = total + got_ref[chip, begin:].astype(f32)
    total = total * factor
    part = share // 2
    weights = slots - begin - 3
    for b in range(weights):
        rows = slice(b * part, (b + 1) * part)
        low, high = total[b, :part], total[b, part:]
        keep_ref[rows, :] = jnp.where(core_ref[0] == 0, low, high)
        send_ref[rows, :] = jnp.where(core_ref[0] == 0, high, low)
    for i in range(3):
        rows = slice(weights * part + i * share, weights * part + (i + 1) * share)
        keep_ref[rows, :] = total[weights + i]
        send_ref[rows, :] = total[weights + i]


def sums_of(core, got, begin, factor):
    chips, slots, share, _ = got.shape
    rows = (slots - begin - 3) * share // 2 + 3 * share
    return pl.pallas_call(
        functools.partial(sums_kernel, begin=begin, factor=factor),
        out_shape=(shaped(rows, 128), shaped(rows, 128)),
        in_specs=[SMEM, VMEM],
        out_specs=(VMEM,) * 2,
        compiler_params=pltpu.CompilerParams(vmem_limit_bytes=16 * MIB),
        cost_estimate=cost(0, 2 << 20),
        name="sums",
    )(core.reshape(1), got)


def input_kernel(got_ref, dy_hbm, grad_hbm, dy_ref, grad_ref, ins, outs):
    chips, groups, width = dy_ref.shape
    share = got_ref.shape[2]
    pieces = ins.shape[0]
    size = chips // pieces
    at = [slice(i * size, (i + 1) * size) for i in range(pieces)]
    fetches = [pltpu.make_async_copy(dy_hbm.at[a], dy_ref.at[a], ins.at[i]) for i, a in enumerate(at)]
    stores = [pltpu.make_async_copy(grad_ref.at[a], grad_hbm.at[a], outs.at[i]) for i, a in enumerate(at)]
    for fetch in fetches:
        fetch.start()
    f32 = jnp.float32
    for i, a in enumerate(at):
        fetches[i].wait()
        slot = 0
        for b in range(width // 128):
            cols = slice(b * 128, (b + 1) * 128)
            for t in range(groups // share):
                rows = slice(t * share, (t + 1) * share)
                branch = got_ref[a, slot].astype(f32)
                grad_ref[a, rows, cols] = (dy_ref[a, rows, cols].astype(f32) + branch).astype(grad_ref.dtype)
                slot += 1
        stores[i].start()
    for store in stores:
        store.wait()


def input_gradient(got, dy):
    pieces = 4
    whole = pltpu.VMEM(dy.shape, dy.dtype)
    sems = pltpu.SemaphoreType.DMA((pieces,))
    return pl.pallas_call(
        input_kernel,
        out_shape=jax.ShapeDtypeStruct(dy.shape, dy.dtype),
        in_specs=[VMEM, HBM],
        out_specs=HBM,
        scratch_shapes=[whole, whole, sems, sems],
        compiler_params=pltpu.CompilerParams(vmem_limit_bytes=16 * MIB),
        cost_estimate=cost(0, 4 << 20),
        name="input_gradient",
    )(got, in_hbm(dy))


def finish_kernel(core_ref, keep_ref, recv_ref, qkv_ref, out_ref, table_ref, gain_ref, shift_ref):
    width = out_ref.shape[1]
    lanes = width // 128
    part, heads = out_ref.shape[0], table_ref.shape[0] // 2
    first = core_ref[0] == 0

    def ordered(mine, other):
        return jnp.where(first, mine, other), jnp.where(first, other, mine)

    for b in range(2 * lanes):
        rows = slice(b * part, (b + 1) * part)
        low, high = ordered(keep_ref[rows, :], recv_ref[rows, :])
        qkv_ref[:, b * 128 : (b + 1) * 128] = low
        if b < lanes:
            qkv_ref[:, 2 * width + b * 128 : 2 * width + (b + 1) * 128] = high
        else:
            out_ref[:, (b - lanes) * 128 : (b - lanes + 1) * 128] = high
    at = 2 * lanes * part
    halves = [jnp.concatenate([ref[at : at + heads], ref[at + heads : at + 2 * heads]], axis=1) for ref in (keep_ref, recv_ref)]
    table = jnp.concatenate(ordered(*halves), axis=0)
    side = 2 * GRID - 1
    place = lax.broadcasted_iota(jnp.int32, (256, side * side), 0)
    offset = lax.broadcasted_iota(jnp.int32, (256, side * side), 1)
    row, column = side - 1 - offset // side, side - 1 - offset % side
    pick = (place == row * 16 + column).astype(jnp.float32)
    table_ref[...] = lax.dot_general(
        table, pick, (((1,), (0,)), ((), ())), precision=lax.Precision.HIGHEST, preferred_element_type=jnp.float32
    )
    at += 2 * heads
    vectors = keep_ref[at:, :] + recv_ref[at:, :]
    for ref, row in ((gain_ref, 0), (shift_ref, lanes)):
        for b in range(lanes):
            ref[:, b * 128 : (b + 1) * 128] = vectors[row + b : row + b + 1]


def finish(core, keep, recv, part, width, heads, offsets):
    return pl.pallas_call(
        finish_kernel,
        out_shape=(
            shaped(part, 3 * width), shaped(part, width), shaped(heads, offsets), shaped(1, width), shaped(1, width)
        ),
        in_specs=[SMEM, VMEM, VMEM],
        out_specs=(VMEM,) * 5,
        compiler_params=pltpu.CompilerParams(vmem_limit_bytes=8 * MIB),
        name="finish",
    )(core.reshape(1), keep, recv)


AXES = ("x_lo", "y", "x_hi", "z", "core")
CHIPS = AXES[:4]


def relative_onehot(members):
    span = 2 * GRID - 1
    second = jnp.arange(members, dtype=jnp.int32)[:, None]
    first = jnp.arange(members, dtype=jnp.int32)[None, :]
    row_delta = first // GRID - second // GRID + GRID - 1
    col_delta = first % GRID - second % GRID + GRID - 1
    rel_index = row_delta * span + col_delta
    offsets = jnp.arange(span * span, dtype=jnp.int32)
    return (rel_index[:, :, None] == offsets).astype(jnp.float32)


def swap(a, axis, mask):
    size = lax.axis_size(axis)
    return lax.ppermute(a, axis, [(i, i ^ mask) for i in range(size)])


def local(block_input, cotangent, qkv_weight, out_weight, bias_table, norm_gain, norm_shift):
    tile_h, tile_w, width = block_input.shape
    heads, offsets = bias_table.shape
    chips = lax.axis_size(CHIPS)
    devices = chips * lax.axis_size("core")
    owned = tile_h * tile_w // chips
    core = lax.axis_index("core")
    onehot = relative_onehot(MEMBERS)
    bias = jnp.einsum(
        "bhr,kqr->bkhq",
        bias_table.reshape(heads // PACK, PACK, offsets),
        onehot,
        precision=lax.Precision.HIGHEST,
    ).reshape(heads // PACK, MEMBERS, PACK * MEMBERS)
    x = block_input.reshape(chips, owned, width)
    dy = cotangent.reshape(chips, owned, width)
    exchange = functools.partial(lax.all_to_all, axis_name=CHIPS, split_axis=0, concat_axis=0, tiled=True)
    got = exchange(pair_of(x, dy))
    keep, send, table, gproj, hat, istd, qkv_copy = local_scores(
        core, got, qkv_weight, out_weight, bias, norm_gain, norm_shift, width // heads
    )
    recv = swap(send, "core", 1)
    branch, gvec = local_back(qkv_copy, norm_gain, gproj, hat, istd, owned)
    got = exchange(outgoing(branch, keep, recv, table, gvec))
    factor = float(tile_h * tile_w * devices) ** (-0.5)
    share = width // chips
    mine, theirs = sums_of(core, got, owned // share * width // 128, factor)
    recv = swap(theirs, "core", 1)
    grad_input = input_gradient(got, dy)
    grad_qkv, grad_out, table, gain, shift = finish(core, mine, recv, share // 2, width, heads, offsets)
    return (
        grad_input.reshape(tile_h, tile_w, width),
        grad_qkv,
        grad_out,
        table,
        gain.reshape(width),
        shift.reshape(width),
    )


def solution(mesh):
    fine = Mesh(mesh.devices.reshape(2, 4, 2, 4, 2), AXES)
    tile = P(("x_lo", "y"), ("x_hi", "z", "core"), None)
    return jax.shard_map(
        local,
        mesh=fine,
        in_specs=(tile, tile, P(), P(), P(), P(), P()),
        out_specs=(tile, P(AXES, None), P(AXES, None), P(), P(), P()),
        check_vma=False,
    )
```

```python
import functools
import jax
import jax.numpy as jnp
from jax import lax
from jax.experimental import pallas as pl
from jax.experimental.pallas import tpu as pltpu
from jax.sharding import Mesh, PartitionSpec as P

GRID = 8
EPSILON = 1e-05
MEMBERS = GRID * GRID
PACK = 4
CHUNK = 256


def dot(a, b, ca, cb):
    return lax.dot_general(a, b, (((ca,), (cb,)), ((), ())), preferred_element_type=jnp.float32)


def put(ref, at, value):
    for b in range(ref.shape[0]):
        ref[b, at, :] = value[:, b * 128 : (b + 1) * 128]


def take(ref, at):
    return jnp.concatenate([ref[b, at, :] for b in range(ref.shape[0])], axis=1)


def forward_and_scores(
    pair_ref, wqkv_ref, wout_ref, bias_ref, gain_ref, shift_ref, gbias_ref,
    normed, gproj, att, dyp, hat, istd, proj, gatt, dyf, head_dim, fetches,
):
    width = gproj.shape[1] // 3
    rows, groups, chunk = gproj.shape[0], gproj.shape[0] // MEMBERS, CHUNK
    per, mem = chunk // MEMBERS, chunk // groups
    bf16, f32 = jnp.bfloat16, jnp.float32
    scale = head_dim ** (-0.5)

    def hat_step(c, carry):
        here = pl.ds(pl.multiple_of(c * chunk, chunk), chunk)
        pair = pair_ref[pl.ds(pl.multiple_of(c * mem, mem), mem)].astype(f32)
        x = pair[:, 0].reshape(chunk, width)
        centred = x - jnp.mean(x, axis=-1, keepdims=True)
        inv = lax.rsqrt(jnp.mean(centred * centred, axis=-1, keepdims=True) + EPSILON)
        put(hat, here, centred * inv)
        istd[here, :] = jnp.broadcast_to(inv, (chunk, 128))
        put(dyf, here, pair[:, 1].reshape(chunk, width))
        return carry

    lax.fori_loop(0, rows // chunk, hat_step, 0)
    for fetch in fetches:
        fetch.wait()

    def by_group(ref, c):
        return jnp.concatenate(
            [take(ref, pl.ds(c * per + g, MEMBERS, stride=groups)) for g in range(per)], axis=0
        )

    def norm_step(c, carry):
        here = pl.ds(pl.multiple_of(c * chunk, chunk), chunk)
        nb = (by_group(hat, c) * gain_ref[...] + shift_ref[...]).astype(bf16)
        dy = by_group(dyf, c).astype(bf16)
        dyp[here, :] = dy
        normed[here, :] = nb
        proj[here, :] = dot(nb, wqkv_ref[...], 1, 0).astype(bf16)
        gatt[here, :] = dot(dy, wout_ref[...], 1, 1).astype(bf16)
        return carry

    lax.fori_loop(0, rows // chunk, norm_step, 0, unroll=True)

    lane = lax.broadcasted_iota(jnp.int32, (MEMBERS, 128), 1) // head_dim

    def spread(a):
        zero = jnp.zeros_like(a)
        return jnp.concatenate([jnp.where(lane == h, a, zero) for h in range(PACK)], axis=0)

    def gather(a):
        out = a[:MEMBERS]
        for h in range(1, PACK):
            out = jnp.where(lane == h, a[h * MEMBERS : (h + 1) * MEMBERS], out)
        return out

    blocks = range(width // 128)

    qcols = [slice(b * 128, (b + 1) * 128) for b in blocks]
    kcols = [slice(width + b * 128, width + (b + 1) * 128) for b in blocks]
    vcols = [slice(2 * width + b * 128, 2 * width + (b + 1) * 128) for b in blocks]

    def stacked(top, low):
        none = jnp.zeros_like(top)
        return jnp.concatenate(
            [jnp.concatenate([top, none], axis=1), jnp.concatenate([none, low], axis=1)], axis=0
        )

    def products(g):
        here = slice(g * MEMBERS, (g + 1) * MEMBERS)
        ws = [jnp.concatenate([spread(proj[here, c]), spread(gatt[here, c])], axis=1) for c in qcols]
        return ws, [dot(stacked(proj[here, k], proj[here, v]), w, 1, 1) for k, v, w in zip(kcols, vcols, ws)]

    def softmax(b, both):
        scores = both[:MEMBERS] * scale + bias_ref[b]
        gp = both[MEMBERS:]
        e = jnp.exp(scores - jnp.max(scores, axis=0, keepdims=True))
        p = e * (1.0 / jnp.sum(e, axis=0, keepdims=True))
        gs = p * (gp - jnp.sum(gp * p, axis=0, keepdims=True))
        gbias_ref[b] += gs
        return jnp.concatenate([p.astype(bf16), (gs * scale).astype(bf16)], axis=0)

    def store(g, keyed, queried):
        here = slice(g * MEMBERS, (g + 1) * MEMBERS)
        for b in blocks:
            att[here, qcols[b]] = gather(queried[b][:, :128]).astype(bf16)
            gproj[here, qcols[b]] = gather(queried[b][:, 128:]).astype(bf16)
            gproj[here, kcols[b]] = keyed[b][MEMBERS:, :128].astype(bf16)
            gproj[here, vcols[b]] = keyed[b][:MEMBERS, 128:].astype(bf16)

    ahead, behind = products(0), None
    for g in range(groups):
        here = slice(g * MEMBERS, (g + 1) * MEMBERS)
        ws, both = ahead
        keyed, queried, ws_next, both_next = [], [], [], []
        more = products(g + 1) if g + 1 < groups else ([], [])
        ws_next, both_next = more
        for b in blocks:
            pd = softmax(b, both[b])
            keyed.append(dot(pd, ws[b], 1, 0))
            queried.append(dot(pd, stacked(proj[here, vcols[b]], proj[here, kcols[b]]), 0, 0))
        if behind is not None:
            store(g - 1, *behind)
        behind = (keyed, queried)
        ahead = (ws_next, both_next)
    store(groups - 1, *behind)


def back_to_input(wqkv_ref, gain_ref, branch_ref, gproj, hat, istd, dyf):
    width = gproj.shape[1] // 3
    rows, groups, chunk = gproj.shape[0], gproj.shape[0] // MEMBERS, CHUNK
    per, mem = chunk // MEMBERS, chunk // groups
    bf16, f32 = jnp.bfloat16, jnp.float32

    def gn_step(c, carry):
        here = pl.ds(pl.multiple_of(c * chunk, chunk), chunk)
        gn = dot(gproj[here, :], wqkv_ref[...], 1, 1)
        for g in range(per):
            put(dyf, pl.ds(c * per + g, MEMBERS, stride=groups), gn[g * MEMBERS : (g + 1) * MEMBERS])
        return carry

    lax.fori_loop(0, rows // chunk, gn_step, 0, unroll=True)

    def back_step(c, carry):
        gg, gsh = carry
        here = pl.ds(pl.multiple_of(c * chunk, chunk), chunk)
        gn = take(dyf, here)
        normalized = take(hat, here)
        prod = gn * normalized
        gg = gg + jnp.sum(prod.reshape(chunk // 8, 8, width), axis=0)
        gsh = gsh + jnp.sum(gn.reshape(chunk // 8, 8, width), axis=0)
        gh = gn * gain_ref[...]
        m1 = jnp.mean(gh, axis=-1, keepdims=True)
        m2 = jnp.mean(prod * gain_ref[...], axis=-1, keepdims=True)
        inv = istd[here, :][:, :1]
        branch = (inv * (gh - m1 - normalized * m2)).astype(bf16)
        branch_ref[pl.ds(pl.multiple_of(c * mem, mem), mem)] = branch.reshape(mem, groups, width)
        return gg, gsh

    zero = jnp.zeros((8, width), f32)
    gg, gsh = lax.fori_loop(0, rows // chunk, back_step, (zero, zero), unroll=True)
    return jnp.sum(gg, axis=0, keepdims=True), jnp.sum(gsh, axis=0, keepdims=True)


def offset_sums(gbias_ref):
    f32, bf16 = jnp.float32, jnp.bfloat16
    blocks, members, lanes = gbias_ref.shape
    i = lax.broadcasted_iota(jnp.int32, (lanes, 2 * lanes), 0)
    o = lax.broadcasted_iota(jnp.int32, (lanes, 2 * lanes), 1)
    query = GRID * GRID - 1 - i % members
    wide = (o == i // members * 128 + query // GRID * 16 + query % GRID).astype(f32).astype(bf16)
    spreads = []
    for b in range(blocks):
        value = gbias_ref[b]
        high = value.astype(bf16)
        rest = value - high.astype(f32)
        low = rest.astype(bf16)
        lowest = (rest - low.astype(f32)).astype(bf16)
        parts = dot(jnp.concatenate([high, low, lowest], axis=0), wide, 1, 0)
        spreads.append(parts[:members] + (parts[members : 2 * members] + parts[2 * members :]))
    sums = []
    for b in range(blocks):
        for h in range(PACK):
            frame = spreads[b][:, h * 128 : (h + 1) * 128]
            total = None
            for row in range(GRID):
                piece = frame[row * GRID : (row + 1) * GRID]
                piece = jnp.concatenate([piece, jnp.zeros_like(piece)], axis=1)
                piece = pltpu.roll(piece, row * 16, 1, stride=1, stride_axis=0)
                total = piece if total is None else total + piece
            sums.append(jnp.sum(total, axis=0, keepdims=True))
    return jnp.concatenate(sums, axis=0)


def scores_kernel(
    core_ref, pair_ref, wqkv_hbm, wout_hbm, bias_ref, gain_ref, shift_ref,
    keep_ref, send_ref, table_ref, gproj, hat, istd, wqkv_ref,
    wout_ref, gbias_ref, normed, att, dyp, proj, gatt, dyf, sems, *, head_dim,
):
    fetches = [
        pltpu.make_async_copy(wqkv_hbm, wqkv_ref, sems.at[0]),
        pltpu.make_async_copy(wout_hbm, wout_ref, sems.at[1]),
    ]
    for fetch in fetches:
        fetch.start()
    gbias_ref[...] = jnp.zeros_like(gbias_ref)
    forward_and_scores(
        pair_ref, wqkv_ref, wout_ref, bias_ref, gain_ref, shift_ref, gbias_ref,
        normed, gproj, att, dyp, hat, istd, proj, gatt, dyf, head_dim, fetches,
    )
    width = wout_ref.shape[0]
    half = 2 * width
    first = core_ref[0] == 0
    table = offset_sums(gbias_ref)
    heads = table.shape[0] // 2
    table_ref[...] = jnp.where(first, table[:heads], table[heads:])
    send_ref[width:, :] = jnp.zeros((send_ref.shape[0] - width, half), send_ref.dtype)
    send_ref[width : width + heads, :256] = jnp.where(first, table[heads:], table[:heads]).astype(send_ref.dtype)

    turned = normed[...].T
    for piece in range(4):
        cols = slice(piece * 256, (piece + 1) * 256)
        low = dot(turned, gproj[:, cols], 1, 0)
        if piece < 2:
            high = dot(turned, gproj[:, half + piece * 256 : half + (piece + 1) * 256], 1, 0)
        else:
            high = dot(att[...], dyp[:, (piece - 2) * 256 : (piece - 1) * 256], 0, 0)
        keep_ref[:, cols] = jnp.where(first, low, high)
        send_ref[:width, cols] = jnp.where(first, high, low).astype(send_ref.dtype)


def back_kernel(wqkv_ref, gain_ref, gproj, hat, istd, branch_ref, gvec_ref, dyf):
    sums = back_to_input(wqkv_ref, gain_ref, branch_ref, gproj, hat, istd, dyf)
    lanes = hat.shape[0]
    for i in range(2):
        for b in range(lanes):
            gvec_ref[i * lanes + b : i * lanes + b + 1, :] = sums[i][:, b * 128 : (b + 1) * 128]


VMEM = pl.BlockSpec(memory_space=pltpu.VMEM)
SMEM = pl.BlockSpec(memory_space=pltpu.SMEM)
HBM = pl.BlockSpec(memory_space=pltpu.HBM)
MIB = 1024 * 1024


def in_hbm(a):
    return pltpu.with_memory_space_constraint(a, pltpu.HBM)


def shaped(*shape, dtype=jnp.float32):
    return jax.ShapeDtypeStruct(shape, dtype)


def cost(flops, size):
    return pl.CostEstimate(flops=flops, bytes_accessed=size, transcendentals=0)


def part_buffers(rows, width):
    bf16, f32 = jnp.bfloat16, jnp.float32
    tall, lanes = (rows, width), (width // 128, rows, 128)
    return [
        (tall, bf16), ((rows, 3 * width), bf16), (tall, bf16), (tall, bf16), (lanes, f32), ((rows, 128), f32),
        ((rows, 3 * width), bf16), (tall, bf16), (lanes, f32),
    ]


def local_scores(core, pair, wqkv, wout, bias, gain, shift, head_dim):
    members, _, groups, width = pair.shape
    bf16, f32 = jnp.bfloat16, jnp.float32
    normed, gproj, att, dyp, hat, istd, proj, gatt, dyf = part_buffers(groups * MEMBERS, width)
    half_heads = width // head_dim // 2
    return pl.pallas_call(
        functools.partial(scores_kernel, head_dim=head_dim),
        out_shape=(
            shaped(width, 2 * width), shaped(width + 16, 2 * width, dtype=bf16), shaped(half_heads, 256)
        )
        + tuple(jax.ShapeDtypeStruct(*b) for b in (gproj, hat, istd))
        + (jax.ShapeDtypeStruct(wqkv.shape, wqkv.dtype),),
        in_specs=[SMEM, VMEM, HBM, HBM] + [VMEM] * 3,
        out_specs=(VMEM,) * 7,
        scratch_shapes=[pltpu.VMEM(wout.shape, wout.dtype), pltpu.VMEM(bias.shape, f32)]
        + [pltpu.VMEM(*b) for b in (normed, att, dyp, proj, gatt, dyf)]
        + [pltpu.SemaphoreType.DMA((2,))],
        compiler_params=pltpu.CompilerParams(vmem_limit_bytes=28 * MIB),
        cost_estimate=cost(20_000_000_000, 8 << 20),
        name="scores",
    )(core.reshape(1), pair, in_hbm(wqkv), in_hbm(wout), bias, gain.reshape(1, width), shift.reshape(1, width))


def local_back(wqkv, gain, gproj, hat, istd, groups):
    width = gain.shape[0]
    return pl.pallas_call(
        back_kernel,
        out_shape=(shaped(MEMBERS, groups, width, dtype=gproj.dtype), shaped(2 * width // 128, 128)),
        in_specs=[VMEM] * 5,
        out_specs=(VMEM,) * 2,
        scratch_shapes=[pltpu.VMEM(hat.shape, jnp.float32)],
        compiler_params=pltpu.CompilerParams(vmem_limit_bytes=16 * MIB),
        cost_estimate=cost(6_000_000_000, 4 << 20),
        name="back",
    )(wqkv, gain.reshape(1, width), gproj, hat, istd)


def pair_kernel(x_ref, dy_ref, out_ref):
    out_ref[:, 0] = x_ref[...]
    out_ref[:, 1] = dy_ref[...]


def pair_of(x, dy):
    chips, groups, width = x.shape
    step = chips // 2
    source = pl.BlockSpec((step, groups, width), lambda i: (i, 0, 0))
    return pl.pallas_call(
        pair_kernel,
        grid=(chips // step,),
        out_shape=shaped(chips, 2, groups, width, dtype=x.dtype),
        in_specs=[source, source],
        out_specs=pl.BlockSpec((step, 2, groups, width), lambda i: (i, 0, 0, 0)),
        cost_estimate=cost(0, 4 << 20),
        name="pair",
    )(x, dy)


def outgoing_kernel(branch_ref, keep_ref, recv_ref, table_ref, gvec_ref, out_ref):
    chips, _, share, _ = out_ref.shape
    _, groups, width = branch_ref.shape
    f32, bf16 = jnp.float32, jnp.bfloat16
    slot = 0
    for b in range(width // 128):
        for t in range(groups // share):
            out_ref[:, slot] = branch_ref[:, t * share : (t + 1) * share, b * 128 : (b + 1) * 128]
            slot += 1
    for b in range(2 * width // 128):
        cols = slice(b * 128, (b + 1) * 128)
        total = (keep_ref[:, cols] + recv_ref[:width, cols].astype(f32)).astype(bf16)
        out_ref[:, slot] = total.reshape(chips, share, 128)
        slot += 1
    table = table_ref[...] + recv_ref[width : width + share, :256].astype(f32)
    for value in (table[:, :128], table[:, 128:], gvec_ref[...]):
        out_ref[:, slot] = jnp.broadcast_to(value.astype(bf16)[None], (chips, share, 128))
        slot += 1


def outgoing(branch, keep, recv, table, gvec):
    chips, groups, width = branch.shape
    share = width // chips
    slots = groups // share * width // 128 + 2 * width // 128 + 3
    return pl.pallas_call(
        outgoing_kernel,
        out_shape=shaped(chips, slots, share, 128, dtype=branch.dtype),
        in_specs=[VMEM] * 5,
        out_specs=VMEM,
        compiler_params=pltpu.CompilerParams(vmem_limit_bytes=16 * MIB),
        cost_estimate=cost(0, 6 << 20),
        name="outgoing",
    )(branch, keep, recv, table, gvec)


def sums_kernel(core_ref, got_ref, keep_ref, send_ref, *, begin, factor):
    f32 = jnp.float32
    chips, slots, share, _ = got_ref.shape
    total = got_ref[0, begin:].astype(f32)
    for chip in range(1, chips):
        total = total + got_ref[chip, begin:].astype(f32)
    total = total * factor
    part = share // 2
    weights = slots - begin - 3
    for b in range(weights):
        rows = slice(b * part, (b + 1) * part)
        low, high = total[b, :part], total[b, part:]
        keep_ref[rows, :] = jnp.where(core_ref[0] == 0, low, high)
        send_ref[rows, :] = jnp.where(core_ref[0] == 0, high, low)
    for i in range(3):
        rows = slice(weights * part + i * share, weights * part + (i + 1) * share)
        keep_ref[rows, :] = total[weights + i]
        send_ref[rows, :] = total[weights + i]


def sums_of(core, got, begin, factor):
    chips, slots, share, _ = got.shape
    rows = (slots - begin - 3) * share // 2 + 3 * share
    return pl.pallas_call(
        functools.partial(sums_kernel, begin=begin, factor=factor),
        out_shape=(shaped(rows, 128), shaped(rows, 128)),
        in_specs=[SMEM, VMEM],
        out_specs=(VMEM,) * 2,
        compiler_params=pltpu.CompilerParams(vmem_limit_bytes=16 * MIB),
        cost_estimate=cost(0, 2 << 20),
        name="sums",
    )(core.reshape(1), got)


def input_kernel(got_ref, dy_ref, grad_ref):
    _, groups, width = dy_ref.shape
    share = got_ref.shape[2]
    f32 = jnp.float32
    slot = 0
    for b in range(width // 128):
        cols = slice(b * 128, (b + 1) * 128)
        for t in range(groups // share):
            rows = slice(t * share, (t + 1) * share)
            branch = got_ref[:, slot].astype(f32)
            grad_ref[:, rows, cols] = (dy_ref[:, rows, cols].astype(f32) + branch).astype(grad_ref.dtype)
            slot += 1


def input_gradient(got, dy):
    return pl.pallas_call(
        input_kernel,
        out_shape=jax.ShapeDtypeStruct(dy.shape, dy.dtype),
        in_specs=[VMEM] * 2,
        out_specs=VMEM,
        compiler_params=pltpu.CompilerParams(vmem_limit_bytes=16 * MIB),
        cost_estimate=cost(0, 4 << 20),
        name="input_gradient",
    )(got, dy)


def finish_kernel(core_ref, keep_ref, recv_ref, qkv_ref, out_ref, table_ref, gain_ref, shift_ref):
    width = out_ref.shape[1]
    lanes = width // 128
    part, heads = out_ref.shape[0], table_ref.shape[0] // 2
    first = core_ref[0] == 0

    def ordered(mine, other):
        return jnp.where(first, mine, other), jnp.where(first, other, mine)

    for b in range(2 * lanes):
        rows = slice(b * part, (b + 1) * part)
        low, high = ordered(keep_ref[rows, :], recv_ref[rows, :])
        qkv_ref[:, b * 128 : (b + 1) * 128] = low
        if b < lanes:
            qkv_ref[:, 2 * width + b * 128 : 2 * width + (b + 1) * 128] = high
        else:
            out_ref[:, (b - lanes) * 128 : (b - lanes + 1) * 128] = high
    at = 2 * lanes * part
    halves = [jnp.concatenate([ref[at : at + heads], ref[at + heads : at + 2 * heads]], axis=1) for ref in (keep_ref, recv_ref)]
    table = jnp.concatenate(ordered(*halves), axis=0)
    side = 2 * GRID - 1
    place = lax.broadcasted_iota(jnp.int32, (256, side * side), 0)
    offset = lax.broadcasted_iota(jnp.int32, (256, side * side), 1)
    row, column = side - 1 - offset // side, side - 1 - offset % side
    pick = (place == row * 16 + column).astype(jnp.float32)
    table_ref[...] = lax.dot_general(
        table, pick, (((1,), (0,)), ((), ())), precision=lax.Precision.HIGHEST, preferred_element_type=jnp.float32
    )
    at += 2 * heads
    vectors = keep_ref[at:, :] + recv_ref[at:, :]
    for ref, row in ((gain_ref, 0), (shift_ref, lanes)):
        for b in range(lanes):
            ref[:, b * 128 : (b + 1) * 128] = vectors[row + b : row + b + 1]


def finish(core, keep, recv, part, width, heads, offsets):
    return pl.pallas_call(
        finish_kernel,
        out_shape=(
            shaped(part, 3 * width), shaped(part, width), shaped(heads, offsets), shaped(1, width), shaped(1, width)
        ),
        in_specs=[SMEM, VMEM, VMEM],
        out_specs=(VMEM,) * 5,
        compiler_params=pltpu.CompilerParams(vmem_limit_bytes=8 * MIB),
        name="finish",
    )(core.reshape(1), keep, recv)


AXES = ("x_lo", "y", "x_hi", "z", "core")
CHIPS = AXES[:4]


def relative_onehot(members):
    span = 2 * GRID - 1
    second = jnp.arange(members, dtype=jnp.int32)[:, None]
    first = jnp.arange(members, dtype=jnp.int32)[None, :]
    row_delta = first // GRID - second // GRID + GRID - 1
    col_delta = first % GRID - second % GRID + GRID - 1
    rel_index = row_delta * span + col_delta
    offsets = jnp.arange(span * span, dtype=jnp.int32)
    return (rel_index[:, :, None] == offsets).astype(jnp.float32)


def swap(a, axis, mask):
    size = lax.axis_size(axis)
    return lax.ppermute(a, axis, [(i, i ^ mask) for i in range(size)])


def local(block_input, cotangent, qkv_weight, out_weight, bias_table, norm_gain, norm_shift):
    tile_h, tile_w, width = block_input.shape
    heads, offsets = bias_table.shape
    chips = lax.axis_size(CHIPS)
    devices = chips * lax.axis_size("core")
    owned = tile_h * tile_w // chips
    core = lax.axis_index("core")
    onehot = relative_onehot(MEMBERS)
    bias = jnp.einsum(
        "bhr,kqr->bkhq",
        bias_table.reshape(heads // PACK, PACK, offsets),
        onehot,
        precision=lax.Precision.HIGHEST,
    ).reshape(heads // PACK, MEMBERS, PACK * MEMBERS)
    x = block_input.reshape(chips, owned, width)
    dy = cotangent.reshape(chips, owned, width)
    exchange = functools.partial(lax.all_to_all, axis_name=CHIPS, split_axis=0, concat_axis=0, tiled=True)
    got = exchange(pair_of(x, dy))
    keep, send, table, gproj, hat, istd, qkv_copy = local_scores(
        core, got, qkv_weight, out_weight, bias, norm_gain, norm_shift, width // heads
    )
    recv = swap(send, "core", 1)
    branch, gvec = local_back(qkv_copy, norm_gain, gproj, hat, istd, owned)
    got = exchange(outgoing(branch, keep, recv, table, gvec))
    factor = float(tile_h * tile_w * devices) ** (-0.5)
    share = width // chips
    mine, theirs = sums_of(core, got, owned // share * width // 128, factor)
    recv = swap(theirs, "core", 1)
    grad_input = input_gradient(got, dy)
    grad_qkv, grad_out, table, gain, shift = finish(core, mine, recv, share // 2, width, heads, offsets)
    return (
        grad_input.reshape(tile_h, tile_w, width),
        grad_qkv,
        grad_out,
        table,
        gain.reshape(width),
        shift.reshape(width),
    )


def solution(mesh):
    fine = Mesh(mesh.devices.reshape(2, 4, 2, 4, 2), AXES)
    tile = P(("x_lo", "y"), ("x_hi", "z", "core"), None)
    return jax.shard_map(
        local,
        mesh=fine,
        in_specs=(tile, tile, P(), P(), P(), P(), P()),
        out_specs=(tile, P(AXES, None), P(AXES, None), P(), P(), P()),
        check_vma=False,
    )
```
